128 devices in a mesh: grp: 4 (over x_lo, core), blk: 32 (over x_hi, y, z).
Axes of the slice: x: 4 (x_hi: 2, x_lo: 2; x = x_hi * 2 + x_lo), y: 4, z: 4, core: 2. Of those that a mesh axis runs over, the one named last changes fastest.
Arguments:
- resid: bfloat16 [2, 3072, 4096], P(None, ('grp', 'blk'))
- attn: bfloat16 [2, 3072, 4096], P(None, ('grp', 'blk')), may hold values from -5 to 5
- out_proj: bfloat16 [4096, 4096], P(None, 'grp'), may hold values from -0.09375 to 0.09375
- out_bias: float32 [4096], replicated, may hold values from -2 to 2
- gain: float32 [4096], replicated, may hold values from 0.5 to 1.5
- task_bias: float32 [8, 4096], replicated, may hold values from -1 to 1
- task_ids: int32 [4], P('grp'), may hold values from 0 to 7
- neg_owner: int32 [3072, 7], P(('grp', 'blk')), may hold values from 0 to 127, as said below
- neg_row: int32 [3072, 7], P(('grp', 'blk')), may hold values from 0 to 23
Outputs:
- losses: float32 [3072], P(('grp', 'blk'))
- grad_attn: float32 [2, 3072, 4096], P(None, ('grp', 'blk'))
- grad_gain: float32 [4096], replicated
- grad_task_bias: float32 [8, 4096], replicated
- grad_out_bias: float32 [4096], replicated
The draws below stay inside these ranges and needn't reach their ends.
Inputs may be any that keep to these rules, and one draw needn't show every extreme that they name: `neg_owner`: within one device's 24 x 7 entries each owner is named at most 2 times, and one owner is named exactly 2 times by every device. Owners number the devices of grp and blk together, grp the slower.
All inputs are finite; a program needn't handle non-finite values.
Results may differ from the reference program's by a relative error of at most 0.014.
Values may be sent and summed in bfloat16 or wider, within the bound.
No kernel may reach another device: no remote copies, remote signals or barrier semaphores. Data moves between devices by JAX's collectives and lax.ppermute only.
A program may use at most 128 MiB of HBM per device.

```python
import jax
import jax.numpy as jnp
from jax import lax

D = 4096
TOK_DEV = 24
HARD = 7
TASKS = 8
GROUP_PAIRS = 768
GROUPS = 4
TOKENS = 3072
CAP = 2
N_GRP = 4
N_BLK = 32


def negative_layout(key):
    dev_count = TOKENS // TOK_DEV
    slot_total = dev_count * CAP
    wanted = TOK_DEV * HARD
    pop_key, hot_key, source_key, row_key = jax.random.split(key, 4)
    popular = jax.random.randint(pop_key, (dev_count,), 0, 4)
    hottest = jax.random.randint(hot_key, (), 0, dev_count)
    popular = jnp.where(jnp.arange(dev_count) == hottest, 4, popular)
    slot_owner = jnp.arange(slot_total) // CAP

    def one_source(single_key):
        score_key, order_key = jax.random.split(single_key)
        noise = jax.random.randint(score_key, (slot_total,), 0, 65536)
        ranking = (popular[slot_owner] * 65536 + noise) * slot_total + jnp.arange(slot_total)
        chosen = jnp.argsort(-ranking)[:wanted]
        shuffled = chosen[jax.random.permutation(order_key, wanted)]
        return shuffled // CAP
    owners = jax.vmap(one_source)(jax.random.split(source_key, dev_count))
    rows = jax.random.randint(row_key, (dev_count, wanted), 0, TOK_DEV)
    return (owners.reshape(TOKENS, HARD).astype(jnp.int32), rows.reshape(TOKENS, HARD).astype(jnp.int32))


def draw_neg_owner(key, part):
    return negative_layout(key)[0]


def draw_neg_row(key, part):
    return negative_layout(key)[1]


def draw_resid(key, part):
    owners, rows = negative_layout(key)
    negative_ids = owners * TOK_DEV + rows
    key = jax.random.fold_in(key, 11)
    pass_key, query_key, column_key, scale_key = jax.random.split(key, 4)
    base_pass = jax.random.normal(pass_key, (TOKENS, D))
    base_query = jax.random.normal(query_key, (TOKENS, D))
    queries = base_query + 0.4 * base_pass
    for slot_index in range(HARD):
        queries = queries + 0.6 * base_pass[negative_ids[:, slot_index]]
    columns = 0.3 * jnp.power(10.0, jax.random.uniform(column_key, (D,)))
    row_scale = 0.3 * jnp.power(10.0, jax.random.uniform(scale_key, (2, TOKENS, 1)))
    stacked = jnp.stack([queries, base_pass]) * columns * row_scale
    return stacked.astype(jnp.bfloat16)


def touch_ends(drawn, rng, least, top_value):
    extent = drawn.shape
    index_at = [jax.random.randint(jax.random.fold_in(rng, axis), (), 0, extent[axis]) for axis in range(len(extent))]
    drawn = drawn.at[tuple(index_at)].set(least)
    longest = extent.index(max(extent))
    index_at[longest] = (index_at[longest] + 1) % extent[longest]
    return drawn.at[tuple(index_at)].set(top_value)


def block_levels(own_key, dims, cuts, least, largest):
    def one(position, blocks):
        steps = jax.random.uniform(jax.random.fold_in(jax.random.fold_in(own_key, 6), position), (blocks,), jnp.float32, least / len(cuts), largest / len(cuts))
        return jnp.repeat(jnp.exp(steps), dims[position] // blocks).reshape((-1,) + (1,) * (len(dims) - position - 1))

    level = one(*cuts[0])
    for cut in cuts[1:]:
        level = level * one(*cut)
    return level


def gaussian(rng, extent, scale, bound, shards=(), kind=jnp.bfloat16):
    entries = jax.random.normal(rng, extent, jnp.float32) * scale
    if len(shards) > 0:
        entries = block_levels(rng, extent, shards, -0.22, 0.18) * entries
    return jnp.clip(entries, min=-bound, max=bound).astype(kind)


def setup_inputs(seed: int = 0) -> dict:
    key_list = jax.random.split(jax.random.key(seed), 10)
    return {
        "resid": draw_resid(jax.random.fold_in(key_list[9], 71), 0),
        "attn": gaussian(key_list[1], (2, TOKENS, D), 0.7, 5.0, ((1, 128),)),
        "out_proj": gaussian(key_list[2], (D, D), D ** -0.5, 0.09375, ((1, 4),)),
        "out_bias": gaussian(key_list[3], (D,), 0.3, 2.0, (), jnp.float32),
        "gain": jnp.clip(1.0 + 0.1 * jax.random.normal(key_list[4], (D,), jnp.float32), 0.5, 1.5),
        "task_bias": gaussian(key_list[5], (TASKS, D), 0.15, 1.0, (), jnp.float32),
        "task_ids": touch_ends(jax.random.randint(key_list[6], (GROUPS,), 0, TASKS), jax.random.fold_in(key_list[6], 1), 0, TASKS - 1).astype(jnp.int32),
        "neg_owner": draw_neg_owner(jax.random.fold_in(key_list[9], 71), 0),
        "neg_row": draw_neg_row(jax.random.fold_in(key_list[9], 71), 0),
    }


TAU = 0.02
LOSS_SCALE = 256.0

def rounded(values):
    return lax.optimization_barrier(values.astype(jnp.bfloat16)).astype(jnp.float32)

def embed_rows(pooled, gain, bias_rows):
    normed = pooled * lax.rsqrt(lax.optimization_barrier(jnp.mean(pooled * pooled, axis=-1, keepdims=True)) + 1e-05)
    mixture = normed * gain + bias_rows
    return mixture * lax.rsqrt(lax.optimization_barrier(jnp.sum(mixture * mixture, axis=-1, keepdims=True)) + 1e-06)

def reference(resid, attn, out_proj, out_bias, gain, task_bias, task_ids, neg_owner, neg_row):
    row_count = 2 * TOKENS
    projected = jnp.dot(attn.reshape(row_count, D), out_proj, preferred_element_type=jnp.float32).astype(jnp.bfloat16)
    pooled = resid.reshape(row_count, D).astype(jnp.float32) + projected.astype(jnp.float32) + out_bias
    group_of = (jnp.arange(row_count) % TOKENS // GROUP_PAIRS).astype(jnp.int32)
    row_task = task_ids[group_of]

    def embed_all(pooled, gain, task_bias):
        return embed_rows(pooled, gain, task_bias[row_task])
    embedded, pullback = jax.vjp(embed_all, pooled, gain, task_bias)
    emb = embedded.astype(jnp.bfloat16)
    query_emb = emb[:TOKENS]
    passage_emb = emb[TOKENS:]
    negative_ids = (neg_owner * TOK_DEV + neg_row).astype(jnp.int32)

    def one_group(hard_sum, group_index):
        offset = (group_index * GROUP_PAIRS).astype(jnp.int32)
        queries = lax.dynamic_slice_in_dim(query_emb, offset, GROUP_PAIRS, 0)
        passages = lax.dynamic_slice_in_dim(passage_emb, offset, GROUP_PAIRS, 0)
        group_ids = lax.dynamic_slice_in_dim(negative_ids, offset, GROUP_PAIRS, 0)
        negatives = passage_emb[group_ids]
        scores = jnp.dot(queries, passages.T, preferred_element_type=jnp.float32) / TAU
        hard = jnp.einsum('id,ikd->ik', queries.astype(jnp.float32), negatives.astype(jnp.float32)) / TAU
        weights = jnp.exp(scores)
        hard_weights = jnp.exp(hard)
        totals = lax.optimization_barrier(jnp.sum(weights, 1)) + lax.optimization_barrier(jnp.sum(hard_weights, 1))
        losses = jnp.log(totals) - jnp.diagonal(scores)
        numerator = jnp.dot(weights.astype(jnp.bfloat16), passages, preferred_element_type=jnp.float32)
        numerator = numerator + jnp.einsum('ik,ikd->id', rounded(hard_weights), negatives.astype(jnp.float32))
        grad_q = numerator / (TAU * totals[:, None]) - passages.astype(jnp.float32) / TAU
        probs = (weights / totals[:, None]).astype(jnp.bfloat16)
        query_blocks = queries.reshape(N_BLK, TOK_DEV, D)
        prob_blocks = probs.reshape(N_BLK, TOK_DEV, GROUP_PAIRS)

        def add_block(running, pair_items):
            partial_value = jnp.dot(pair_items[0].T, pair_items[1], preferred_element_type=jnp.float32)
            return (running + rounded(partial_value), None)
        summed, _ = lax.scan(add_block, jnp.zeros((GROUP_PAIRS, D), jnp.float32), (prob_blocks, query_blocks))
        grad_p = summed / TAU - queries.astype(jnp.float32) / TAU
        hard_probs = rounded(hard_weights / totals[:, None])
        slot_grads = (hard_probs[:, :, None] * queries.astype(jnp.float32)[:, None, :] / TAU).astype(jnp.bfloat16)
        hard_sum = hard_sum.at[group_ids.reshape(-1)].add(slot_grads.reshape(-1, D).astype(jnp.float32))
        return (hard_sum, (losses, grad_q, grad_p))
    hard_sum, (losses, grad_q, grad_p) = lax.scan(one_group, jnp.zeros((TOKENS, D), jnp.float32), jnp.arange(N_GRP).astype(jnp.int32))
    grad_q = grad_q.reshape(TOKENS, D)
    grad_p = grad_p.reshape(TOKENS, D) + hard_sum
    d_pooled, grad_gain, grad_task_bias = pullback(jnp.concatenate([grad_q, grad_p], 0))
    grad_out_bias = lax.optimization_barrier(jnp.sum(d_pooled, 0))
    scaled = (LOSS_SCALE * d_pooled).astype(jnp.bfloat16)
    grad_attn = jnp.dot(scaled, out_proj.T, preferred_element_type=jnp.float32).reshape(2, TOKENS, D)
    return (losses.reshape(TOKENS), grad_attn, grad_gain, grad_task_bias, grad_out_bias)
```

```python
import jax
import jax.numpy as jnp
from jax import lax
from jax.experimental import pallas as pl
from jax.experimental.pallas import tpu as pltpu
from jax.sharding import Mesh, PartitionSpec as P

TAU = 0.02
LOSS_SCALE = 256.0
GRP = ("xl", "co")
BLK = ("xh", "y", "z")
ALL = GRP + BLK
SWAP = [(0, 1), (1, 0)]
LANES = 128
F32 = jnp.float32
BF16 = jnp.bfloat16
SEND = jnp.float16


def swap_core(values):
    return lax.ppermute(values, "co", SWAP)


def swap_chip(values):
    return lax.ppermute(values, "xl", SWAP)


def exchange(values, axes):
    return lax.all_to_all(values, axes, split_axis=0, concat_axis=0, tiled=True)


def embed_rows(pooled, gain, bias_rows):
    normed = pooled * lax.rsqrt(jnp.mean(pooled * pooled, axis=-1, keepdims=True) + 1e-05)
    mixture = normed * gain + bias_rows
    return mixture * lax.rsqrt(jnp.sum(mixture * mixture, axis=-1, keepdims=True) + 1e-06)


def gather_kernel(hard_count, ids, q_ref, p_ref, neg_ref, hard_ref, wide, picked):
    rows = q_ref.shape[0]
    wide[...] = p_ref[...].astype(F32)

    def pick(i, carry):
        for k in range(hard_count):
            source = ids[i * hard_count + k]
            picked[k, pl.ds(i, 1), :] = wide[pl.ds(source, 1), :]
        return carry

    lax.fori_loop(0, rows, pick, 0, unroll=8)
    q = q_ref[...].astype(F32)
    lane = lax.broadcasted_iota(jnp.int32, (rows, LANES), 1)
    hard = jnp.zeros((rows, LANES), F32)
    for k in range(hard_count):
        chosen = picked[k]
        neg_ref[k] = chosen.astype(BF16)
        hard = jnp.where(lane == k, jnp.sum(q * chosen, axis=1, keepdims=True), hard)
    hard_ref[...] = hard


def scatter_kernel(hard_count, ids, w_ref, q_ref, neg_ref, add_ref, sum_ref, slot, *parts):
    rows = q_ref.shape[0]
    q = q_ref[...].astype(F32)
    total = jnp.zeros((rows, LANES), F32)
    for k in range(hard_count):
        weight = w_ref[:, k : k + 1].astype(F32)
        slot[k] = weight * q
        total = total + weight * neg_ref[k].astype(F32)
        parts[k][...] = jnp.zeros_like(parts[k])
    sum_ref[...] = total

    def place(i, carry):
        for k in range(hard_count):
            target = pl.ds(ids[i * hard_count + k], 1)
            parts[k][target, :] = parts[k][target, :] + slot[k, pl.ds(i, 1), :]
        return carry

    lax.fori_loop(0, rows, place, 0, unroll=4)
    added = parts[0][...]
    for k in range(1, hard_count):
        added = added + parts[k][...]
    add_ref[...] = added.astype(BF16)


def local(resid, attn, out_proj, out_bias, gain, task_bias, task_ids, neg_owner, neg_row):
    tok_rows = resid.shape[1]
    width = resid.shape[2]
    hard_count = neg_owner.shape[1]
    row_count = 2 * tok_rows
    blocks = lax.axis_size(BLK)
    pairs = blocks * tok_rows
    me = lax.axis_index(GRP)
    core = lax.axis_index("co")
    chip = lax.axis_index("xl")
    vmem = pl.BlockSpec(memory_space=pltpu.VMEM)
    smem = pl.BlockSpec(memory_space=pltpu.SMEM)
    params = pltpu.CompilerParams(vmem_limit_bytes=40 * 1024 * 1024)

    attn_rows = attn.reshape(row_count, width)
    far_rows = swap_chip(attn_rows)
    near_rows = swap_core(attn_rows)

    owner_group = (neg_owner // blocks) ^ me
    own_ids = (owner_group * pairs + (neg_owner % blocks) * tok_rows + neg_row).reshape(1, -1)
    ids = exchange(jnp.broadcast_to(own_ids, (blocks, tok_rows * hard_count)), BLK).reshape(-1)
    near_task = swap_core(task_ids)
    tasks = jnp.concatenate([task_ids, near_task])
    tasks = jnp.concatenate([tasks, swap_chip(tasks)])

    def project(rows):
        return jnp.dot(rows, out_proj, preferred_element_type=F32).astype(BF16)

    chip_columns = project(jnp.concatenate([attn_rows, near_rows]))
    far_columns = project(jnp.concatenate([far_rows, swap_core(far_rows)]))
    parts = [
        chip_columns[:row_count],
        swap_core(chip_columns[row_count:]),
        swap_chip(far_columns[:row_count]),
        lax.ppermute(far_columns[row_count:], GRP, [(0, 3), (1, 2), (2, 1), (3, 0)]),
    ]

    def by_group(items):
        items = [jnp.where(core == 1, items[i ^ 1], items[i]) for i in range(4)]
        return [jnp.where(chip == 1, items[i ^ 2], items[i]) for i in range(4)]

    projected = jnp.concatenate(by_group(parts), axis=1)
    pooled = resid.reshape(row_count, width).astype(F32) + projected.astype(F32) + out_bias
    task_onehot = (jnp.arange(task_bias.shape[0]) == task_ids[0]).astype(F32)
    bias_row = jnp.sum(task_onehot[:, None] * task_bias, axis=0)

    embedded, pullback = jax.vjp(
        lambda a, b, c: embed_rows(a, b, c[None, :]), pooled, gain, bias_row
    )
    emb = embedded.astype(BF16)

    spread = exchange(
        emb.reshape(2, tok_rows, blocks, LANES).transpose(2, 0, 1, 3), BLK
    )
    q_all = spread[:, 0].reshape(pairs, LANES)
    p_own = spread[:, 1].reshape(pairs, LANES)
    p_far = swap_chip(p_own)
    p_all = jnp.concatenate([p_own, swap_core(p_own), p_far, swap_core(p_far)])

    score_part = lax.dot_general(
        q_all, p_own, (((1,), (1,)), ((), ())), preferred_element_type=F32
    )
    negatives, hard_part = pl.pallas_call(
        lambda *refs: gather_kernel(hard_count, *refs),
        out_shape=(
            jax.ShapeDtypeStruct((hard_count, pairs, LANES), BF16),
            jax.ShapeDtypeStruct((pairs, LANES), F32),
        ),
        in_specs=[smem, vmem, vmem],
        out_specs=(vmem, vmem),
        scratch_shapes=[
            pltpu.VMEM((4 * pairs, LANES), F32),
            pltpu.VMEM((hard_count, pairs, LANES), F32),
        ],
        compiler_params=params,
    )(ids, q_all, p_all)
    part = jnp.concatenate([score_part, hard_part], axis=1).astype(SEND)
    part = exchange(part.reshape(blocks, tok_rows, pairs + LANES), BLK)
    scores = jnp.sum(part.astype(F32), axis=0) / TAU

    column = lax.broadcasted_iota(jnp.int32, scores.shape, 1)
    row = lax.broadcasted_iota(jnp.int32, scores.shape, 0)
    weights = jnp.where(column < pairs + hard_count, jnp.exp(scores), 0.0)
    totals = jnp.sum(weights, axis=1, keepdims=True)
    own_column = lax.axis_index(BLK) * tok_rows + row
    own_score = jnp.sum(jnp.where(column == own_column, scores, 0.0), axis=1)
    losses = jnp.log(totals[:, 0]) - own_score
    probs = (weights / totals).astype(BF16)
    probs = exchange(
        jnp.broadcast_to(probs[None], (blocks, tok_rows, pairs + LANES)), BLK
    ).reshape(pairs, pairs + LANES)

    group_probs = probs[:, :pairs]
    hard_add, hard_sum = pl.pallas_call(
        lambda *refs: scatter_kernel(hard_count, *refs),
        out_shape=(
            jax.ShapeDtypeStruct((4 * pairs, LANES), BF16),
            jax.ShapeDtypeStruct((pairs, LANES), F32),
        ),
        in_specs=[smem, vmem, vmem, vmem],
        out_specs=(vmem, vmem),
        scratch_shapes=[pltpu.VMEM((hard_count, pairs, LANES), F32)]
        + [pltpu.VMEM((4 * pairs, LANES), F32)] * hard_count,
        compiler_params=params,
    )(ids, probs[:, pairs:], q_all, negatives)
    hard_add = hard_add.reshape(4, pairs, LANES)
    crossed = swap_core(jnp.stack([hard_add[1], hard_add[3]])).astype(F32)
    over_chip = swap_chip((hard_add[2].astype(F32) + crossed[1]).astype(BF16)).astype(F32)
    sum_q = jnp.dot(group_probs, p_own, preferred_element_type=F32) + hard_sum
    sum_p = lax.dot_general(
        group_probs, q_all, (((0,), (0,)), ((), ())), preferred_element_type=F32
    )
    sum_p = sum_p + (hard_add[0].astype(F32) + crossed[0] + over_chip)
    sums = jnp.stack(
        [sum_q.reshape(blocks, tok_rows, LANES), sum_p.reshape(blocks, tok_rows, LANES)], axis=1
    ).astype(BF16)
    sums = exchange(sums, BLK).transpose(1, 2, 0, 3).reshape(2, tok_rows, width).astype(F32)
    other = jnp.stack([emb[tok_rows:], emb[:tok_rows]]).astype(F32)
    cotangent = ((sums - other) / TAU).reshape(row_count, width)

    d_pooled, d_gain, d_bias = pullback(cotangent)
    d_out_bias = jnp.sum(d_pooled, 0)
    scaled = (LOSS_SCALE * d_pooled).astype(BF16)

    cols = [scaled[:, i * (width // 4) : (i + 1) * (width // 4)] for i in range(4)]
    cols = by_group(cols)
    far_cols = swap_chip(cols[2])
    diag_cols = lax.ppermute(cols[3], GRP, [(0, 3), (1, 2), (2, 1), (3, 0)])
    near_cols = swap_core(cols[1])

    def back(rows):
        return lax.dot_general(
            rows, out_proj, (((1,), (1,)), ((), ())), preferred_element_type=F32
        )

    far_part = back(jnp.concatenate([far_cols, diag_cols]))
    near_part = back(jnp.concatenate([cols[0], near_cols]))
    far_sum = far_part[:row_count] + swap_core(far_part[row_count:].astype(BF16)).astype(F32)
    far_sum = swap_chip(far_sum.astype(BF16)).astype(F32)
    near_sum = near_part[:row_count] + swap_core(near_part[row_count:].astype(BF16)).astype(F32)
    grad_attn = near_sum + far_sum

    vectors = jnp.stack([d_gain, d_out_bias, d_bias]).reshape(3, blocks, LANES).transpose(1, 0, 2)
    vectors = jnp.sum(exchange(vectors, BLK), axis=0)
    pair = jnp.stack([vectors, swap_core(vectors)])
    four = jnp.concatenate([pair, swap_chip(pair)])
    onehot = (tasks[:, None] == jnp.arange(task_bias.shape[0])[None, :]).astype(F32)
    placed = jnp.concatenate(
        [four[:, :2], onehot[:, :, None] * four[:, 2:3]], axis=1
    )
    placed = (placed[0] + placed[1]) + (placed[2] + placed[3])
    whole = exchange(jnp.broadcast_to(placed[None], (blocks,) + placed.shape), BLK)
    whole = whole.transpose(1, 0, 2).reshape(placed.shape[0], width)
    return (
        losses,
        grad_attn.reshape(2, tok_rows, width),
        whole[0],
        whole[2:],
        whole[1],
    )


def solution(mesh):
    fine = Mesh(mesh.devices.reshape(2, 2, 2, 4, 4), ALL)
    in_specs = (
        P(None, ALL, None),
        P(None, ALL, None),
        P(None, GRP),
        P(),
        P(),
        P(),
        P(GRP),
        P(ALL, None),
        P(ALL, None),
    )
    out_specs = (P(ALL), P(None, ALL, None), P(), P(), P())
    return jax.shard_map(local, mesh=fine, in_specs=in_specs, out_specs=out_specs, check_vma=False)
```

```python
import jax
import jax.numpy as jnp
from jax import lax
from jax.experimental import pallas as pl
from jax.experimental.pallas import tpu as pltpu
from jax.sharding import Mesh, PartitionSpec as P

TAU = 0.02
LOSS_SCALE = 256.0
GRP = ("xl", "co")
BLK = ("xh", "y", "z")
ALL = GRP + BLK
SWAP = [(0, 1), (1, 0)]
LANES = 128
F32 = jnp.float32
BF16 = jnp.bfloat16
SEND = jnp.float16


def swap_core(values):
    return lax.ppermute(values, "co", SWAP)


def swap_chip(values):
    return lax.ppermute(values, "xl", SWAP)


def exchange(values, axes):
    return lax.all_to_all(values, axes, split_axis=0, concat_axis=0, tiled=True)


def embed_rows(pooled, gain, bias_rows):
    normed = pooled * lax.rsqrt(jnp.mean(pooled * pooled, axis=-1, keepdims=True) + 1e-05)
    mixture = normed * gain + bias_rows
    return mixture * lax.rsqrt(jnp.sum(mixture * mixture, axis=-1, keepdims=True) + 1e-06)


def gather_kernel(hard_count, tok_rows, ids, q_ref, p_ref, neg_ref, hard_ref, wide, picked):
    rows = q_ref.shape[0]
    wide[...] = p_ref[...].astype(F32)

    def pick(block, carry):
        for i in range(tok_rows):
            for k in range(hard_count):
                source = ids[(block * hard_count + k) * tok_rows + i]
                picked[k, pl.ds(block * tok_rows + i, 1), :] = wide[pl.ds(source, 1), :]
        return carry

    lax.fori_loop(0, rows // tok_rows, pick, 0)
    q = q_ref[...].astype(F32)
    lane = lax.broadcasted_iota(jnp.int32, (rows, LANES), 1)
    hard = jnp.zeros((rows, LANES), F32)
    for k in range(hard_count):
        chosen = picked[k]
        neg_ref[k] = chosen.astype(BF16)
        hard = jnp.where(lane == k, jnp.sum(q * chosen, axis=1, keepdims=True), hard)
    hard_ref[...] = hard


def scatter_kernel(hard_count, tok_rows, ids, w_ref, q_ref, neg_ref, add_ref, sum_ref, slot, *parts):
    rows = q_ref.shape[0]
    q = q_ref[...].astype(F32)
    total = jnp.zeros((rows, LANES), F32)
    for k in range(hard_count):
        weight = w_ref[:, k : k + 1].astype(F32)
        slot[k] = weight * q
        total = total + weight * neg_ref[k].astype(F32)
        parts[k][...] = jnp.zeros_like(parts[k])
    sum_ref[...] = total

    def place(block, carry):
        for i in range(tok_rows):
            for k in range(hard_count):
                target = pl.ds(ids[(block * hard_count + k) * tok_rows + i], 1)
                parts[k][target, :] += slot[k, pl.ds(block * tok_rows + i, 1), :]
        return carry

    lax.fori_loop(0, rows // tok_rows, place, 0)
    added = parts[0][...]
    for k in range(1, hard_count):
        added = added + parts[k][...]
    add_ref[...] = added.astype(BF16)


def local(resid, attn, out_proj, out_bias, gain, task_bias, task_ids, neg_owner, neg_row):
    tok_rows = resid.shape[1]
    width = resid.shape[2]
    hard_count = neg_owner.shape[1]
    row_count = 2 * tok_rows
    blocks = lax.axis_size(BLK)
    pairs = blocks * tok_rows
    me = lax.axis_index(GRP)
    core = lax.axis_index("co")
    chip = lax.axis_index("xl")
    vmem = pl.BlockSpec(memory_space=pltpu.VMEM)
    smem = pl.BlockSpec(memory_space=pltpu.SMEM)
    params = pltpu.CompilerParams(vmem_limit_bytes=40 * 1024 * 1024)

    attn_rows = attn.reshape(row_count, width)
    far_rows = swap_chip(attn_rows)
    near_rows = swap_core(attn_rows)

    out_proj_t = lax.optimization_barrier(out_proj.T)
    near_task = swap_core(task_ids)
    tasks = jnp.concatenate([task_ids, near_task])
    tasks = jnp.concatenate([tasks, swap_chip(tasks)])

    def project(rows):
        return jnp.dot(rows, out_proj, preferred_element_type=F32).astype(BF16)

    chip_columns = project(jnp.concatenate([attn_rows, near_rows]))
    far_rows, chip_columns = lax.optimization_barrier((far_rows, chip_columns))
    far_columns = project(jnp.concatenate([far_rows, swap_core(far_rows)]))
    parts = [
        chip_columns[:row_count],
        swap_core(chip_columns[row_count:]),
        swap_chip(far_columns[:row_count]),
        lax.ppermute(far_columns[row_count:], GRP, [(0, 3), (1, 2), (2, 1), (3, 0)]),
    ]

    def by_group(items):
        items = [jnp.where(core == 1, items[i ^ 1], items[i]) for i in range(4)]
        return [jnp.where(chip == 1, items[i ^ 2], items[i]) for i in range(4)]

    projected = jnp.concatenate(by_group(parts), axis=1)
    pooled = resid.reshape(row_count, width).astype(F32) + projected.astype(F32) + out_bias
    task_onehot = (jnp.arange(task_bias.shape[0]) == task_ids[0]).astype(F32)
    bias_row = jnp.sum(task_onehot[:, None] * task_bias, axis=0)

    embedded, pullback = jax.vjp(
        lambda a, b, c: embed_rows(a, b, c[None, :]), pooled, gain, bias_row
    )
    emb = embedded.astype(BF16)

    half = LANES // 2
    fill = ((0, 1), (0, half - tok_rows))
    requests = jnp.concatenate(
        [jnp.pad(neg_owner.T, fill), jnp.pad(neg_row.T, fill)], axis=1
    ).astype(BF16)
    spread = emb.reshape(2, tok_rows, blocks, LANES).transpose(2, 0, 1, 3)
    spread = jnp.concatenate(
        [
            spread.reshape(blocks, row_count, LANES),
            jnp.broadcast_to(requests[None], (blocks,) + requests.shape),
        ],
        axis=1,
    )
    spread = exchange(spread, BLK)
    q_all = spread[:, :tok_rows].reshape(pairs, LANES)
    p_own = spread[:, tok_rows:row_count].reshape(pairs, LANES)
    requests = spread[:, row_count : row_count + hard_count].astype(jnp.int32)
    owner = requests[:, :, :tok_rows]
    ids = ((owner // blocks) ^ me) * pairs + (owner % blocks) * tok_rows
    ids = (ids + requests[:, :, half : half + tok_rows]).reshape(-1)
    p_far = swap_chip(p_own)
    p_all = jnp.concatenate([p_own, swap_core(p_own), p_far, swap_core(p_far)])

    score_part = lax.dot_general(
        q_all, p_own, (((1,), (1,)), ((), ())), preferred_element_type=F32
    )
    negatives, hard_part = pl.pallas_call(
        lambda *refs: gather_kernel(hard_count, tok_rows, *refs),
        out_shape=(
            jax.ShapeDtypeStruct((hard_count, pairs, LANES), BF16),
            jax.ShapeDtypeStruct((pairs, LANES), F32),
        ),
        in_specs=[smem, vmem, vmem],
        out_specs=(vmem, vmem),
        scratch_shapes=[
            pltpu.VMEM((4 * pairs, LANES), F32),
            pltpu.VMEM((hard_count, pairs, LANES), F32),
        ],
        compiler_params=params,
    )(ids, q_all, p_all)
    score_part = exchange(score_part.astype(SEND).reshape(blocks, tok_rows, pairs), BLK)
    score_part, hard_part = lax.optimization_barrier((score_part, hard_part))
    hard_part = exchange(hard_part.astype(SEND).reshape(blocks, tok_rows, LANES), BLK)
    scores = jnp.sum(score_part.astype(F32), axis=0) / TAU
    hard = jnp.sum(hard_part.astype(F32), axis=0) / TAU

    column = lax.broadcasted_iota(jnp.int32, scores.shape, 1)
    row = lax.broadcasted_iota(jnp.int32, scores.shape, 0)
    weights = jnp.exp(scores)
    slot = lax.broadcasted_iota(jnp.int32, hard.shape, 1)
    hard_weights = jnp.where(slot < hard_count, jnp.exp(hard), 0.0)
    totals = jnp.sum(weights, axis=1, keepdims=True) + jnp.sum(hard_weights, axis=1, keepdims=True)
    own_column = lax.axis_index(BLK) * tok_rows + row
    own_score = jnp.sum(jnp.where(column == own_column, scores, 0.0), axis=1)
    losses = jnp.log(totals[:, 0]) - own_score

    def spread_rows(values):
        values = values.astype(BF16)
        values = exchange(jnp.broadcast_to(values[None], (blocks,) + values.shape), BLK)
        return values.reshape((pairs,) + values.shape[2:])

    group_probs = spread_rows(weights / totals)
    hard_probs = spread_rows(hard_weights / totals)

    hard_add, hard_sum = pl.pallas_call(
        lambda *refs: scatter_kernel(hard_count, tok_rows, *refs),
        out_shape=(
            jax.ShapeDtypeStruct((4 * pairs, LANES), BF16),
            jax.ShapeDtypeStruct((pairs, LANES), F32),
        ),
        in_specs=[smem, vmem, vmem, vmem],
        out_specs=(vmem, vmem),
        scratch_shapes=[pltpu.VMEM((hard_count, pairs, LANES), F32)]
        + [pltpu.VMEM((4 * pairs, LANES), F32)] * hard_count,
        compiler_params=params,
    )(ids, hard_probs, q_all, negatives)
    hard_add = hard_add.reshape(4, pairs, LANES)
    crossed = swap_core(jnp.stack([hard_add[1], hard_add[3]])).astype(F32)
    over_chip = swap_chip((hard_add[2].astype(F32) + crossed[1]).astype(BF16)).astype(F32)
    sum_q = jnp.dot(group_probs, p_own, preferred_element_type=F32) + hard_sum
    sum_p = lax.dot_general(
        group_probs, q_all, (((0,), (0,)), ((), ())), preferred_element_type=F32
    )
    sum_p = sum_p + (hard_add[0].astype(F32) + crossed[0] + over_chip)
    sums = jnp.stack(
        [sum_q.reshape(blocks, tok_rows, LANES), sum_p.reshape(blocks, tok_rows, LANES)], axis=1
    ).astype(BF16)
    sums = exchange(sums, BLK).transpose(1, 2, 0, 3).reshape(2, tok_rows, width).astype(F32)
    other = jnp.stack([emb[tok_rows:], emb[:tok_rows]]).astype(F32)
    cotangent = ((sums - other) / TAU).reshape(row_count, width)

    d_pooled, d_gain, d_bias = pullback(cotangent)
    d_out_bias = jnp.sum(d_pooled, 0)
    scaled = (LOSS_SCALE * d_pooled).astype(BF16)


    cols = [scaled[:, i * (width // 4) : (i + 1) * (width // 4)] for i in range(4)]
    cols = by_group(cols)
    far_cols = swap_chip(cols[2])
    diag_cols = lax.ppermute(cols[3], GRP, [(0, 3), (1, 2), (2, 1), (3, 0)])
    near_cols = swap_core(cols[1])
    d_gain, d_out_bias, d_bias, near_cols = lax.optimization_barrier(
        (d_gain, d_out_bias, d_bias, near_cols)
    )

    def back(rows):
        return lax.dot_general(
            rows, out_proj_t, (((1,), (0,)), ((), ())), preferred_element_type=F32
        )

    vectors = jnp.stack([d_gain, d_out_bias, d_bias]).reshape(3, blocks, LANES).transpose(1, 0, 2)
    vectors, far_cols, diag_cols = lax.optimization_barrier(
        (exchange(vectors, BLK), far_cols, diag_cols)
    )
    vectors = jnp.sum(vectors, axis=0)
    far_part = back(jnp.concatenate([far_cols, diag_cols]))
    far_sum = far_part[:row_count] + swap_core(far_part[row_count:].astype(BF16)).astype(F32)
    far_sum, near_cols = lax.optimization_barrier((far_sum.astype(BF16), near_cols))
    far_sum = swap_chip(far_sum).astype(F32)
    near_part = back(jnp.concatenate([cols[0], near_cols]))
    near_sum = near_part[:row_count] + swap_core(near_part[row_count:].astype(BF16)).astype(F32)
    grad_attn = near_sum + far_sum

    pair = jnp.stack([vectors, swap_core(vectors)])
    four = jnp.concatenate([pair, swap_chip(pair)])
    onehot = (tasks[:, None] == jnp.arange(task_bias.shape[0])[None, :]).astype(F32)
    placed = jnp.concatenate(
        [four[:, :2], onehot[:, :, None] * four[:, 2:3]], axis=1
    )
    placed = (placed[0] + placed[1]) + (placed[2] + placed[3])
    whole = exchange(jnp.broadcast_to(placed[None], (blocks,) + placed.shape), BLK)
    whole = whole.transpose(1, 0, 2).reshape(placed.shape[0], width)
    return (
        losses,
        grad_attn.reshape(2, tok_rows, width),
        whole[0],
        whole[2:],
        whole[1],
    )


def solution(mesh):
    fine = Mesh(mesh.devices.reshape(2, 2, 2, 4, 4), ALL)
    in_specs = (
        P(None, ALL, None),
        P(None, ALL, None),
        P(None, GRP),
        P(),
        P(),
        P(),
        P(GRP),
        P(ALL, None),
        P(ALL, None),
    )
    out_specs = (P(ALL), P(None, ALL, None), P(), P(), P())
    return jax.shard_map(local, mesh=fine, in_specs=in_specs, out_specs=out_specs, check_vma=False)
```

```python
import jax
import jax.numpy as jnp
from jax import lax
from jax.experimental import pallas as pl
from jax.experimental.pallas import tpu as pltpu
from jax.sharding import Mesh, PartitionSpec as P

TAU = 0.02
LOSS_SCALE = 256.0
GRP = ("xl", "co")
BLK = ("xh", "y", "z")
ALL = GRP + BLK
SWAP = [(0, 1), (1, 0)]
LANES = 128
F32 = jnp.float32
BF16 = jnp.bfloat16
SEND = jnp.float16


def swap_core(values):
    return lax.ppermute(values, "co", SWAP)


def swap_chip(values):
    return lax.ppermute(values, "xl", SWAP)


def from_ahead(values, axis, step):
    size = lax.axis_size(axis)
    return lax.ppermute(values, axis, [((i + step) % size, i) for i in range(size)])


def sum_over(values, axis):
    if lax.axis_size(axis) == 2:
        return values + from_ahead(values, axis, 1)
    one, two, three = [from_ahead(values, axis, step) for step in (1, 2, 3)]
    return (values + two) + (one + three)


def gather_ahead(values, axis):
    return jnp.stack(
        [values] + [from_ahead(values, axis, step) for step in range(1, lax.axis_size(axis))]
    )


def exchange(values, axes):
    return lax.all_to_all(values, axes, split_axis=0, concat_axis=0, tiled=True)


def embed_rows(pooled, gain, bias_rows):
    normed = pooled * lax.rsqrt(jnp.mean(pooled * pooled, axis=-1, keepdims=True) + 1e-05)
    mixture = normed * gain + bias_rows
    return mixture * lax.rsqrt(jnp.sum(mixture * mixture, axis=-1, keepdims=True) + 1e-06)


def gather_kernel(hard_count, tok_rows, ids, q_ref, p_ref, neg_ref, hard_ref, wide, picked):
    rows = q_ref.shape[0]
    wide[...] = p_ref[...].astype(F32)

    def pick(block, carry):
        for i in range(tok_rows):
            for k in range(hard_count):
                source = ids[(block * hard_count + k) * tok_rows + i]
                picked[k, pl.ds(block * tok_rows + i, 1), :] = wide[pl.ds(source, 1), :]
        return carry

    lax.fori_loop(0, rows // tok_rows, pick, 0)
    q = q_ref[...].astype(F32)
    lane = lax.broadcasted_iota(jnp.int32, (rows, LANES), 1)
    hard = jnp.zeros((rows, LANES), F32)
    for k in range(hard_count):
        chosen = picked[k]
        neg_ref[k] = chosen.astype(BF16)
        hard = jnp.where(lane == k, jnp.sum(q * chosen, axis=1, keepdims=True), hard)
    hard_ref[...] = hard


def scatter_kernel(hard_count, tok_rows, ids, place_ref, w_ref, q_ref, neg_ref, add_ref, sum_ref, slot, negf, *parts):
    rows = q_ref.shape[0]
    for k in range(hard_count):
        negf[k] = neg_ref[k].astype(F32)
    for part in parts:
        part[...] = jnp.zeros_like(part)
    q = q_ref[...].astype(F32)
    for block in range(rows // tok_rows):
        ahead_z = lax.rem(block % 4 + 4 - place_ref[2], 4)
        ahead_y = lax.rem(block // 4 % 4 + 4 - place_ref[1], 4)
        ahead_x = lax.rem(block // 16 + 2 - place_ref[0], 2)
        source = pl.multiple_of((ahead_z * 8 + ahead_y * 2 + ahead_x) * tok_rows, 8)
        weight = w_ref[pl.ds(source, tok_rows), :]
        here = slice(block * tok_rows, (block + 1) * tok_rows)
        total = jnp.zeros((tok_rows, LANES), F32)
        for k in range(hard_count):
            one = weight[:, k : k + 1]
            slot[k, here, :] = one * q[here]
            total = total + one * negf[k, here, :]
        sum_ref[here, :] = total

    def place(block, carry):
        for i in range(tok_rows):
            for k in range(hard_count):
                target = pl.ds(ids[(block * hard_count + k) * tok_rows + i], 1)
                parts[k][target, :] += slot[k, pl.ds(block * tok_rows + i, 1), :]
        return carry

    lax.fori_loop(0, rows // tok_rows, place, 0)
    added = parts[0][...]
    for k in range(1, hard_count):
        added = added + parts[k][...]
    add_ref[...] = added.astype(BF16)


def local(resid, attn, out_proj, out_bias, gain, task_bias, task_ids, neg_owner, neg_row):
    tok_rows = resid.shape[1]
    width = resid.shape[2]
    hard_count = neg_owner.shape[1]
    row_count = 2 * tok_rows
    blocks = lax.axis_size(BLK)
    pairs = blocks * tok_rows
    me = lax.axis_index(GRP)
    core = lax.axis_index("co")
    chip = lax.axis_index("xl")
    vmem = pl.BlockSpec(memory_space=pltpu.VMEM)
    smem = pl.BlockSpec(memory_space=pltpu.SMEM)
    params = pltpu.CompilerParams(vmem_limit_bytes=24 * 1024 * 1024)

    attn_rows = attn.reshape(row_count, width)
    far_rows = swap_chip(attn_rows)
    near_rows = swap_core(attn_rows)

    out_proj_t = lax.optimization_barrier(out_proj.T)
    near_task = swap_core(task_ids)
    tasks = jnp.concatenate([task_ids, near_task])
    tasks = jnp.concatenate([tasks, swap_chip(tasks)])

    def project(rows):
        return jnp.dot(rows, out_proj, preferred_element_type=F32).astype(BF16)

    chip_columns = project(jnp.concatenate([attn_rows, near_rows]))
    far_rows, chip_columns = lax.optimization_barrier((far_rows, chip_columns))
    far_columns = project(jnp.concatenate([far_rows, swap_core(far_rows)]))
    tasks, far_columns = lax.optimization_barrier((tasks, far_columns))
    parts = [
        chip_columns[:row_count],
        swap_core(chip_columns[row_count:]),
        swap_chip(far_columns[:row_count]),
        lax.ppermute(far_columns[row_count:], GRP, [(0, 3), (1, 2), (2, 1), (3, 0)]),
    ]

    def by_group(items):
        items = [jnp.where(core == 1, items[i ^ 1], items[i]) for i in range(4)]
        return [jnp.where(chip == 1, items[i ^ 2], items[i]) for i in range(4)]

    projected = jnp.concatenate(by_group(parts), axis=1)
    pooled = resid.reshape(row_count, width).astype(F32) + projected.astype(F32) + out_bias
    task_onehot = (jnp.arange(task_bias.shape[0]) == task_ids[0]).astype(F32)
    bias_row = jnp.sum(task_onehot[:, None] * task_bias, axis=0)

    embedded, pullback = jax.vjp(
        lambda a, b, c: embed_rows(a, b, c[None, :]), pooled, gain, bias_row
    )
    emb = embedded.astype(BF16)

    half = LANES // 2
    fill = ((0, 1), (0, half - tok_rows))
    requests = jnp.concatenate(
        [jnp.pad(neg_owner.T, fill), jnp.pad(neg_row.T, fill)], axis=1
    ).astype(BF16)
    spread = emb.reshape(2, tok_rows, blocks, LANES).transpose(2, 0, 1, 3)
    spread = jnp.concatenate(
        [
            spread.reshape(blocks, row_count, LANES),
            jnp.broadcast_to(requests[None], (blocks,) + requests.shape),
        ],
        axis=1,
    )
    spread = exchange(spread, BLK)
    q_all = spread[:, :tok_rows].reshape(pairs, LANES)
    p_own = spread[:, tok_rows:row_count].reshape(pairs, LANES)
    requests = spread[:, row_count : row_count + hard_count].astype(jnp.int32)
    owner = requests[:, :, :tok_rows]
    ids = ((owner // blocks) ^ me) * pairs + (owner % blocks) * tok_rows
    ids = (ids + requests[:, :, half : half + tok_rows]).reshape(-1)
    p_far = swap_chip(p_own)
    p_all = jnp.concatenate([p_own, swap_core(p_own), p_far, swap_core(p_far)])

    score_part = lax.dot_general(
        q_all, p_own, (((1,), (1,)), ((), ())), preferred_element_type=F32
    )
    negatives, hard_part = pl.pallas_call(
        lambda *refs: gather_kernel(hard_count, tok_rows, *refs),
        out_shape=(
            jax.ShapeDtypeStruct((hard_count, pairs, LANES), BF16),
            jax.ShapeDtypeStruct((pairs, LANES), F32),
        ),
        in_specs=[smem, vmem, vmem],
        out_specs=(vmem, vmem),
        scratch_shapes=[
            pltpu.VMEM((4 * pairs, LANES), F32),
            pltpu.VMEM((hard_count, pairs, LANES), F32),
        ],
        compiler_params=params,
    )(ids, q_all, p_all)
    part = jnp.concatenate([score_part, hard_part], axis=1).astype(SEND)
    part = exchange(part.reshape(blocks, tok_rows, pairs + LANES), BLK)
    part = jnp.sum(part.astype(F32), axis=0) / TAU
    scores = part[:, :pairs]
    hard = part[:, pairs:]

    column = lax.broadcasted_iota(jnp.int32, scores.shape, 1)
    row = lax.broadcasted_iota(jnp.int32, scores.shape, 0)
    weights = jnp.exp(scores)
    slot = lax.broadcasted_iota(jnp.int32, hard.shape, 1)
    hard_weights = jnp.where(slot < hard_count, jnp.exp(hard), 0.0)
    totals = jnp.sum(weights, axis=1, keepdims=True) + jnp.sum(hard_weights, axis=1, keepdims=True)
    own_column = lax.axis_index(BLK) * tok_rows + row
    own_score = jnp.sum(jnp.where(column == own_column, scores, 0.0), axis=1)
    losses = jnp.log(totals[:, 0]) - own_score

    def spread_rows(values):
        values = values.astype(BF16)
        values = exchange(jnp.broadcast_to(values[None], (blocks,) + values.shape), BLK)
        return values.reshape((pairs,) + values.shape[2:])

    hard_probs = (hard_weights / totals).astype(BF16)
    for axis in BLK:
        hard_probs = gather_ahead(hard_probs, axis)
    hard_probs = hard_probs.astype(F32).reshape(pairs, LANES)
    hard_probs, probs = lax.optimization_barrier((hard_probs, weights / totals))
    group_probs = spread_rows(probs)
    place = jnp.stack([lax.axis_index(axis) for axis in BLK]).astype(jnp.int32)

    hard_add, hard_sum = pl.pallas_call(
        lambda *refs: scatter_kernel(hard_count, tok_rows, *refs),
        out_shape=(
            jax.ShapeDtypeStruct((4 * pairs, LANES), BF16),
            jax.ShapeDtypeStruct((pairs, LANES), F32),
        ),
        in_specs=[smem, smem, vmem, vmem, vmem],
        out_specs=(vmem, vmem),
        scratch_shapes=[pltpu.VMEM((hard_count, pairs, LANES), F32)] * 2
        + [pltpu.VMEM((4 * pairs, LANES), F32)] * hard_count,
        compiler_params=params,
    )(ids, place, hard_probs, q_all, negatives)
    hard_add = hard_add.reshape(4, pairs, LANES)
    crossed = swap_core(jnp.stack([hard_add[1], hard_add[3]])).astype(F32)
    over_chip = swap_chip((hard_add[2].astype(F32) + crossed[1]).astype(BF16)).astype(F32)
    sum_q = jnp.dot(group_probs, p_own, preferred_element_type=F32) + hard_sum
    sum_p = lax.dot_general(
        group_probs, q_all, (((0,), (0,)), ((), ())), preferred_element_type=F32
    )
    sum_p = sum_p + (hard_add[0].astype(F32) + crossed[0] + over_chip)
    sums = jnp.stack(
        [sum_q.reshape(blocks, tok_rows, LANES), sum_p.reshape(blocks, tok_rows, LANES)], axis=1
    ).astype(BF16)
    sums = exchange(sums, BLK).transpose(1, 2, 0, 3).reshape(2, tok_rows, width).astype(F32)
    other = jnp.stack([emb[tok_rows:], emb[:tok_rows]]).astype(F32)
    cotangent = ((sums - other) / TAU).reshape(row_count, width)

    d_pooled, d_gain, d_bias = pullback(cotangent)
    d_out_bias = jnp.sum(d_pooled, 0)
    scaled = (LOSS_SCALE * d_pooled).astype(BF16)


    cols = [scaled[:, i * (width // 4) : (i + 1) * (width // 4)] for i in range(4)]
    lines = width // LANES
    vectors = jnp.concatenate([d_gain, d_out_bias, d_bias]).reshape(3 * lines, LANES)
    cols = by_group(cols)
    far_cols = swap_chip(cols[2])
    diag_cols = lax.ppermute(cols[3], GRP, [(0, 3), (1, 2), (2, 1), (3, 0)])
    near_cols = swap_core(cols[1])

    def back(rows):
        return lax.dot_general(
            rows, out_proj_t, (((1,), (0,)), ((), ())), preferred_element_type=F32
        )

    vectors, near_cols = lax.optimization_barrier((vectors, near_cols))
    vectors = sum_over(sum_over(vectors, "z"), "y")
    near_part = back(jnp.concatenate([cols[0], near_cols]))
    far_cols, diag_cols, near_part, vectors = lax.optimization_barrier(
        (far_cols, diag_cols, near_part, vectors)
    )
    far_part = back(jnp.concatenate([far_cols, diag_cols]))
    vectors = sum_over(vectors, "xh")
    far_part, vectors = lax.optimization_barrier((far_part, vectors))
    far_sum = far_part[:row_count] + swap_core(far_part[row_count:].astype(BF16)).astype(F32)
    near = swap_core(vectors)
    far_sum, near = lax.optimization_barrier((far_sum.astype(BF16), near))
    far_sum = swap_chip(far_sum).astype(F32)
    near_sum = near_part[:row_count] + swap_core(near_part[row_count:].astype(BF16)).astype(F32)
    grad_attn = near_sum + far_sum

    vectors = jnp.concatenate(
        [vectors[: 2 * lines] + near[: 2 * lines], vectors[2 * lines :], near[2 * lines :]]
    )
    far = swap_chip(vectors)
    both = (vectors + far)[: 2 * lines].reshape(2, width)
    task_rows = jnp.concatenate([vectors[2 * lines :], far[2 * lines :]]).reshape(4, 1, width)
    onehot = (tasks[:, None] == jnp.arange(task_bias.shape[0])[None, :]).astype(F32)
    placed = onehot[:, :, None] * task_rows
    placed = (placed[0] + placed[1]) + (placed[2] + placed[3])
    return (
        losses,
        grad_attn.reshape(2, tok_rows, width),
        both[0],
        placed,
        both[1],
    )


def solution(mesh):
    fine = Mesh(mesh.devices.reshape(2, 2, 2, 4, 4), ALL)
    in_specs = (
        P(None, ALL, None),
        P(None, ALL, None),
        P(None, GRP),
        P(),
        P(),
        P(),
        P(GRP),
        P(ALL, None),
        P(ALL, None),
    )
    out_specs = (P(ALL), P(None, ALL, None), P(), P(), P())
    return jax.shard_map(local, mesh=fine, in_specs=in_specs, out_specs=out_specs, check_vma=False)
```

```python
import jax
import jax.numpy as jnp
from jax import lax
from jax.experimental import pallas as pl
from jax.experimental.pallas import tpu as pltpu
from jax.sharding import Mesh, PartitionSpec as P

TAU = 0.02
LOSS_SCALE = 256.0
GRP = ("xl", "co")
BLK = ("xh", "y", "z")
ALL = GRP + BLK
SWAP = [(0, 1), (1, 0)]
DIAGONAL = [(0, 3), (1, 2), (2, 1), (3, 0)]
LANES = 128
F32 = jnp.float32
BF16 = jnp.bfloat16
SEND = jnp.float16


def swap_core(values):
    return lax.ppermute(values, "co", SWAP)


def swap_chip(values):
    return lax.ppermute(values, "xl", SWAP)


def from_ahead(values, axis, step):
    size = lax.axis_size(axis)
    return lax.ppermute(values, axis, [((i + step) % size, i) for i in range(size)])


def sum_over(values, axis):
    if lax.axis_size(axis) == 2:
        return values + from_ahead(values, axis, 1)
    one, two, three = [from_ahead(values, axis, step) for step in (1, 2, 3)]
    return (values + two) + (one + three)


def gather_ahead(values, axis):
    return jnp.stack(
        [values] + [from_ahead(values, axis, step) for step in range(1, lax.axis_size(axis))]
    )


def exchange(values, axes):
    return lax.all_to_all(values, axes, split_axis=0, concat_axis=0, tiled=True)


def embed_rows(pooled, gain, bias_rows):
    normed = pooled * lax.rsqrt(jnp.mean(pooled * pooled, axis=-1, keepdims=True) + 1e-05)
    mixture = normed * gain + bias_rows
    return mixture * lax.rsqrt(jnp.sum(mixture * mixture, axis=-1, keepdims=True) + 1e-06)


def gather_kernel(hard_count, tok_rows, ids, q_ref, p_ref, neg_ref, hard_ref, wide, picked):
    rows = q_ref.shape[0]
    wide[...] = p_ref[...].astype(F32)

    def pick(block, carry):
        for i in range(tok_rows):
            for k in range(hard_count):
                source = ids[(block * hard_count + k) * tok_rows + i]
                picked[k, pl.ds(block * tok_rows + i, 1), :] = wide[pl.ds(source, 1), :]
        return carry

    lax.fori_loop(0, rows // tok_rows, pick, 0)
    q = q_ref[...].astype(F32)
    lane = lax.broadcasted_iota(jnp.int32, (rows, LANES), 1)
    hard = jnp.zeros((rows, LANES), F32)
    for k in range(hard_count):
        chosen = picked[k]
        neg_ref[k] = chosen.astype(BF16)
        hard = jnp.where(lane == k, jnp.sum(q * chosen, axis=1, keepdims=True), hard)
    hard_ref[...] = hard


def scatter_kernel(hard_count, tok_rows, ids, w_ref, q_ref, neg_ref, add_ref, sum_ref, slot, *parts):
    rows = q_ref.shape[0]
    for part in parts:
        part[...] = jnp.zeros_like(part)
    q = q_ref[...].astype(F32)
    total = jnp.zeros((rows, LANES), F32)
    for k in range(hard_count):
        weight = w_ref[:, k : k + 1].astype(F32)
        slot[k] = weight * q
        total = total + weight * neg_ref[k].astype(F32)
    sum_ref[...] = total

    def place(block, carry):
        for i in range(tok_rows):
            for k in range(hard_count):
                target = pl.ds(ids[(block * hard_count + k) * tok_rows + i], 1)
                parts[k][target, :] += slot[k, pl.ds(block * tok_rows + i, 1), :]
        return carry

    lax.fori_loop(0, rows // tok_rows, place, 0)
    added = parts[0][...]
    for k in range(1, hard_count):
        added = added + parts[k][...]
    add_ref[...] = added.astype(BF16)


def stream_chunks(w_ref, held, sems):
    chunks, depth = held.shape[0], held.shape[1]
    copies = [
        pltpu.make_async_copy(w_ref.at[pl.ds(c * depth, depth), :], held.at[c], sems.at[c])
        for c in range(chunks)
    ]
    for copy in copies:
        copy.start()
    return copies


def forward_kernel(x0, x1, x2, x3, w_ref, y0, y1, y2, y3, held, total, sems):
    depth = held.shape[1]
    rows = y0.shape[0]
    for c, copy in enumerate(stream_chunks(w_ref, held, sems)):
        copy.wait()
        here = slice(c * depth, (c + 1) * depth)
        x = jnp.concatenate([x_ref[:, here] for x_ref in (x0, x1, x2, x3)])
        term = jnp.dot(x, held[c], preferred_element_type=F32)
        total[...] = term if c == 0 else total[...] + term
    for i, y_ref in enumerate((y0, y1, y2, y3)):
        y_ref[...] = total[i * rows : (i + 1) * rows, :].astype(BF16)


def backward_kernel(x0, x1, x2, x3, w_ref, y0, y1, y2, y3, held, sems):
    depth = held.shape[1]
    rows = y0.shape[0]
    copies = stream_chunks(w_ref, held, sems)
    x = jnp.concatenate([x_ref[:rows, :] for x_ref in (x0, x1, x2, x3)])
    for c, copy in enumerate(copies):
        copy.wait()
        term = lax.dot_general(x, held[c], (((1,), (1,)), ((), ())), preferred_element_type=F32)
        for i, y_ref in enumerate((y0, y1, y2, y3)):
            y_ref[:, c * depth : (c + 1) * depth] = term[i * rows : (i + 1) * rows].astype(BF16)


def local(resid, attn, out_proj, out_bias, gain, task_bias, task_ids, neg_owner, neg_row):
    tok_rows = resid.shape[1]
    width = resid.shape[2]
    hard_count = neg_owner.shape[1]
    row_count = 2 * tok_rows
    blocks = lax.axis_size(BLK)
    pairs = blocks * tok_rows
    me = lax.axis_index(GRP)
    core = lax.axis_index("co")
    chip = lax.axis_index("xl")
    vmem = pl.BlockSpec(memory_space=pltpu.VMEM)
    smem = pl.BlockSpec(memory_space=pltpu.SMEM)
    params = pltpu.CompilerParams(vmem_limit_bytes=24 * 1024 * 1024)

    attn_rows = attn.reshape(row_count, width)
    far_rows = swap_chip(attn_rows)
    near_rows = swap_core(attn_rows)


    chunks = 8
    held = [
        pltpu.VMEM((chunks, out_proj.shape[0] // chunks, out_proj.shape[1]), BF16),
        pltpu.SemaphoreType.DMA((chunks,)),
    ]
    hbm = pl.BlockSpec(memory_space=pl.ANY)
    columns = pl.pallas_call(
        forward_kernel,
        out_shape=[jax.ShapeDtypeStruct((row_count, out_proj.shape[1]), BF16)] * 4,
        in_specs=[vmem] * 4 + [hbm],
        out_specs=[vmem] * 4,
        scratch_shapes=[held[0], pltpu.VMEM((4 * row_count, out_proj.shape[1]), F32), held[1]],
        compiler_params=params,
    )(attn_rows, near_rows, far_rows, swap_core(far_rows), out_proj)
    parts = [
        columns[0],
        swap_core(columns[1]),
        swap_chip(columns[2]),
        lax.ppermute(columns[3], GRP, DIAGONAL),
    ]

    def by_group(items):
        items = [jnp.where(core == 1, items[i ^ 1], items[i]) for i in range(4)]
        return [jnp.where(chip == 1, items[i ^ 2], items[i]) for i in range(4)]

    projected = jnp.concatenate(by_group(parts), axis=1)
    pooled = resid.reshape(row_count, width).astype(F32) + projected.astype(F32) + out_bias
    task_onehot = (jnp.arange(task_bias.shape[0]) == task_ids[0]).astype(F32)
    bias_row = jnp.sum(task_onehot[:, None] * task_bias, axis=0)

    embedded, pullback = jax.vjp(
        lambda a, b, c: embed_rows(a, b, c[None, :]), pooled, gain, bias_row
    )
    emb = embedded.astype(BF16)

    half = LANES // 2
    fill = ((0, 1), (0, half - tok_rows))
    requests = jnp.concatenate(
        [jnp.pad(neg_owner.T, fill), jnp.pad(neg_row.T, fill)], axis=1
    ).astype(BF16)
    spread = emb.reshape(2, tok_rows, blocks, LANES).transpose(2, 0, 1, 3)
    spread = jnp.concatenate(
        [
            spread.reshape(blocks, row_count, LANES),
            jnp.broadcast_to(requests[None], (blocks,) + requests.shape),
        ],
        axis=1,
    )
    spread = exchange(spread, BLK)
    q_all = spread[:, :tok_rows].reshape(pairs, LANES)
    p_own = spread[:, tok_rows:row_count].reshape(pairs, LANES)
    requests = spread[:, row_count : row_count + hard_count].astype(jnp.int32)
    owner = requests[:, :, :tok_rows]
    ids = ((owner // blocks) ^ me) * pairs + (owner % blocks) * tok_rows
    ids = (ids + requests[:, :, half : half + tok_rows]).reshape(-1)
    p_far = swap_chip(p_own)
    p_all = jnp.concatenate([p_own, swap_core(p_own), p_far, swap_core(p_far)])

    score_part = lax.dot_general(
        q_all, p_own, (((1,), (1,)), ((), ())), preferred_element_type=F32
    )
    negatives, hard_part = pl.pallas_call(
        lambda *refs: gather_kernel(hard_count, tok_rows, *refs),
        out_shape=(
            jax.ShapeDtypeStruct((hard_count, pairs, LANES), BF16),
            jax.ShapeDtypeStruct((pairs, LANES), F32),
        ),
        in_specs=[smem, vmem, vmem],
        out_specs=(vmem, vmem),
        scratch_shapes=[
            pltpu.VMEM((4 * pairs, LANES), F32),
            pltpu.VMEM((hard_count, pairs, LANES), F32),
        ],
        compiler_params=params,
    )(ids, q_all, p_all)
    part = jnp.concatenate([score_part, hard_part], axis=1).astype(SEND)
    part = exchange(part.reshape(blocks, tok_rows, pairs + LANES), BLK)
    part = jnp.sum(part.astype(F32), axis=0) / TAU
    scores = part[:, :pairs]
    hard = part[:, pairs:]

    column = lax.broadcasted_iota(jnp.int32, scores.shape, 1)
    row = lax.broadcasted_iota(jnp.int32, scores.shape, 0)
    weights = jnp.exp(scores)
    slot = lax.broadcasted_iota(jnp.int32, hard.shape, 1)
    hard_weights = jnp.where(slot < hard_count, jnp.exp(hard), 0.0)
    totals = jnp.sum(weights, axis=1, keepdims=True) + jnp.sum(hard_weights, axis=1, keepdims=True)
    own_column = lax.axis_index(BLK) * tok_rows + row
    own_score = jnp.sum(jnp.where(column == own_column, scores, 0.0), axis=1)
    losses = jnp.log(totals[:, 0]) - own_score

    def spread_rows(values):
        values = values.astype(BF16)
        values = exchange(jnp.broadcast_to(values[None], (blocks,) + values.shape), BLK)
        return values.reshape((pairs,) + values.shape[2:])

    hard_probs = spread_rows(hard_weights / totals)
    group_probs = spread_rows(weights / totals)

    hard_add, hard_sum = pl.pallas_call(
        lambda *refs: scatter_kernel(hard_count, tok_rows, *refs),
        out_shape=(
            jax.ShapeDtypeStruct((4 * pairs, LANES), BF16),
            jax.ShapeDtypeStruct((pairs, LANES), F32),
        ),
        in_specs=[smem, vmem, vmem, vmem],
        out_specs=(vmem, vmem),
        scratch_shapes=[pltpu.VMEM((hard_count, pairs, LANES), F32)]
        + [pltpu.VMEM((4 * pairs, LANES), F32)] * hard_count,
        compiler_params=params,
    )(ids, hard_probs, q_all, negatives)
    hard_add = hard_add.reshape(4, pairs, LANES)
    crossed = swap_core(jnp.stack([hard_add[1], hard_add[3]])).astype(F32)
    over_chip = swap_chip((hard_add[2].astype(F32) + crossed[1]).astype(BF16)).astype(F32)
    sum_q = jnp.dot(group_probs, p_own, preferred_element_type=F32) + hard_sum
    sum_p = lax.dot_general(
        group_probs, q_all, (((0,), (0,)), ((), ())), preferred_element_type=F32
    )
    sum_p = sum_p + (hard_add[0].astype(F32) + crossed[0] + over_chip)
    sums = jnp.stack(
        [sum_q.reshape(blocks, tok_rows, LANES), sum_p.reshape(blocks, tok_rows, LANES)], axis=1
    ).astype(BF16)
    sums = exchange(sums, BLK).transpose(1, 2, 0, 3).reshape(2, tok_rows, width).astype(F32)
    other = jnp.stack([emb[tok_rows:], emb[:tok_rows]]).astype(F32)
    cotangent = ((sums - other) / TAU).reshape(row_count, width)

    d_pooled, d_gain, d_bias = pullback(cotangent)
    d_out_bias = jnp.sum(d_pooled, 0)
    scaled = (LOSS_SCALE * d_pooled).astype(BF16)


    vectors = jnp.stack([d_gain, d_out_bias, d_bias])
    high = vectors.astype(BF16)
    low = (vectors - high.astype(F32)).astype(BF16)
    task = jnp.broadcast_to(task_ids.astype(BF16)[:, None], (2, width))
    cols = jnp.concatenate([scaled, high, low, task])
    cols = by_group(jnp.split(cols, 4, axis=1))
    cols = [
        cols[0],
        swap_core(cols[1]),
        swap_chip(cols[2]),
        lax.ppermute(cols[3], GRP, DIAGONAL),
    ]
    extra = jnp.stack([part[row_count:] for part in cols])
    vectors = extra[:, :3].astype(F32) + extra[:, 3:6].astype(F32)
    tasks = extra[:, 6, :1].astype(jnp.int32)
    both = (vectors[0, :2] + vectors[1, :2]) + (vectors[2, :2] + vectors[3, :2])
    vectors = jnp.concatenate([both, vectors[:, 2]]).reshape(-1, LANES)
    back = pl.pallas_call(
        backward_kernel,
        out_shape=[jax.ShapeDtypeStruct((row_count, width), BF16)] * 4,
        in_specs=[vmem] * 4 + [hbm],
        out_specs=[vmem] * 4,
        scratch_shapes=held,
        compiler_params=params,
    )(*cols, out_proj)
    vectors = sum_over(vectors, "z")
    vectors, *back = lax.optimization_barrier((vectors, *back))
    vectors = sum_over(vectors, "y")
    far_sum = back[2].astype(F32) + swap_core(back[3]).astype(F32)
    far_sum, vectors = lax.optimization_barrier((far_sum.astype(BF16), vectors))
    far_sum = swap_chip(far_sum).astype(F32)
    grad_attn = back[0].astype(F32) + swap_core(back[1]).astype(F32) + far_sum

    vectors = sum_over(vectors, "xh")
    vectors = vectors.reshape(6, -1)
    onehot = (tasks == jnp.arange(task_bias.shape[0])[None, :]).astype(F32)
    placed = onehot[:, :, None] * vectors[2:, None, :]
    placed = (placed[0] + placed[1]) + (placed[2] + placed[3])
    placed = jnp.concatenate([vectors[:2], placed])
    pair = jnp.stack([placed, swap_core(placed)])
    pair, grad_attn = lax.optimization_barrier((pair, grad_attn))
    far = swap_chip(pair)
    whole = jnp.concatenate(by_group([pair[0], pair[1], far[0], far[1]]), axis=1)
    return (
        losses,
        grad_attn.reshape(2, tok_rows, width),
        whole[0],
        whole[2:],
        whole[1],
    )


def solution(mesh):
    fine = Mesh(mesh.devices.reshape(2, 2, 2, 4, 4), ALL)
    in_specs = (
        P(None, ALL, None),
        P(None, ALL, None),
        P(None, GRP),
        P(),
        P(),
        P(),
        P(GRP),
        P(ALL, None),
        P(ALL, None),
    )
    out_specs = (P(ALL), P(None, ALL, None), P(), P(), P())
    return jax.shard_map(local, mesh=fine, in_specs=in_specs, out_specs=out_specs, check_vma=False)
```

```python
import jax
import jax.numpy as jnp
from jax import lax
from jax.experimental import pallas as pl
from jax.experimental.pallas import tpu as pltpu
from jax.sharding import Mesh, PartitionSpec as P

TAU = 0.02
LOSS_SCALE = 256.0
GRP = ("xl", "co")
BLK = ("xh", "y", "z")
ALL = GRP + BLK
SWAP = [(0, 1), (1, 0)]
DIAGONAL = [(0, 3), (1, 2), (2, 1), (3, 0)]
LANES = 128
F32 = jnp.float32
BF16 = jnp.bfloat16
SEND = jnp.float16


def swap_core(values):
    return lax.ppermute(values, "co", SWAP)


def swap_chip(values):
    return lax.ppermute(values, "xl", SWAP)


def from_ahead(values, axis, step):
    size = lax.axis_size(axis)
    return lax.ppermute(values, axis, [((i + step) % size, i) for i in range(size)])


def sum_over(values, axis):
    if lax.axis_size(axis) == 2:
        return values + from_ahead(values, axis, 1)
    one, two, three = [from_ahead(values, axis, step) for step in (1, 2, 3)]
    return (values + two) + (one + three)


def gather_ahead(values, axis):
    return jnp.stack(
        [values] + [from_ahead(values, axis, step) for step in range(1, lax.axis_size(axis))]
    )


def exchange(values, axes):
    return lax.all_to_all(values, axes, split_axis=0, concat_axis=0, tiled=True)


def embed_kernel(
    me, x0, x1, x2, x3, resid, out_bias, gain, bias_row, requests,
    spread, pooled, inv_rms, inv_norm, held,
):
    rows, width = resid.shape
    quarter = width // 4
    for i, x_ref in enumerate((x0, x1, x2, x3)):
        held[i] = x_ref[...]
    squares = jnp.zeros((rows, LANES), F32)
    for b in range(width // LANES):
        here = slice(b * LANES, (b + 1) * LANES)
        start = b * LANES % quarter
        projected = held[me[0] ^ (b * LANES // quarter), :, start : start + LANES]
        value = resid[:, here].astype(F32) + projected.astype(F32) + out_bias[:, here]
        pooled[:, here] = value
        squares = squares + value * value
    mean = jnp.sum(squares, axis=1, keepdims=True) / width
    rms = jnp.broadcast_to(lax.rsqrt(mean + 1e-05), (rows, LANES))
    inv_rms[...] = rms

    def mixture(b):
        here = slice(b * LANES, (b + 1) * LANES)
        return pooled[:, here] * rms * gain[:, here] + bias_row[:, here]

    squares = jnp.zeros((rows, LANES), F32)
    for b in range(width // LANES):
        value = mixture(b)
        squares = squares + value * value
    total = jnp.sum(squares, axis=1, keepdims=True)
    norm = jnp.broadcast_to(lax.rsqrt(total + 1e-06), (rows, LANES))
    inv_norm[...] = norm
    wanted = requests[...].astype(F32)
    for b in range(width // LANES):
        spread[b] = jnp.concatenate([mixture(b) * norm, wanted]).astype(BF16)


def pullback_kernel(
    me, task, sums, spread, pooled, inv_rms, inv_norm, gain, bias_row,
    y0, y1, y2, y3, grad, vectors, held,
):
    rows, width = pooled.shape
    half = rows // 2
    quarter = width // 4
    rms, norm = inv_rms[...], inv_norm[...]

    def across(values):
        return jnp.broadcast_to(jnp.sum(values, axis=1, keepdims=True), values.shape)

    def embedded(b):
        here = slice(b * LANES, (b + 1) * LANES)
        normed = pooled[:, here] * rms
        return normed, (normed * gain[:, here] + bias_row[:, here]) * norm

    along = jnp.zeros((rows, LANES), F32)
    for b in range(width // LANES):
        own = spread[b].astype(F32)
        other = jnp.concatenate([own[half:rows], own[:half]])
        both = jnp.concatenate([sums[b, 0].astype(F32), sums[b, 1].astype(F32)])
        cotangent = (both - other) / TAU
        grad[:, b * LANES : (b + 1) * LANES] = cotangent
        along = along + embedded(b)[1] * cotangent
    along = across(along)
    inner = jnp.zeros((rows, LANES), F32)
    for b in range(width // LANES):
        here = slice(b * LANES, (b + 1) * LANES)
        normed, unit = embedded(b)
        d_mixture = norm * (grad[:, here] - unit * along)
        vectors[0:1, here] = jnp.sum(d_mixture * normed, axis=0, keepdims=True)
        vectors[2:3, here] = jnp.sum(d_mixture, axis=0, keepdims=True)
        d_normed = d_mixture * gain[:, here]
        grad[:, here] = d_normed
        inner = inner + d_normed * normed
    inner = across(inner) / width
    line = lax.broadcasted_iota(jnp.int32, (8, LANES), 0)
    for b in range(width // LANES):
        here = slice(b * LANES, (b + 1) * LANES)
        d_pooled = rms * (grad[:, here] - pooled[:, here] * rms * inner)
        three = [
            vectors[0:1, here],
            jnp.sum(d_pooled, axis=0, keepdims=True),
            vectors[2:3, here],
        ]
        extra = jnp.full((8, LANES), task[0].astype(F32))
        for i, value in enumerate(three):
            high = value.astype(BF16).astype(F32)
            extra = jnp.where(line == i, high, extra)
            extra = jnp.where(line == i + 3, value - high, extra)
        start = b * LANES % quarter
        held[b * LANES // quarter, :, start : start + LANES] = jnp.concatenate(
            [LOSS_SCALE * d_pooled, extra]
        ).astype(BF16)
    for i, y_ref in enumerate((y0, y1, y2, y3)):
        y_ref[...] = held[me[0] ^ i]


def gather_kernel(hard_count, tok_rows, ids, q_ref, p_ref, neg_ref, hard_ref, wide, picked):
    rows = q_ref.shape[0]
    wide[...] = p_ref[...].astype(F32)

    def pick(block, carry):
        for i in range(tok_rows):
            for k in range(hard_count):
                source = ids[(block * hard_count + k) * tok_rows + i]
                picked[k, pl.ds(block * tok_rows + i, 1), :] = wide[pl.ds(source, 1), :]
        return carry

    lax.fori_loop(0, rows // tok_rows, pick, 0)
    q = q_ref[...].astype(F32)
    lane = lax.broadcasted_iota(jnp.int32, (rows, LANES), 1)
    hard = jnp.zeros((rows, LANES), F32)
    for k in range(hard_count):
        chosen = picked[k]
        neg_ref[k] = chosen.astype(BF16)
        hard = jnp.where(lane == k, jnp.sum(q * chosen, axis=1, keepdims=True), hard)
    hard_ref[...] = hard


def scatter_kernel(hard_count, tok_rows, ids, w_ref, q_ref, neg_ref, add_ref, sum_ref, slot, *parts):
    rows = q_ref.shape[0]
    for part in parts:
        part[...] = jnp.zeros_like(part)
    q = q_ref[...].astype(F32)
    total = jnp.zeros((rows, LANES), F32)
    for k in range(hard_count):
        weight = w_ref[:, k : k + 1].astype(F32)
        slot[k] = weight * q
        total = total + weight * neg_ref[k].astype(F32)
    sum_ref[...] = total

    def place(block, carry):
        for i in range(tok_rows):
            for k in range(hard_count):
                target = pl.ds(ids[(block * hard_count + k) * tok_rows + i], 1)
                parts[k][target, :] += slot[k, pl.ds(block * tok_rows + i, 1), :]
        return carry

    lax.fori_loop(0, rows // tok_rows, place, 0)
    added = parts[0][...]
    for k in range(1, hard_count):
        added = added + parts[k][...]
    add_ref[...] = added.astype(BF16)


def stream_chunks(w_ref, held, sems):
    chunks, depth = held.shape[0], held.shape[1]
    copies = [
        pltpu.make_async_copy(w_ref.at[pl.ds(c * depth, depth), :], held.at[c], sems.at[c])
        for c in range(chunks)
    ]
    for copy in copies:
        copy.start()
    return copies


def forward_kernel(x0, x1, x2, x3, w_ref, y0, y1, y2, y3, held, total, sems):
    depth = held.shape[1]
    rows = y0.shape[0]
    for c, copy in enumerate(stream_chunks(w_ref, held, sems)):
        copy.wait()
        here = slice(c * depth, (c + 1) * depth)
        x = jnp.concatenate([x_ref[:, here] for x_ref in (x0, x1, x2, x3)])
        term = jnp.dot(x, held[c], preferred_element_type=F32)
        total[...] = term if c == 0 else total[...] + term
    for i, y_ref in enumerate((y0, y1, y2, y3)):
        y_ref[...] = total[i * rows : (i + 1) * rows, :].astype(BF16)


def backward_kernel(x0, x1, x2, x3, w_ref, keep_ref, send_ref, held, sems):
    depth = held.shape[1]
    rows = keep_ref.shape[1]
    copies = stream_chunks(w_ref, held, sems)
    x = jnp.concatenate([x_ref[:rows, :] for x_ref in (x0, x1, x2, x3)])
    for c, copy in enumerate(copies):
        copy.wait()
        term = lax.dot_general(x, held[c], (((1,), (1,)), ((), ())), preferred_element_type=F32)
        here = slice(c * depth, (c + 1) * depth)
        for i in range(4):
            out_ref = send_ref if i % 2 else keep_ref
            out_ref[i // 2, :, here] = term[i * rows : (i + 1) * rows].astype(BF16)


def local(resid, attn, out_proj, out_bias, gain, task_bias, task_ids, neg_owner, neg_row):
    tok_rows = resid.shape[1]
    width = resid.shape[2]
    hard_count = neg_owner.shape[1]
    row_count = 2 * tok_rows
    blocks = lax.axis_size(BLK)
    pairs = blocks * tok_rows
    me = lax.axis_index(GRP)
    core = lax.axis_index("co")
    chip = lax.axis_index("xl")
    vmem = pl.BlockSpec(memory_space=pltpu.VMEM)
    smem = pl.BlockSpec(memory_space=pltpu.SMEM)
    params = pltpu.CompilerParams(vmem_limit_bytes=24 * 1024 * 1024)

    stream = pltpu.CompilerParams(vmem_limit_bytes=52 * 1024 * 1024)

    attn_rows = attn.reshape(row_count, width)
    far_rows = swap_chip(attn_rows)
    near_rows = swap_core(attn_rows)


    chunks = 8
    held = [
        pltpu.VMEM((chunks, out_proj.shape[0] // chunks, out_proj.shape[1]), BF16),
        pltpu.SemaphoreType.DMA((chunks,)),
    ]
    hbm = pl.BlockSpec(memory_space=pltpu.HBM)
    columns = pl.pallas_call(
        forward_kernel,
        out_shape=[jax.ShapeDtypeStruct((row_count, out_proj.shape[1]), BF16)] * 4,
        in_specs=[vmem] * 4 + [hbm],
        out_specs=[vmem] * 4,
        scratch_shapes=[held[0], pltpu.VMEM((4 * row_count, out_proj.shape[1]), F32), held[1]],
        compiler_params=stream,
    )(attn_rows, near_rows, far_rows, swap_core(far_rows), out_proj)
    parts = [
        columns[0],
        swap_core(columns[1]),
        swap_chip(columns[2]),
        lax.ppermute(columns[3], GRP, DIAGONAL),
    ]

    def by_group(items):
        items = [jnp.where(core == 1, items[i ^ 1], items[i]) for i in range(4)]
        return [jnp.where(chip == 1, items[i ^ 2], items[i]) for i in range(4)]

    half = LANES // 2
    fill = ((0, 1), (0, half - tok_rows))
    requests = jnp.concatenate(
        [jnp.pad(neg_owner.T, fill), jnp.pad(neg_row.T, fill)], axis=1
    ).astype(BF16)
    task_onehot = (jnp.arange(task_bias.shape[0]) == task_ids[0]).astype(F32)
    bias_row = jnp.sum(task_onehot[:, None] * task_bias, axis=0, keepdims=True)
    place = me.astype(jnp.int32).reshape(1)
    rows_f32 = jax.ShapeDtypeStruct((row_count, LANES), F32)
    own_spread, pooled, inv_rms, inv_norm = pl.pallas_call(
        embed_kernel,
        out_shape=(
            jax.ShapeDtypeStruct((blocks, row_count + 8, LANES), BF16),
            jax.ShapeDtypeStruct((row_count, width), F32),
            rows_f32,
            rows_f32,
        ),
        in_specs=[smem] + [vmem] * 9,
        out_specs=(vmem,) * 4,
        scratch_shapes=[pltpu.VMEM((4, row_count, width // 4), BF16)],
        compiler_params=params,
    )(
        place,
        *parts,
        resid.reshape(row_count, width),
        out_bias[None],
        gain[None],
        bias_row,
        requests,
    )
    spread = exchange(own_spread, BLK)
    q_all = spread[:, :tok_rows].reshape(pairs, LANES)
    p_own = spread[:, tok_rows:row_count].reshape(pairs, LANES)
    requests = spread[:, row_count : row_count + hard_count].astype(jnp.int32)
    owner = requests[:, :, :tok_rows]
    ids = ((owner // blocks) ^ me) * pairs + (owner % blocks) * tok_rows
    ids = (ids + requests[:, :, half : half + tok_rows]).reshape(-1)
    p_far = swap_chip(p_own)
    p_all = jnp.concatenate([p_own, swap_core(p_own), p_far, swap_core(p_far)])

    score_part = lax.dot_general(
        q_all, p_own, (((1,), (1,)), ((), ())), preferred_element_type=F32
    )
    negatives, hard_part = pl.pallas_call(
        lambda *refs: gather_kernel(hard_count, tok_rows, *refs),
        out_shape=(
            jax.ShapeDtypeStruct((hard_count, pairs, LANES), BF16),
            jax.ShapeDtypeStruct((pairs, LANES), F32),
        ),
        in_specs=[smem, vmem, vmem],
        out_specs=(vmem, vmem),
        scratch_shapes=[
            pltpu.VMEM((4 * pairs, LANES), F32),
            pltpu.VMEM((hard_count, pairs, LANES), F32),
        ],
        compiler_params=params,
    )(ids, q_all, p_all)
    part = jnp.concatenate([score_part, hard_part], axis=1).astype(SEND)
    part = exchange(part.reshape(blocks, tok_rows, pairs + LANES), BLK)
    part = jnp.sum(part.astype(F32), axis=0) / TAU
    scores = part[:, :pairs]
    hard = part[:, pairs:]

    column = lax.broadcasted_iota(jnp.int32, scores.shape, 1)
    row = lax.broadcasted_iota(jnp.int32, scores.shape, 0)
    weights = jnp.exp(scores)
    slot = lax.broadcasted_iota(jnp.int32, hard.shape, 1)
    hard_weights = jnp.where(slot < hard_count, jnp.exp(hard), 0.0)
    totals = jnp.sum(weights, axis=1, keepdims=True) + jnp.sum(hard_weights, axis=1, keepdims=True)
    own_column = lax.axis_index(BLK) * tok_rows + row
    own_score = jnp.sum(jnp.where(column == own_column, scores, 0.0), axis=1)
    losses = jnp.log(totals[:, 0]) - own_score

    def spread_rows(values):
        values = values.astype(BF16)
        values = exchange(jnp.broadcast_to(values[None], (blocks,) + values.shape), BLK)
        return values.reshape((pairs,) + values.shape[2:])

    hard_probs = spread_rows(hard_weights / totals)
    group_probs = spread_rows(weights / totals)

    hard_add, hard_sum = pl.pallas_call(
        lambda *refs: scatter_kernel(hard_count, tok_rows, *refs),
        out_shape=(
            jax.ShapeDtypeStruct((4 * pairs, LANES), BF16),
            jax.ShapeDtypeStruct((pairs, LANES), F32),
        ),
        in_specs=[smem, vmem, vmem, vmem],
        out_specs=(vmem, vmem),
        scratch_shapes=[pltpu.VMEM((hard_count, pairs, LANES), F32)]
        + [pltpu.VMEM((4 * pairs, LANES), F32)] * hard_count,
        compiler_params=params,
    )(ids, hard_probs, q_all, negatives)
    hard_add = hard_add.reshape(4, pairs, LANES)
    crossed = swap_core(jnp.stack([hard_add[1], hard_add[3]])).astype(F32)
    over_chip = swap_chip((hard_add[2].astype(F32) + crossed[1]).astype(BF16)).astype(F32)
    sum_q = jnp.dot(group_probs, p_own, preferred_element_type=F32) + hard_sum
    sum_p = lax.dot_general(
        group_probs, q_all, (((0,), (0,)), ((), ())), preferred_element_type=F32
    )
    sum_p = sum_p + (hard_add[0].astype(F32) + crossed[0] + over_chip)
    sums = jnp.stack(
        [sum_q.reshape(blocks, tok_rows, LANES), sum_p.reshape(blocks, tok_rows, LANES)], axis=1
    ).astype(BF16)
    sums = exchange(sums, BLK)

    part_shape = jax.ShapeDtypeStruct((row_count + 8, width // 4), BF16)
    cols = pl.pallas_call(
        pullback_kernel,
        out_shape=[part_shape] * 4,
        in_specs=[smem] * 2 + [vmem] * 7,
        out_specs=[vmem] * 4,
        scratch_shapes=[
            pltpu.VMEM((row_count, width), F32),
            pltpu.VMEM((8, width), F32),
            pltpu.VMEM((4, row_count + 8, width // 4), BF16),
        ],
        compiler_params=params,
    )(place, task_ids, sums, own_spread, pooled, inv_rms, inv_norm, gain[None], bias_row)
    cols = [
        cols[0],
        swap_core(cols[1]),
        swap_chip(cols[2]),
        lax.ppermute(cols[3], GRP, DIAGONAL),
    ]
    extra = jnp.stack([part[row_count:] for part in cols])
    vectors = extra[:, :3].astype(F32) + extra[:, 3:6].astype(F32)
    tasks = extra[:, 6, :1].astype(jnp.int32)
    both = (vectors[0, :2] + vectors[1, :2]) + (vectors[2, :2] + vectors[3, :2])
    vectors = jnp.concatenate([both, vectors[:, 2]]).reshape(-1, LANES)
    keep, send = pl.pallas_call(
        backward_kernel,
        out_shape=[jax.ShapeDtypeStruct((2, row_count, width), BF16)] * 2,
        in_specs=[vmem] * 4 + [hbm],
        out_specs=[vmem] * 2,
        scratch_shapes=held,
        compiler_params=stream,
    )(*cols, out_proj)
    crossed = swap_core(send)
    far_sum = (keep[1].astype(F32) + crossed[1].astype(F32)).astype(BF16)
    far_sum, vectors = lax.optimization_barrier((far_sum, vectors))
    first = swap_chip(far_sum[:, : width // 2])
    vectors, first = lax.optimization_barrier((sum_over(vectors, "z"), first))
    second = swap_chip(far_sum[:, width // 2 :])
    vectors, second = lax.optimization_barrier((sum_over(vectors, "y"), second))
    far_sum = jnp.concatenate([first, second], axis=1).astype(F32)
    grad_attn = keep[0].astype(F32) + crossed[0].astype(F32) + far_sum

    vectors = sum_over(vectors, "xh")
    vectors = vectors.reshape(6, -1)
    onehot = (tasks == jnp.arange(task_bias.shape[0])[None, :]).astype(F32)
    placed = onehot[:, :, None] * vectors[2:, None, :]
    placed = (placed[0] + placed[1]) + (placed[2] + placed[3])
    placed = jnp.concatenate([vectors[:2], placed])
    whole = [
        placed,
        swap_core(placed),
        swap_chip(placed),
        lax.ppermute(placed, GRP, DIAGONAL),
    ]
    whole = jnp.concatenate(by_group(whole), axis=1)
    return (
        losses,
        grad_attn.reshape(2, tok_rows, width),
        whole[0],
        whole[2:],
        whole[1],
    )


def solution(mesh):
    fine = Mesh(mesh.devices.reshape(2, 2, 2, 4, 4), ALL)
    in_specs = (
        P(None, ALL, None),
        P(None, ALL, None),
        P(None, GRP),
        P(),
        P(),
        P(),
        P(GRP),
        P(ALL, None),
        P(ALL, None),
    )
    out_specs = (P(ALL), P(None, ALL, None), P(), P(), P())
    return jax.shard_map(local, mesh=fine, in_specs=in_specs, out_specs=out_specs, check_vma=False)
```

```python
import jax
import jax.numpy as jnp
from jax import lax
from jax.experimental import pallas as pl
from jax.experimental.pallas import tpu as pltpu
from jax.sharding import Mesh, PartitionSpec as P

TAU = 0.02
LOSS_SCALE = 256.0
GRP = ("xl", "co")
BLK = ("xh", "y", "z")
ALL = GRP + BLK
SWAP = [(0, 1), (1, 0)]
DIAGONAL = [(0, 3), (1, 2), (2, 1), (3, 0)]
LANES = 128
F32 = jnp.float32
BF16 = jnp.bfloat16
SEND = jnp.float16


def swap_core(values):
    return lax.ppermute(values, "co", SWAP)


def swap_chip(values):
    return lax.ppermute(values, "xl", SWAP)


def from_ahead(values, axis, step):
    size = lax.axis_size(axis)
    return lax.ppermute(values, axis, [((i + step) % size, i) for i in range(size)])


def sum_over(values, axis):
    if lax.axis_size(axis) == 2:
        return values + from_ahead(values, axis, 1)
    one, two, three = [from_ahead(values, axis, step) for step in (1, 2, 3)]
    return (values + two) + (one + three)


def exchange(values, axes):
    return lax.all_to_all(values, axes, split_axis=0, concat_axis=0, tiled=True)


def embed_kernel(
    me, x0, x1, x2, x3, resid, out_bias, gain, bias_row, requests,
    spread, pooled, inv_rms, inv_norm, held,
):
    rows, width = resid.shape
    quarter = width // 4
    for i, x_ref in enumerate((x0, x1, x2, x3)):
        held[i] = x_ref[...]
    squares = jnp.zeros((rows, LANES), F32)
    for b in range(width // LANES):
        here = slice(b * LANES, (b + 1) * LANES)
        start = b * LANES % quarter
        projected = held[me[0] ^ (b * LANES // quarter), :, start : start + LANES]
        value = resid[:, here].astype(F32) + projected.astype(F32) + out_bias[:, here]
        pooled[:, here] = value
        squares = squares + value * value
    mean = jnp.sum(squares, axis=1, keepdims=True) / width
    rms = jnp.broadcast_to(lax.rsqrt(mean + 1e-05), (rows, LANES))
    inv_rms[...] = rms

    def mixture(b):
        here = slice(b * LANES, (b + 1) * LANES)
        return pooled[:, here] * rms * gain[:, here] + bias_row[:, here]

    squares = jnp.zeros((rows, LANES), F32)
    for b in range(width // LANES):
        value = mixture(b)
        squares = squares + value * value
    total = jnp.sum(squares, axis=1, keepdims=True)
    norm = jnp.broadcast_to(lax.rsqrt(total + 1e-06), (rows, LANES))
    inv_norm[...] = norm
    wanted = requests[...].astype(F32)
    for b in range(width // LANES):
        spread[b] = jnp.concatenate([mixture(b) * norm, wanted]).astype(BF16)


def pullback_kernel(
    me, task, sums, spread, pooled, inv_rms, inv_norm, gain, bias_row,
    y0, y1, y2, y3, vectors, grad, held,
):
    rows, width = pooled.shape
    half = rows // 2
    quarter = width // 4
    lines = width // LANES
    rms, norm = inv_rms[...], inv_norm[...]

    def across(values):
        return jnp.broadcast_to(jnp.sum(values, axis=1, keepdims=True), values.shape)

    def embedded(b):
        here = slice(b * LANES, (b + 1) * LANES)
        normed = pooled[:, here] * rms
        return normed, (normed * gain[:, here] + bias_row[:, here]) * norm

    along = jnp.zeros((rows, LANES), F32)
    for b in range(width // LANES):
        own = spread[b].astype(F32)
        other = jnp.concatenate([own[half:rows], own[:half]])
        both = jnp.concatenate([sums[b, 0].astype(F32), sums[b, 1].astype(F32)])
        cotangent = (both - other) / TAU
        grad[:, b * LANES : (b + 1) * LANES] = cotangent
        along = along + embedded(b)[1] * cotangent
    along = across(along)
    inner = jnp.zeros((rows, LANES), F32)
    for b in range(width // LANES):
        here = slice(b * LANES, (b + 1) * LANES)
        normed, unit = embedded(b)
        d_mixture = norm * (grad[:, here] - unit * along)
        vectors[b : b + 1, :] = jnp.sum(d_mixture * normed, axis=0, keepdims=True)
        vectors[2 * lines + b : 2 * lines + b + 1, :] = jnp.sum(d_mixture, axis=0, keepdims=True)
        d_normed = d_mixture * gain[:, here]
        grad[:, here] = d_normed
        inner = inner + d_normed * normed
    inner = across(inner) / width
    for b in range(lines):
        here = slice(b * LANES, (b + 1) * LANES)
        d_pooled = rms * (grad[:, here] - pooled[:, here] * rms * inner)
        vectors[lines + b : lines + b + 1, :] = jnp.sum(d_pooled, axis=0, keepdims=True)
        start = b * LANES % quarter
        held[b * LANES // quarter, :, start : start + LANES] = (LOSS_SCALE * d_pooled).astype(BF16)
    vectors[3 * lines :, :] = jnp.full((8, LANES), task[0].astype(F32))
    for i, y_ref in enumerate((y0, y1, y2, y3)):
        y_ref[...] = held[me[0] ^ i]


def gather_kernel(hard_count, tok_rows, ids, q_ref, p_ref, neg_ref, hard_ref, wide, picked):
    rows = q_ref.shape[0]
    wide[...] = p_ref[...].astype(F32)

    def pick(block, carry):
        for i in range(tok_rows):
            for k in range(hard_count):
                source = ids[(block * hard_count + k) * tok_rows + i]
                picked[k, pl.ds(block * tok_rows + i, 1), :] = wide[pl.ds(source, 1), :]
        return carry

    lax.fori_loop(0, rows // tok_rows, pick, 0)
    q = q_ref[...].astype(F32)
    lane = lax.broadcasted_iota(jnp.int32, (rows, LANES), 1)
    hard = jnp.zeros((rows, LANES), F32)
    for k in range(hard_count):
        chosen = picked[k]
        neg_ref[k] = chosen.astype(BF16)
        hard = jnp.where(lane == k, jnp.sum(q * chosen, axis=1, keepdims=True), hard)
    hard_ref[...] = hard


def scatter_kernel(hard_count, tok_rows, ids, w_ref, q_ref, neg_ref, add_ref, sum_ref, slot, *parts):
    rows = q_ref.shape[0]
    for part in parts:
        part[...] = jnp.zeros_like(part)
    q = q_ref[...].astype(F32)
    total = jnp.zeros((rows, LANES), F32)
    for k in range(hard_count):
        weight = w_ref[:, k : k + 1].astype(F32)
        slot[k] = weight * q
        total = total + weight * neg_ref[k].astype(F32)
    sum_ref[...] = total

    def place(block, carry):
        for i in range(tok_rows):
            for k in range(hard_count):
                target = pl.ds(ids[(block * hard_count + k) * tok_rows + i], 1)
                parts[k][target, :] += slot[k, pl.ds(block * tok_rows + i, 1), :]
        return carry

    lax.fori_loop(0, rows // tok_rows, place, 0)
    added = parts[0][...]
    for k in range(1, hard_count):
        added = added + parts[k][...]
    add_ref[...] = added.astype(BF16)


def stream_chunks(w_ref, held, sems):
    chunks, depth = held.shape[0], held.shape[1]
    copies = [
        pltpu.make_async_copy(w_ref.at[pl.ds(c * depth, depth), :], held.at[c], sems.at[c])
        for c in range(chunks)
    ]
    for copy in copies:
        copy.start()
    return copies


def forward_kernel(x0, x1, x2, x3, w_ref, y0, y1, y2, y3, held, total, sems):
    depth = held.shape[1]
    rows = y0.shape[0]
    for c, copy in enumerate(stream_chunks(w_ref, held, sems)):
        copy.wait()
        here = slice(c * depth, (c + 1) * depth)
        x = jnp.concatenate([x_ref[:, here] for x_ref in (x0, x1, x2, x3)])
        term = jnp.dot(x, held[c], preferred_element_type=F32)
        total[...] = term if c == 0 else total[...] + term
    for i, y_ref in enumerate((y0, y1, y2, y3)):
        y_ref[...] = total[i * rows : (i + 1) * rows, :].astype(BF16)


def backward_kernel(x0, x1, x2, x3, w_ref, keep_ref, send_ref, held, sems):
    depth = held.shape[1]
    rows = keep_ref.shape[1]
    copies = stream_chunks(w_ref, held, sems)
    x = jnp.concatenate([x_ref[...] for x_ref in (x0, x1, x2, x3)])
    for c, copy in enumerate(copies):
        copy.wait()
        term = lax.dot_general(x, held[c], (((1,), (1,)), ((), ())), preferred_element_type=F32)
        here = slice(c * depth, (c + 1) * depth)
        for i in range(4):
            out_ref = send_ref if i % 2 else keep_ref
            out_ref[i // 2, :, here] = term[i * rows : (i + 1) * rows].astype(BF16)


def finish_kernel(blocks, v0, v1, v2, v3, gain_ref, bias_ref, task_ref):
    lines = gain_ref.shape[0]
    four = (v0, v1, v2, v3)

    def total(start):
        parts = [v[start : start + lines, :] for v in four]
        return (parts[0] + parts[1]) + (parts[2] + parts[3])

    gain_ref[...] = total(0)
    bias_ref[...] = total(lines)
    row = lax.broadcasted_iota(jnp.int32, (8, LANES), 0).astype(F32)
    chosen = [
        jnp.where(jnp.abs(v[3 * lines :, :] / blocks - row) < 0.5, 1.0, 0.0) for v in four
    ]
    for b in range(lines):
        here = slice(2 * lines + b, 2 * lines + b + 1)
        parts = [mask * v[here, :] for mask, v in zip(chosen, four)]
        task_ref[:, b * LANES : (b + 1) * LANES] = (parts[0] + parts[1]) + (parts[2] + parts[3])


def local(resid, attn, out_proj, out_bias, gain, task_bias, task_ids, neg_owner, neg_row):
    tok_rows = resid.shape[1]
    width = resid.shape[2]
    hard_count = neg_owner.shape[1]
    row_count = 2 * tok_rows
    blocks = lax.axis_size(BLK)
    pairs = blocks * tok_rows
    me = lax.axis_index(GRP)
    vmem = pl.BlockSpec(memory_space=pltpu.VMEM)
    smem = pl.BlockSpec(memory_space=pltpu.SMEM)
    params = pltpu.CompilerParams(vmem_limit_bytes=24 * 1024 * 1024)

    stream = pltpu.CompilerParams(vmem_limit_bytes=52 * 1024 * 1024)

    attn_rows = attn.reshape(row_count, width)
    far_rows = swap_chip(attn_rows)
    near_rows = swap_core(attn_rows)


    chunks = 8
    held = [
        pltpu.VMEM((chunks, out_proj.shape[0] // chunks, out_proj.shape[1]), BF16),
        pltpu.SemaphoreType.DMA((chunks,)),
    ]
    hbm = pl.BlockSpec(memory_space=pltpu.HBM)
    columns = pl.pallas_call(
        forward_kernel,
        out_shape=[jax.ShapeDtypeStruct((row_count, out_proj.shape[1]), BF16)] * 4,
        in_specs=[vmem] * 4 + [hbm],
        out_specs=[vmem] * 4,
        scratch_shapes=[held[0], pltpu.VMEM((4 * row_count, out_proj.shape[1]), F32), held[1]],
        compiler_params=stream,
    )(attn_rows, near_rows, far_rows, swap_core(far_rows), out_proj)
    parts = [
        columns[0],
        swap_core(columns[1]),
        swap_chip(columns[2]),
        lax.ppermute(columns[3], GRP, DIAGONAL),
    ]

    half = LANES // 2
    fill = ((0, 1), (0, half - tok_rows))
    requests = jnp.concatenate(
        [jnp.pad(neg_owner.T, fill), jnp.pad(neg_row.T, fill)], axis=1
    ).astype(BF16)
    task_onehot = (jnp.arange(task_bias.shape[0]) == task_ids[0]).astype(F32)
    bias_row = jnp.sum(task_onehot[:, None] * task_bias, axis=0, keepdims=True)
    place = me.astype(jnp.int32).reshape(1)
    rows_f32 = jax.ShapeDtypeStruct((row_count, LANES), F32)
    own_spread, pooled, inv_rms, inv_norm = pl.pallas_call(
        embed_kernel,
        out_shape=(
            jax.ShapeDtypeStruct((blocks, row_count + 8, LANES), BF16),
            jax.ShapeDtypeStruct((row_count, width), F32),
            rows_f32,
            rows_f32,
        ),
        in_specs=[smem] + [vmem] * 9,
        out_specs=(vmem,) * 4,
        scratch_shapes=[pltpu.VMEM((4, row_count, width // 4), BF16)],
        compiler_params=params,
    )(
        place,
        *parts,
        resid.reshape(row_count, width),
        out_bias[None],
        gain[None],
        bias_row,
        requests,
    )
    spread = exchange(own_spread, BLK)
    q_all = spread[:, :tok_rows].reshape(pairs, LANES)
    p_own = spread[:, tok_rows:row_count].reshape(pairs, LANES)
    requests = spread[:, row_count : row_count + hard_count].astype(jnp.int32)
    owner = requests[:, :, :tok_rows]
    ids = ((owner // blocks) ^ me) * pairs + (owner % blocks) * tok_rows
    ids = (ids + requests[:, :, half : half + tok_rows]).reshape(-1)
    p_far = swap_chip(p_own)
    p_all = jnp.concatenate([p_own, swap_core(p_own), p_far, swap_core(p_far)])

    score_part = lax.dot_general(
        q_all, p_own, (((1,), (1,)), ((), ())), preferred_element_type=F32
    )
    negatives, hard_part = pl.pallas_call(
        lambda *refs: gather_kernel(hard_count, tok_rows, *refs),
        out_shape=(
            jax.ShapeDtypeStruct((hard_count, pairs, LANES), BF16),
            jax.ShapeDtypeStruct((pairs, LANES), F32),
        ),
        in_specs=[smem, vmem, vmem],
        out_specs=(vmem, vmem),
        scratch_shapes=[
            pltpu.VMEM((4 * pairs, LANES), F32),
            pltpu.VMEM((hard_count, pairs, LANES), F32),
        ],
        compiler_params=params,
    )(ids, q_all, p_all)
    part = jnp.concatenate([score_part, hard_part], axis=1).astype(SEND)
    part = exchange(part.reshape(blocks, tok_rows, pairs + LANES), BLK)
    part = jnp.sum(part.astype(F32), axis=0) / TAU
    scores = part[:, :pairs]
    hard = part[:, pairs:]

    column = lax.broadcasted_iota(jnp.int32, scores.shape, 1)
    row = lax.broadcasted_iota(jnp.int32, scores.shape, 0)
    weights = jnp.exp(scores)
    slot = lax.broadcasted_iota(jnp.int32, hard.shape, 1)
    hard_weights = jnp.where(slot < hard_count, jnp.exp(hard), 0.0)
    totals = jnp.sum(weights, axis=1, keepdims=True) + jnp.sum(hard_weights, axis=1, keepdims=True)
    own_column = lax.axis_index(BLK) * tok_rows + row
    own_score = jnp.sum(jnp.where(column == own_column, scores, 0.0), axis=1)
    losses = jnp.log(totals[:, 0]) - own_score

    def spread_rows(values):
        values = values.astype(BF16)
        values = exchange(jnp.broadcast_to(values[None], (blocks,) + values.shape), BLK)
        return values.reshape((pairs,) + values.shape[2:])

    hard_probs = spread_rows(hard_weights / totals)
    group_probs = spread_rows(weights / totals)

    hard_add, hard_sum = pl.pallas_call(
        lambda *refs: scatter_kernel(hard_count, tok_rows, *refs),
        out_shape=(
            jax.ShapeDtypeStruct((4 * pairs, LANES), BF16),
            jax.ShapeDtypeStruct((pairs, LANES), F32),
        ),
        in_specs=[smem, vmem, vmem, vmem],
        out_specs=(vmem, vmem),
        scratch_shapes=[pltpu.VMEM((hard_count, pairs, LANES), F32)]
        + [pltpu.VMEM((4 * pairs, LANES), F32)] * hard_count,
        compiler_params=params,
    )(ids, hard_probs, q_all, negatives)
    hard_add = hard_add.reshape(4, pairs, LANES)
    crossed = swap_core(jnp.stack([hard_add[1], hard_add[3]])).astype(F32)
    over_chip = swap_chip((hard_add[2].astype(F32) + crossed[1]).astype(BF16)).astype(F32)
    sum_q = jnp.dot(group_probs, p_own, preferred_element_type=F32) + hard_sum
    sum_p = lax.dot_general(
        group_probs, q_all, (((0,), (0,)), ((), ())), preferred_element_type=F32
    )
    sum_p = sum_p + (hard_add[0].astype(F32) + crossed[0] + over_chip)
    sums = jnp.stack(
        [sum_q.reshape(blocks, tok_rows, LANES), sum_p.reshape(blocks, tok_rows, LANES)], axis=1
    ).astype(BF16)
    sums = exchange(sums, BLK)

    lines = width // LANES
    *cols, vectors = pl.pallas_call(
        pullback_kernel,
        out_shape=[jax.ShapeDtypeStruct((row_count, width // 4), BF16)] * 4
        + [jax.ShapeDtypeStruct((3 * lines + 8, LANES), F32)],
        in_specs=[smem] * 2 + [vmem] * 7,
        out_specs=[vmem] * 5,
        scratch_shapes=[
            pltpu.VMEM((row_count, width), F32),
            pltpu.VMEM((4, row_count, width // 4), BF16),
        ],
        compiler_params=params,
    )(place, task_ids, sums, own_spread, pooled, inv_rms, inv_norm, gain[None], bias_row)
    cols = [
        cols[0],
        swap_core(cols[1]),
        swap_chip(cols[2]),
        lax.ppermute(cols[3], GRP, DIAGONAL),
    ]
    vectors, *cols = lax.optimization_barrier((sum_over(vectors, "z"), *cols))
    keep, send = pl.pallas_call(
        backward_kernel,
        out_shape=[jax.ShapeDtypeStruct((2, row_count, width), BF16)] * 2,
        in_specs=[vmem] * 4 + [hbm],
        out_specs=[vmem] * 2,
        scratch_shapes=held,
        compiler_params=stream,
    )(*cols, out_proj)
    vectors, keep, send = lax.optimization_barrier((vectors, keep, send))
    vectors = sum_over(sum_over(vectors, "y"), "xh")
    crossed = swap_core(send)
    far_sum = (keep[1].astype(F32) + crossed[1].astype(F32)).astype(BF16)
    first = swap_chip(far_sum[:, : width // 2])
    second = swap_chip(far_sum[:, width // 2 :])
    vectors, first = lax.optimization_barrier((vectors, first))
    far_sum = jnp.concatenate([first, second], axis=1).astype(F32)
    grad_attn = keep[0].astype(F32) + crossed[0].astype(F32) + far_sum

    four = [
        vectors,
        swap_core(vectors),
        swap_chip(vectors),
        lax.ppermute(vectors, GRP, DIAGONAL),
    ]
    grad_gain, grad_out_bias, grad_task_bias = pl.pallas_call(
        lambda *refs: finish_kernel(blocks, *refs),
        out_shape=[jax.ShapeDtypeStruct((lines, LANES), F32)] * 2
        + [jax.ShapeDtypeStruct(task_bias.shape, F32)],
        in_specs=[vmem] * 4,
        out_specs=[vmem] * 3,
        compiler_params=params,
    )(*four)
    return (
        losses,
        grad_attn.reshape(2, tok_rows, width),
        grad_gain.reshape(width),
        grad_task_bias,
        grad_out_bias.reshape(width),
    )


def solution(mesh):
    fine = Mesh(mesh.devices.reshape(2, 2, 2, 4, 4), ALL)
    in_specs = (
        P(None, ALL, None),
        P(None, ALL, None),
        P(None, GRP),
        P(),
        P(),
        P(),
        P(GRP),
        P(ALL, None),
        P(ALL, None),
    )
    out_specs = (P(ALL), P(None, ALL, None), P(), P(), P())
    return jax.shard_map(local, mesh=fine, in_specs=in_specs, out_specs=out_specs, check_vma=False)
```

```python
import jax
import jax.numpy as jnp
from jax import lax
from jax.experimental import pallas as pl
from jax.experimental.pallas import tpu as pltpu
from jax.sharding import Mesh, PartitionSpec as P

TAU = 0.02
LOSS_SCALE = 256.0
GRP = ("xl", "co")
BLK = ("xh", "y", "z")
ALL = GRP + BLK
SWAP = [(0, 1), (1, 0)]
DIAGONAL = [(0, 3), (1, 2), (2, 1), (3, 0)]
LANES = 128
F32 = jnp.float32
BF16 = jnp.bfloat16
SEND = jnp.float16


def swap_core(values):
    return lax.ppermute(values, "co", SWAP)


def swap_chip(values):
    return lax.ppermute(values, "xl", SWAP)


def from_ahead(values, axis, step):
    size = lax.axis_size(axis)
    return lax.ppermute(values, axis, [((i + step) % size, i) for i in range(size)])


def sum_over(values, axis):
    if lax.axis_size(axis) == 2:
        return values + from_ahead(values, axis, 1)
    one, two, three = [from_ahead(values, axis, step) for step in (1, 2, 3)]
    return (values + two) + (one + three)


def exchange(values, axes):
    return lax.all_to_all(values, axes, split_axis=0, concat_axis=0, tiled=True)


def embed_kernel(
    me, x0, x1, x2, x3, resid, out_bias, gain, bias_row, requests,
    spread, pooled, inv_rms, inv_norm, held,
):
    rows, width = resid.shape
    quarter = width // 4
    for i, x_ref in enumerate((x0, x1, x2, x3)):
        held[i] = x_ref[...]
    squares = jnp.zeros((rows, LANES), F32)
    for b in range(width // LANES):
        here = slice(b * LANES, (b + 1) * LANES)
        start = b * LANES % quarter
        projected = held[me[0] ^ (b * LANES // quarter), :, start : start + LANES]
        value = resid[:, here].astype(F32) + projected.astype(F32) + out_bias[:, here]
        pooled[:, here] = value
        squares = squares + value * value
    mean = jnp.sum(squares, axis=1, keepdims=True) / width
    rms = jnp.broadcast_to(lax.rsqrt(mean + 1e-05), (rows, LANES))
    inv_rms[...] = rms

    def mixture(b):
        here = slice(b * LANES, (b + 1) * LANES)
        return pooled[:, here] * rms * gain[:, here] + bias_row[:, here]

    squares = jnp.zeros((rows, LANES), F32)
    for b in range(width // LANES):
        value = mixture(b)
        squares = squares + value * value
    total = jnp.sum(squares, axis=1, keepdims=True)
    norm = jnp.broadcast_to(lax.rsqrt(total + 1e-06), (rows, LANES))
    inv_norm[...] = norm
    wanted = requests[...].astype(F32)
    for b in range(width // LANES):
        spread[b] = jnp.concatenate([mixture(b) * norm, wanted]).astype(BF16)


def pullback_kernel(
    me, task, sums, spread, pooled, inv_rms, inv_norm, gain, bias_row,
    y0, y1, y2, y3, vectors, grad, held,
):
    rows, width = pooled.shape
    half = rows // 2
    quarter = width // 4
    lines = width // LANES
    rms, norm = inv_rms[...], inv_norm[...]

    def across(values):
        return jnp.broadcast_to(jnp.sum(values, axis=1, keepdims=True), values.shape)

    def embedded(b):
        here = slice(b * LANES, (b + 1) * LANES)
        normed = pooled[:, here] * rms
        return normed, (normed * gain[:, here] + bias_row[:, here]) * norm

    along = jnp.zeros((rows, LANES), F32)
    for b in range(width // LANES):
        own = spread[b].astype(F32)
        other = jnp.concatenate([own[half:rows], own[:half]])
        both = jnp.concatenate([sums[b, 0].astype(F32), sums[b, 1].astype(F32)])
        cotangent = (both - other) / TAU
        grad[:, b * LANES : (b + 1) * LANES] = cotangent
        along = along + embedded(b)[1] * cotangent
    along = across(along)
    inner = jnp.zeros((rows, LANES), F32)
    for b in range(width // LANES):
        here = slice(b * LANES, (b + 1) * LANES)
        normed, unit = embedded(b)
        d_mixture = norm * (grad[:, here] - unit * along)
        vectors[b : b + 1, :] = jnp.sum(d_mixture * normed, axis=0, keepdims=True)
        vectors[2 * lines + b : 2 * lines + b + 1, :] = jnp.sum(d_mixture, axis=0, keepdims=True)
        d_normed = d_mixture * gain[:, here]
        grad[:, here] = d_normed
        inner = inner + d_normed * normed
    inner = across(inner) / width
    for b in range(lines):
        here = slice(b * LANES, (b + 1) * LANES)
        d_pooled = rms * (grad[:, here] - pooled[:, here] * rms * inner)
        vectors[lines + b : lines + b + 1, :] = jnp.sum(d_pooled, axis=0, keepdims=True)
        start = b * LANES % quarter
        held[b * LANES // quarter, :, start : start + LANES] = (LOSS_SCALE * d_pooled).astype(BF16)
    vectors[3 * lines :, :] = jnp.full((8, LANES), task[0].astype(F32))
    for i, y_ref in enumerate((y0, y1, y2, y3)):
        y_ref[...] = held[me[0] ^ i]


def gather_kernel(hard_count, tok_rows, ids, q_ref, p_ref, neg_ref, hard_ref, wide, picked):
    rows = q_ref.shape[0]
    wide[...] = p_ref[...].astype(F32)

    def pick(block, carry):
        for i in range(tok_rows):
            for k in range(hard_count):
                source = ids[(block * hard_count + k) * tok_rows + i]
                picked[k, pl.ds(block * tok_rows + i, 1), :] = wide[pl.ds(source, 1), :]
        return carry

    lax.fori_loop(0, rows // tok_rows, pick, 0)
    q = q_ref[...].astype(F32)
    lane = lax.broadcasted_iota(jnp.int32, (rows, LANES), 1)
    hard = jnp.zeros((rows, LANES), F32)
    for k in range(hard_count):
        chosen = picked[k]
        neg_ref[k] = chosen.astype(BF16)
        hard = jnp.where(lane == k, jnp.sum(q * chosen, axis=1, keepdims=True), hard)
    hard_ref[...] = hard


def scatter_kernel(hard_count, tok_rows, ids, w_ref, q_ref, neg_ref, add_ref, sum_ref, slot, *parts):
    rows = q_ref.shape[0]
    for part in parts:
        part[...] = jnp.zeros_like(part)
    q = q_ref[...].astype(F32)
    total = jnp.zeros((rows, LANES), F32)
    for k in range(hard_count):
        weight = w_ref[:, k : k + 1].astype(F32)
        slot[k] = weight * q
        total = total + weight * neg_ref[k].astype(F32)
    sum_ref[...] = total

    def place(block, carry):
        for i in range(tok_rows):
            for k in range(hard_count):
                target = pl.ds(ids[(block * hard_count + k) * tok_rows + i], 1)
                parts[k][target, :] += slot[k, pl.ds(block * tok_rows + i, 1), :]
        return carry

    lax.fori_loop(0, rows // tok_rows, place, 0)
    added = parts[0][...]
    for k in range(1, hard_count):
        added = added + parts[k][...]
    add_ref[...] = added.astype(BF16)


def stream_chunks(w_ref, held, sems):
    chunks, depth = held.shape[0], held.shape[1]
    copies = [
        pltpu.make_async_copy(w_ref.at[pl.ds(c * depth, depth), :], held.at[c], sems.at[c])
        for c in range(chunks)
    ]
    for copy in copies:
        copy.start()
    return copies


def forward_kernel(x0, x1, x2, x3, w_ref, y0, y1, y2, y3, held, total, sems):
    depth = held.shape[1]
    rows = y0.shape[0]
    for c, copy in enumerate(stream_chunks(w_ref, held, sems)):
        copy.wait()
        here = slice(c * depth, (c + 1) * depth)
        x = jnp.concatenate([x_ref[:, here] for x_ref in (x0, x1, x2, x3)])
        term = jnp.dot(x, held[c], preferred_element_type=F32)
        total[...] = term if c == 0 else total[...] + term
    for i, y_ref in enumerate((y0, y1, y2, y3)):
        y_ref[...] = total[i * rows : (i + 1) * rows, :].astype(BF16)


def backward_kernel(x0, x1, x2, x3, w_ref, keep_ref, send_ref, held, sems):
    depth = held.shape[1]
    rows = keep_ref.shape[1]
    copies = stream_chunks(w_ref, held, sems)
    x = jnp.concatenate([x_ref[...] for x_ref in (x0, x1, x2, x3)])
    for c, copy in enumerate(copies):
        copy.wait()
        term = lax.dot_general(x, held[c], (((1,), (1,)), ((), ())), preferred_element_type=F32)
        here = slice(c * depth, (c + 1) * depth)
        for i in range(4):
            out_ref = send_ref if i % 2 else keep_ref
            out_ref[i // 2, :, here] = term[i * rows : (i + 1) * rows].astype(BF16)


def softmax_kernel(hard_count, at, score_ref, losses_ref, hard_ref, group_ref):
    rows, width = score_ref.shape
    pairs = width - LANES
    scores = score_ref[:, :pairs] / TAU
    weights = jnp.exp(scores)
    slot = lax.broadcasted_iota(jnp.int32, (rows, LANES), 1)
    hard_weights = jnp.where(slot < hard_count, jnp.exp(score_ref[:, pairs:] / TAU), 0.0)
    totals = jnp.sum(weights, axis=1, keepdims=True) + jnp.sum(hard_weights, axis=1, keepdims=True)
    column = lax.broadcasted_iota(jnp.int32, (rows, pairs), 1)
    row = lax.broadcasted_iota(jnp.int32, (rows, pairs), 0)
    own = jnp.sum(jnp.where(column == row + at[0], scores, 0.0), axis=1, keepdims=True)
    losses_ref[...] = jnp.broadcast_to(jnp.log(totals) - own, (rows, LANES))
    hard_probs = (hard_weights / totals).astype(BF16)
    probs = (weights / totals).astype(BF16)
    for b in range(hard_ref.shape[0]):
        hard_ref[b] = hard_probs
        group_ref[b] = probs


def sums_kernel(probs_ref, q_ref, p_ref, hard_ref, add_ref, near_ref, far_ref, out_ref):
    tok_rows = out_ref.shape[2]
    probs = probs_ref[...]
    sum_q = jnp.dot(probs, p_ref[...], preferred_element_type=F32) + hard_ref[...]
    sum_p = lax.dot_general(
        probs, q_ref[...], (((0,), (0,)), ((), ())), preferred_element_type=F32
    )
    sum_p = sum_p + add_ref[...].astype(F32) + near_ref[...].astype(F32) + far_ref[...].astype(F32)
    for b in range(out_ref.shape[0]):
        here = slice(b * tok_rows, (b + 1) * tok_rows)
        out_ref[b, 0] = sum_q[here].astype(BF16)
        out_ref[b, 1] = sum_p[here].astype(BF16)


def finish_kernel(blocks, v0, v1, v2, v3, gain_ref, bias_ref, task_ref):
    lines = gain_ref.shape[0]
    four = (v0, v1, v2, v3)

    def total(start):
        parts = [v[start : start + lines, :] for v in four]
        return (parts[0] + parts[1]) + (parts[2] + parts[3])

    gain_ref[...] = total(0)
    bias_ref[...] = total(lines)
    row = lax.broadcasted_iota(jnp.int32, (8, LANES), 0).astype(F32)
    chosen = [
        jnp.where(jnp.abs(v[3 * lines :, :] / blocks - row) < 0.5, 1.0, 0.0) for v in four
    ]
    for b in range(lines):
        here = slice(2 * lines + b, 2 * lines + b + 1)
        parts = [mask * v[here, :] for mask, v in zip(chosen, four)]
        task_ref[:, b * LANES : (b + 1) * LANES] = (parts[0] + parts[1]) + (parts[2] + parts[3])


def local(resid, attn, out_proj, out_bias, gain, task_bias, task_ids, neg_owner, neg_row):
    tok_rows = resid.shape[1]
    width = resid.shape[2]
    hard_count = neg_owner.shape[1]
    row_count = 2 * tok_rows
    blocks = lax.axis_size(BLK)
    pairs = blocks * tok_rows
    me = lax.axis_index(GRP)
    vmem = pl.BlockSpec(memory_space=pltpu.VMEM)
    smem = pl.BlockSpec(memory_space=pltpu.SMEM)
    params = pltpu.CompilerParams(vmem_limit_bytes=24 * 1024 * 1024)

    stream = pltpu.CompilerParams(vmem_limit_bytes=52 * 1024 * 1024)

    attn_rows = attn.reshape(row_count, width)
    far_rows = swap_chip(attn_rows)
    near_rows = swap_core(attn_rows)


    chunks = 8
    held = [
        pltpu.VMEM((chunks, out_proj.shape[0] // chunks, out_proj.shape[1]), BF16),
        pltpu.SemaphoreType.DMA((chunks,)),
    ]
    hbm = pl.BlockSpec(memory_space=pltpu.HBM)
    columns = pl.pallas_call(
        forward_kernel,
        out_shape=[jax.ShapeDtypeStruct((row_count, out_proj.shape[1]), BF16)] * 4,
        in_specs=[vmem] * 4 + [hbm],
        out_specs=[vmem] * 4,
        scratch_shapes=[held[0], pltpu.VMEM((4 * row_count, out_proj.shape[1]), F32), held[1]],
        compiler_params=stream,
    )(attn_rows, near_rows, far_rows, swap_core(far_rows), out_proj)
    parts = [
        columns[0],
        swap_core(columns[1]),
        swap_chip(columns[2]),
        lax.ppermute(columns[3], GRP, DIAGONAL),
    ]

    half = LANES // 2
    fill = ((0, 1), (0, half - tok_rows))
    requests = jnp.concatenate(
        [jnp.pad(neg_owner.T, fill), jnp.pad(neg_row.T, fill)], axis=1
    ).astype(BF16)
    task_onehot = (jnp.arange(task_bias.shape[0]) == task_ids[0]).astype(F32)
    bias_row = jnp.sum(task_onehot[:, None] * task_bias, axis=0, keepdims=True)
    place = me.astype(jnp.int32).reshape(1)
    rows_f32 = jax.ShapeDtypeStruct((row_count, LANES), F32)
    own_spread, pooled, inv_rms, inv_norm = pl.pallas_call(
        embed_kernel,
        out_shape=(
            jax.ShapeDtypeStruct((blocks, row_count + 8, LANES), BF16),
            jax.ShapeDtypeStruct((row_count, width), F32),
            rows_f32,
            rows_f32,
        ),
        in_specs=[smem] + [vmem] * 9,
        out_specs=(vmem,) * 4,
        scratch_shapes=[pltpu.VMEM((4, row_count, width // 4), BF16)],
        compiler_params=params,
    )(
        place,
        *parts,
        resid.reshape(row_count, width),
        out_bias[None],
        gain[None],
        bias_row,
        requests,
    )
    spread = exchange(own_spread, BLK)
    q_all = spread[:, :tok_rows].reshape(pairs, LANES)
    p_own = spread[:, tok_rows:row_count].reshape(pairs, LANES)
    requests = spread[:, row_count : row_count + hard_count].astype(jnp.int32)
    owner = requests[:, :, :tok_rows]
    ids = ((owner // blocks) ^ me) * pairs + (owner % blocks) * tok_rows
    ids = (ids + requests[:, :, half : half + tok_rows]).reshape(-1)
    p_far = swap_chip(p_own)
    p_all = jnp.concatenate([p_own, swap_core(p_own), p_far, swap_core(p_far)])

    score_part = lax.dot_general(
        q_all, p_own, (((1,), (1,)), ((), ())), preferred_element_type=F32
    )
    negatives, hard_part = pl.pallas_call(
        lambda *refs: gather_kernel(hard_count, tok_rows, *refs),
        out_shape=(
            jax.ShapeDtypeStruct((hard_count, pairs, LANES), BF16),
            jax.ShapeDtypeStruct((pairs, LANES), F32),
        ),
        in_specs=[smem, vmem, vmem],
        out_specs=(vmem, vmem),
        scratch_shapes=[
            pltpu.VMEM((4 * pairs, LANES), F32),
            pltpu.VMEM((hard_count, pairs, LANES), F32),
        ],
        compiler_params=params,
    )(ids, q_all, p_all)
    part = jnp.concatenate([score_part, hard_part], axis=1).astype(SEND)
    part = exchange(part.reshape(blocks, tok_rows, pairs + LANES), BLK)
    part = jnp.sum(part.astype(F32), axis=0)
    losses, hard_probs, group_probs = pl.pallas_call(
        lambda *refs: softmax_kernel(hard_count, *refs),
        out_shape=(
            jax.ShapeDtypeStruct((tok_rows, LANES), F32),
            jax.ShapeDtypeStruct((blocks, tok_rows, LANES), BF16),
            jax.ShapeDtypeStruct((blocks, tok_rows, pairs), BF16),
        ),
        in_specs=[smem, vmem],
        out_specs=(vmem,) * 3,
        compiler_params=params,
    )((lax.axis_index(BLK) * tok_rows).astype(jnp.int32).reshape(1), part)
    losses = losses[:, 0]
    hard_probs = exchange(hard_probs, BLK).reshape(pairs, LANES)
    group_probs = exchange(group_probs, BLK).reshape(pairs, pairs)

    hard_add, hard_sum = pl.pallas_call(
        lambda *refs: scatter_kernel(hard_count, tok_rows, *refs),
        out_shape=(
            jax.ShapeDtypeStruct((4 * pairs, LANES), BF16),
            jax.ShapeDtypeStruct((pairs, LANES), F32),
        ),
        in_specs=[smem, vmem, vmem, vmem],
        out_specs=(vmem, vmem),
        scratch_shapes=[pltpu.VMEM((hard_count, pairs, LANES), F32)]
        + [pltpu.VMEM((4 * pairs, LANES), F32)] * hard_count,
        compiler_params=params,
    )(ids, hard_probs, q_all, negatives)
    hard_add = hard_add.reshape(4, pairs, LANES)
    crossed = swap_core(jnp.stack([hard_add[1], hard_add[3]]))
    over_chip = swap_chip((hard_add[2].astype(F32) + crossed[1].astype(F32)).astype(BF16))
    sums = pl.pallas_call(
        sums_kernel,
        out_shape=jax.ShapeDtypeStruct((blocks, 2, tok_rows, LANES), BF16),
        in_specs=[vmem] * 7,
        out_specs=vmem,
        compiler_params=params,
    )(group_probs, q_all, p_own, hard_sum, hard_add[0], crossed[0], over_chip)
    sums = exchange(sums, BLK)

    lines = width // LANES
    *cols, vectors = pl.pallas_call(
        pullback_kernel,
        out_shape=[jax.ShapeDtypeStruct((row_count, width // 4), BF16)] * 4
        + [jax.ShapeDtypeStruct((3 * lines + 8, LANES), F32)],
        in_specs=[smem] * 2 + [vmem] * 7,
        out_specs=[vmem] * 5,
        scratch_shapes=[
            pltpu.VMEM((row_count, width), F32),
            pltpu.VMEM((4, row_count, width // 4), BF16),
        ],
        compiler_params=params,
    )(place, task_ids, sums, own_spread, pooled, inv_rms, inv_norm, gain[None], bias_row)
    cols = [
        cols[0],
        swap_core(cols[1]),
        swap_chip(cols[2]),
        lax.ppermute(cols[3], GRP, DIAGONAL),
    ]
    vectors, *cols = lax.optimization_barrier((sum_over(vectors, "xh"), *cols))
    keep, send = pl.pallas_call(
        backward_kernel,
        out_shape=[jax.ShapeDtypeStruct((2, row_count, width), BF16)] * 2,
        in_specs=[vmem] * 4 + [hbm],
        out_specs=[vmem] * 2,
        scratch_shapes=held,
        compiler_params=stream,
    )(*cols, out_proj)
    vectors, keep, send = lax.optimization_barrier((vectors, keep, send))
    vectors = sum_over(vectors, "y")
    crossed = swap_core(send)
    far_sum = (keep[1].astype(F32) + crossed[1].astype(F32)).astype(BF16)
    far_sum, vectors = lax.optimization_barrier((far_sum, vectors))
    vectors = sum_over(vectors, "z")
    first = swap_chip(far_sum[:, : width // 2])
    second = swap_chip(far_sum[:, width // 2 :])
    vectors, first = lax.optimization_barrier((vectors, first))
    far_sum = jnp.concatenate([first, second], axis=1).astype(F32)
    grad_attn = keep[0].astype(F32) + crossed[0].astype(F32) + far_sum

    four = [
        vectors,
        swap_core(vectors),
        swap_chip(vectors),
        lax.ppermute(vectors, GRP, DIAGONAL),
    ]
    grad_gain, grad_out_bias, grad_task_bias = pl.pallas_call(
        lambda *refs: finish_kernel(blocks, *refs),
        out_shape=[jax.ShapeDtypeStruct((lines, LANES), F32)] * 2
        + [jax.ShapeDtypeStruct(task_bias.shape, F32)],
        in_specs=[vmem] * 4,
        out_specs=[vmem] * 3,
        compiler_params=params,
    )(*four)
    return (
        losses,
        grad_attn.reshape(2, tok_rows, width),
        grad_gain.reshape(width),
        grad_task_bias,
        grad_out_bias.reshape(width),
    )


def solution(mesh):
    fine = Mesh(mesh.devices.reshape(2, 2, 2, 4, 4), ALL)
    in_specs = (
        P(None, ALL, None),
        P(None, ALL, None),
        P(None, GRP),
        P(),
        P(),
        P(),
        P(GRP),
        P(ALL, None),
        P(ALL, None),
    )
    out_specs = (P(ALL), P(None, ALL, None), P(), P(), P())
    return jax.shard_map(local, mesh=fine, in_specs=in_specs, out_specs=out_specs, check_vma=False)
```

```python
import jax
import jax.numpy as jnp
from jax import lax
from jax.experimental import pallas as pl
from jax.experimental.pallas import tpu as pltpu
from jax.sharding import Mesh, PartitionSpec as P

TAU = 0.02
LOSS_SCALE = 256.0
GRP = ("xl", "co")
BLK = ("xh", "y", "z")
ALL = GRP + BLK
SWAP = [(0, 1), (1, 0)]
DIAGONAL = [(0, 3), (1, 2), (2, 1), (3, 0)]
LANES = 128
F32 = jnp.float32
BF16 = jnp.bfloat16
SEND = jnp.float16


def swap_core(values):
    return lax.ppermute(values, "co", SWAP)


def swap_chip(values):
    return lax.ppermute(values, "xl", SWAP)


def from_ahead(values, axis, step):
    size = lax.axis_size(axis)
    return lax.ppermute(values, axis, [((i + step) % size, i) for i in range(size)])


def sum_over(values, axis):
    if lax.axis_size(axis) == 2:
        return values + from_ahead(values, axis, 1)
    one, two, three = [from_ahead(values, axis, step) for step in (1, 2, 3)]
    return (values + two) + (one + three)


def exchange(values, axes):
    return lax.all_to_all(values, axes, split_axis=0, concat_axis=0, tiled=True)


def embed_kernel(
    me, x0, x1, x2, x3, resid, out_bias, gain, bias_row, requests,
    spread, pooled, inv_rms, inv_norm, held,
):
    rows, width = resid.shape
    quarter = width // 4
    for i, x_ref in enumerate((x0, x1, x2, x3)):
        held[i] = x_ref[...]
    squares = jnp.zeros((rows, LANES), F32)
    for b in range(width // LANES):
        here = slice(b * LANES, (b + 1) * LANES)
        start = b * LANES % quarter
        projected = held[me[0] ^ (b * LANES // quarter), :, start : start + LANES]
        value = resid[:, here].astype(F32) + projected.astype(F32) + out_bias[:, here]
        pooled[:, here] = value
        squares = squares + value * value
    mean = jnp.sum(squares, axis=1, keepdims=True) / width
    rms = jnp.broadcast_to(lax.rsqrt(mean + 1e-05), (rows, LANES))
    inv_rms[...] = rms

    def mixture(b):
        here = slice(b * LANES, (b + 1) * LANES)
        return pooled[:, here] * rms * gain[:, here] + bias_row[:, here]

    squares = jnp.zeros((rows, LANES), F32)
    for b in range(width // LANES):
        value = mixture(b)
        squares = squares + value * value
    total = jnp.sum(squares, axis=1, keepdims=True)
    norm = jnp.broadcast_to(lax.rsqrt(total + 1e-06), (rows, LANES))
    inv_norm[...] = norm
    wanted = requests[...].astype(F32)
    for b in range(width // LANES):
        spread[b] = jnp.concatenate([mixture(b) * norm, wanted]).astype(BF16)


def pullback_kernel(
    me, task, sums, spread, pooled, inv_rms, inv_norm, gain, bias_row,
    y0, y1, y2, y3, vectors, grad, held,
):
    rows, width = pooled.shape
    half = rows // 2
    quarter = width // 4
    lines = width // LANES
    rms, norm = inv_rms[...], inv_norm[...]

    def across(values):
        return jnp.broadcast_to(jnp.sum(values, axis=1, keepdims=True), values.shape)

    def embedded(b):
        here = slice(b * LANES, (b + 1) * LANES)
        normed = pooled[:, here] * rms
        return normed, (normed * gain[:, here] + bias_row[:, here]) * norm

    along = jnp.zeros((rows, LANES), F32)
    for b in range(width // LANES):
        own = spread[b].astype(F32)
        other = jnp.concatenate([own[half:rows], own[:half]])
        both = jnp.concatenate([sums[b, 0].astype(F32), sums[b, 1].astype(F32)])
        cotangent = (both - other) / TAU
        grad[:, b * LANES : (b + 1) * LANES] = cotangent
        along = along + embedded(b)[1] * cotangent
    along = across(along)
    inner = jnp.zeros((rows, LANES), F32)
    for b in range(width // LANES):
        here = slice(b * LANES, (b + 1) * LANES)
        normed, unit = embedded(b)
        d_mixture = norm * (grad[:, here] - unit * along)
        vectors[b : b + 1, :] = jnp.sum(d_mixture * normed, axis=0, keepdims=True)
        vectors[2 * lines + b : 2 * lines + b + 1, :] = jnp.sum(d_mixture, axis=0, keepdims=True)
        d_normed = d_mixture * gain[:, here]
        grad[:, here] = d_normed
        inner = inner + d_normed * normed
    inner = across(inner) / width
    for b in range(lines):
        here = slice(b * LANES, (b + 1) * LANES)
        d_pooled = rms * (grad[:, here] - pooled[:, here] * rms * inner)
        vectors[lines + b : lines + b + 1, :] = jnp.sum(d_pooled, axis=0, keepdims=True)
        start = b * LANES % quarter
        held[b * LANES // quarter, :, start : start + LANES] = (LOSS_SCALE * d_pooled).astype(BF16)
    vectors[3 * lines :, :] = jnp.full((8, LANES), task[0].astype(F32))
    for i, y_ref in enumerate((y0, y1, y2, y3)):
        y_ref[...] = held[me[0] ^ i]


def gather_kernel(hard_count, tok_rows, ids, q_ref, p_ref, neg_ref, hard_ref, wide, picked):
    rows = q_ref.shape[0]
    wide[...] = p_ref[...].astype(F32)

    def pick(block, carry):
        for i in range(tok_rows):
            for k in range(hard_count):
                source = ids[(block * hard_count + k) * tok_rows + i]
                picked[k, pl.ds(block * tok_rows + i, 1), :] = wide[pl.ds(source, 1), :]
        return carry

    lax.fori_loop(0, rows // tok_rows, pick, 0)
    q = q_ref[...].astype(F32)
    lane = lax.broadcasted_iota(jnp.int32, (rows, LANES), 1)
    hard = jnp.zeros((rows, LANES), F32)
    for k in range(hard_count):
        chosen = picked[k]
        neg_ref[k] = chosen.astype(BF16)
        hard = jnp.where(lane == k, jnp.sum(q * chosen, axis=1, keepdims=True), hard)
    hard_ref[...] = hard


def scatter_kernel(hard_count, tok_rows, ids, w_ref, q_ref, neg_ref, add_ref, sum_ref, slot, *parts):
    rows = q_ref.shape[0]
    for part in parts:
        part[...] = jnp.zeros_like(part)
    q = q_ref[...].astype(F32)
    total = jnp.zeros((rows, LANES), F32)
    for k in range(hard_count):
        weight = w_ref[:, k : k + 1].astype(F32)
        slot[k] = weight * q
        total = total + weight * neg_ref[k].astype(F32)
    sum_ref[...] = total

    def place(block, carry):
        for i in range(tok_rows):
            for k in range(hard_count):
                target = pl.ds(ids[(block * hard_count + k) * tok_rows + i], 1)
                parts[k][target, :] += slot[k, pl.ds(block * tok_rows + i, 1), :]
        return carry

    lax.fori_loop(0, rows // tok_rows, place, 0)
    added = parts[0][...]
    for k in range(1, hard_count):
        added = added + parts[k][...]
    add_ref[...] = added.astype(BF16)


def stream_chunks(w_ref, held, sems):
    chunks, depth = held.shape[0], held.shape[1]
    copies = [
        pltpu.make_async_copy(w_ref.at[pl.ds(c * depth, depth), :], held.at[c], sems.at[c])
        for c in range(chunks)
    ]
    for copy in copies:
        copy.start()
    return copies


def forward_kernel(x0, x1, x2, x3, w_ref, y0, y1, y2, y3, held, total, sems):
    depth = held.shape[1]
    rows = y0.shape[0]
    for c, copy in enumerate(stream_chunks(w_ref, held, sems)):
        copy.wait()
        here = slice(c * depth, (c + 1) * depth)
        x = jnp.concatenate([x_ref[:, here] for x_ref in (x0, x1, x2, x3)])
        term = jnp.dot(x, held[c], preferred_element_type=F32)
        total[...] = term if c == 0 else total[...] + term
    for i, y_ref in enumerate((y0, y1, y2, y3)):
        y_ref[...] = total[i * rows : (i + 1) * rows, :].astype(BF16)


def backward_kernel(x0, x1, x2, x3, w_ref, keep_ref, send_ref, held, sems):
    depth = held.shape[1]
    rows = keep_ref.shape[1]
    copies = stream_chunks(w_ref, held, sems)
    x = jnp.concatenate([x_ref[...] for x_ref in (x0, x1, x2, x3)])
    for c, copy in enumerate(copies):
        copy.wait()
        term = lax.dot_general(x, held[c], (((1,), (1,)), ((), ())), preferred_element_type=F32)
        here = slice(c * depth, (c + 1) * depth)
        for i in range(4):
            out_ref = send_ref if i % 2 else keep_ref
            out_ref[i // 2, :, here] = term[i * rows : (i + 1) * rows].astype(BF16)


def softmax_kernel(hard_count, at, score_ref, losses_ref, hard_ref, group_ref):
    rows, width = score_ref.shape
    pairs = width - LANES
    scores = score_ref[:, :pairs] / TAU
    weights = jnp.exp(scores)
    slot = lax.broadcasted_iota(jnp.int32, (rows, LANES), 1)
    hard_weights = jnp.where(slot < hard_count, jnp.exp(score_ref[:, pairs:] / TAU), 0.0)
    totals = jnp.sum(weights, axis=1, keepdims=True) + jnp.sum(hard_weights, axis=1, keepdims=True)
    column = lax.broadcasted_iota(jnp.int32, (rows, pairs), 1)
    row = lax.broadcasted_iota(jnp.int32, (rows, pairs), 0)
    own = jnp.sum(jnp.where(column == row + at[0], scores, 0.0), axis=1, keepdims=True)
    losses_ref[...] = jnp.broadcast_to(jnp.log(totals) - own, (rows, LANES))
    hard_probs = (hard_weights / totals).astype(BF16)
    probs = (weights / totals).astype(BF16)
    for b in range(hard_ref.shape[0]):
        hard_ref[b] = hard_probs
        group_ref[b] = probs


def sums_kernel(probs_ref, q_ref, p_ref, hard_ref, add_ref, near_ref, far_ref, out_ref):
    tok_rows = out_ref.shape[2]
    probs = probs_ref[...]
    sum_q = jnp.dot(probs, p_ref[...], preferred_element_type=F32) + hard_ref[...]
    sum_p = lax.dot_general(
        probs, q_ref[...], (((0,), (0,)), ((), ())), preferred_element_type=F32
    )
    sum_p = sum_p + add_ref[...].astype(F32) + near_ref[...].astype(F32) + far_ref[...].astype(F32)
    for b in range(out_ref.shape[0]):
        here = slice(b * tok_rows, (b + 1) * tok_rows)
        out_ref[b, 0] = sum_q[here].astype(BF16)
        out_ref[b, 1] = sum_p[here].astype(BF16)


def finish_kernel(blocks, v0, v1, v2, v3, gain_ref, bias_ref, task_ref):
    lines = gain_ref.shape[0]
    four = (v0, v1, v2, v3)

    def total(start):
        parts = [v[start : start + lines, :] for v in four]
        return (parts[0] + parts[1]) + (parts[2] + parts[3])

    gain_ref[...] = total(0)
    bias_ref[...] = total(lines)
    row = lax.broadcasted_iota(jnp.int32, (8, LANES), 0).astype(F32)
    chosen = [
        jnp.where(jnp.abs(v[3 * lines :, :] / blocks - row) < 0.5, 1.0, 0.0) for v in four
    ]
    for b in range(lines):
        here = slice(2 * lines + b, 2 * lines + b + 1)
        parts = [mask * v[here, :] for mask, v in zip(chosen, four)]
        task_ref[:, b * LANES : (b + 1) * LANES] = (parts[0] + parts[1]) + (parts[2] + parts[3])


def local(resid, attn, out_proj, out_bias, gain, task_bias, task_ids, neg_owner, neg_row):
    tok_rows = resid.shape[1]
    width = resid.shape[2]
    hard_count = neg_owner.shape[1]
    row_count = 2 * tok_rows
    blocks = lax.axis_size(BLK)
    pairs = blocks * tok_rows
    me = lax.axis_index(GRP)
    vmem = pl.BlockSpec(memory_space=pltpu.VMEM)
    smem = pl.BlockSpec(memory_space=pltpu.SMEM)
    params = pltpu.CompilerParams(vmem_limit_bytes=24 * 1024 * 1024)

    stream = pltpu.CompilerParams(vmem_limit_bytes=52 * 1024 * 1024)

    attn_rows = attn.reshape(row_count, width)
    far_rows = swap_chip(attn_rows)
    near_rows = swap_core(attn_rows)
    half = LANES // 2
    fill = ((0, 1), (0, half - tok_rows))
    requests = jnp.concatenate(
        [jnp.pad(neg_owner.T, fill), jnp.pad(neg_row.T, fill)], axis=1
    ).astype(BF16)
    task_onehot = (jnp.arange(task_bias.shape[0]) == task_ids[0]).astype(F32)
    bias_row = jnp.sum(task_onehot[:, None] * task_bias, axis=0, keepdims=True)
    far_rows, near_rows, requests, bias_row = lax.optimization_barrier(
        (far_rows, near_rows, requests, bias_row)
    )


    chunks = 8
    held = [
        pltpu.VMEM((chunks, out_proj.shape[0] // chunks, out_proj.shape[1]), BF16),
        pltpu.SemaphoreType.DMA((chunks,)),
    ]
    hbm = pl.BlockSpec(memory_space=pltpu.HBM)
    columns = pl.pallas_call(
        forward_kernel,
        out_shape=[jax.ShapeDtypeStruct((row_count, out_proj.shape[1]), BF16)] * 4,
        in_specs=[vmem] * 4 + [hbm],
        out_specs=[vmem] * 4,
        scratch_shapes=[held[0], pltpu.VMEM((4 * row_count, out_proj.shape[1]), F32), held[1]],
        compiler_params=stream,
    )(attn_rows, near_rows, far_rows, swap_core(far_rows), out_proj)
    parts = [
        columns[0],
        swap_core(columns[1]),
        swap_chip(columns[2]),
        lax.ppermute(columns[3], GRP, DIAGONAL),
    ]

    place = me.astype(jnp.int32).reshape(1)
    rows_f32 = jax.ShapeDtypeStruct((row_count, LANES), F32)
    own_spread, pooled, inv_rms, inv_norm = pl.pallas_call(
        embed_kernel,
        out_shape=(
            jax.ShapeDtypeStruct((blocks, row_count + 8, LANES), BF16),
            jax.ShapeDtypeStruct((row_count, width), F32),
            rows_f32,
            rows_f32,
        ),
        in_specs=[smem] + [vmem] * 9,
        out_specs=(vmem,) * 4,
        scratch_shapes=[pltpu.VMEM((4, row_count, width // 4), BF16)],
        compiler_params=params,
    )(
        place,
        *parts,
        resid.reshape(row_count, width),
        out_bias[None],
        gain[None],
        bias_row,
        requests,
    )
    spread = exchange(own_spread, BLK)
    q_all = spread[:, :tok_rows].reshape(pairs, LANES)
    p_own = spread[:, tok_rows:row_count].reshape(pairs, LANES)
    requests = spread[:, row_count : row_count + hard_count].astype(jnp.int32)
    owner = requests[:, :, :tok_rows]
    ids = ((owner // blocks) ^ me) * pairs + (owner % blocks) * tok_rows
    ids = (ids + requests[:, :, half : half + tok_rows]).reshape(-1)
    p_far = swap_chip(p_own)
    p_all = jnp.concatenate([p_own, swap_core(p_own), p_far, swap_core(p_far)])

    score_part = lax.dot_general(
        q_all, p_own, (((1,), (1,)), ((), ())), preferred_element_type=F32
    )
    negatives, hard_part = pl.pallas_call(
        lambda *refs: gather_kernel(hard_count, tok_rows, *refs),
        out_shape=(
            jax.ShapeDtypeStruct((hard_count, pairs, LANES), BF16),
            jax.ShapeDtypeStruct((pairs, LANES), F32),
        ),
        in_specs=[smem, vmem, vmem],
        out_specs=(vmem, vmem),
        scratch_shapes=[
            pltpu.VMEM((4 * pairs, LANES), F32),
            pltpu.VMEM((hard_count, pairs, LANES), F32),
        ],
        compiler_params=params,
    )(ids, q_all, p_all)
    part = jnp.concatenate([score_part, hard_part], axis=1).astype(SEND)
    part = exchange(part.reshape(blocks, tok_rows, pairs + LANES), BLK)
    part = jnp.sum(part.astype(F32), axis=0)
    losses, hard_probs, group_probs = pl.pallas_call(
        lambda *refs: softmax_kernel(hard_count, *refs),
        out_shape=(
            jax.ShapeDtypeStruct((tok_rows, LANES), F32),
            jax.ShapeDtypeStruct((blocks, tok_rows, LANES), BF16),
            jax.ShapeDtypeStruct((blocks, tok_rows, pairs), BF16),
        ),
        in_specs=[smem, vmem],
        out_specs=(vmem,) * 3,
        compiler_params=params,
    )((lax.axis_index(BLK) * tok_rows).astype(jnp.int32).reshape(1), part)
    losses = losses[:, 0]
    hard_probs = exchange(hard_probs, BLK).reshape(pairs, LANES)
    group_probs = exchange(group_probs, BLK).reshape(pairs, pairs)

    hard_add, hard_sum = pl.pallas_call(
        lambda *refs: scatter_kernel(hard_count, tok_rows, *refs),
        out_shape=(
            jax.ShapeDtypeStruct((4 * pairs, LANES), BF16),
            jax.ShapeDtypeStruct((pairs, LANES), F32),
        ),
        in_specs=[smem, vmem, vmem, vmem],
        out_specs=(vmem, vmem),
        scratch_shapes=[pltpu.VMEM((hard_count, pairs, LANES), F32)]
        + [pltpu.VMEM((4 * pairs, LANES), F32)] * hard_count,
        compiler_params=params,
    )(ids, hard_probs, q_all, negatives)
    hard_add = hard_add.reshape(4, pairs, LANES)
    crossed = swap_core(jnp.stack([hard_add[1], hard_add[3]]))
    over_chip = swap_chip((hard_add[2].astype(F32) + crossed[1].astype(F32)).astype(BF16))
    sums = pl.pallas_call(
        sums_kernel,
        out_shape=jax.ShapeDtypeStruct((blocks, 2, tok_rows, LANES), BF16),
        in_specs=[vmem] * 7,
        out_specs=vmem,
        compiler_params=params,
    )(group_probs, q_all, p_own, hard_sum, hard_add[0], crossed[0], over_chip)
    sums = exchange(sums, BLK)

    lines = width // LANES
    *cols, vectors = pl.pallas_call(
        pullback_kernel,
        out_shape=[jax.ShapeDtypeStruct((row_count, width // 4), BF16)] * 4
        + [jax.ShapeDtypeStruct((3 * lines + 8, LANES), F32)],
        in_specs=[smem] * 2 + [vmem] * 7,
        out_specs=[vmem] * 5,
        scratch_shapes=[
            pltpu.VMEM((row_count, width), F32),
            pltpu.VMEM((4, row_count, width // 4), BF16),
        ],
        compiler_params=params,
    )(place, task_ids, sums, own_spread, pooled, inv_rms, inv_norm, gain[None], bias_row)
    cols = [
        cols[0],
        swap_core(cols[1]),
        swap_chip(cols[2]),
        lax.ppermute(cols[3], GRP, DIAGONAL),
    ]
    vectors, *cols = lax.optimization_barrier((sum_over(vectors, "xh"), *cols))
    keep, send = pl.pallas_call(
        backward_kernel,
        out_shape=[jax.ShapeDtypeStruct((2, row_count, width), BF16)] * 2,
        in_specs=[vmem] * 4 + [hbm],
        out_specs=[vmem] * 2,
        scratch_shapes=held,
        compiler_params=stream,
    )(*cols, out_proj)
    vectors, keep, send = lax.optimization_barrier((vectors, keep, send))
    vectors = sum_over(vectors, "y")
    crossed = swap_core(send)
    far_sum = (keep[1].astype(F32) + crossed[1].astype(F32)).astype(BF16)
    first = swap_chip(far_sum[:, : width // 2])
    second = swap_chip(far_sum[:, width // 2 :])
    vectors, first = lax.optimization_barrier((vectors, first))
    vectors = sum_over(vectors, "z")
    far_sum = jnp.concatenate([first, second], axis=1).astype(F32)
    grad_attn = keep[0].astype(F32) + crossed[0].astype(F32) + far_sum

    four = [
        vectors,
        swap_core(vectors),
        swap_chip(vectors),
        lax.ppermute(vectors, GRP, DIAGONAL),
    ]
    grad_gain, grad_out_bias, grad_task_bias = pl.pallas_call(
        lambda *refs: finish_kernel(blocks, *refs),
        out_shape=[jax.ShapeDtypeStruct((lines, LANES), F32)] * 2
        + [jax.ShapeDtypeStruct(task_bias.shape, F32)],
        in_specs=[vmem] * 4,
        out_specs=[vmem] * 3,
        compiler_params=params,
    )(*four)
    return (
        losses,
        grad_attn.reshape(2, tok_rows, width),
        grad_gain.reshape(width),
        grad_task_bias,
        grad_out_bias.reshape(width),
    )


def solution(mesh):
    fine = Mesh(mesh.devices.reshape(2, 2, 2, 4, 4), ALL)
    in_specs = (
        P(None, ALL, None),
        P(None, ALL, None),
        P(None, GRP),
        P(),
        P(),
        P(),
        P(GRP),
        P(ALL, None),
        P(ALL, None),
    )
    out_specs = (P(ALL), P(None, ALL, None), P(), P(), P())
    return jax.shard_map(local, mesh=fine, in_specs=in_specs, out_specs=out_specs, check_vma=False)
```

```python
import jax
import jax.numpy as jnp
from jax import lax
from jax.experimental import pallas as pl
from jax.experimental.pallas import tpu as pltpu
from jax.sharding import Mesh, PartitionSpec as P

TAU = 0.02
LOSS_SCALE = 256.0
GRP = ("xl", "co")
BLK = ("xh", "y", "z")
ALL = GRP + BLK
SWAP = [(0, 1), (1, 0)]
DIAGONAL = [(0, 3), (1, 2), (2, 1), (3, 0)]
LANES = 128
F32 = jnp.float32
BF16 = jnp.bfloat16
SEND = jnp.float16


def swap_core(values):
    return lax.ppermute(values, "co", SWAP)


def swap_chip(values):
    return lax.ppermute(values, "xl", SWAP)


def from_ahead(values, axis, step):
    size = lax.axis_size(axis)
    return lax.ppermute(values, axis, [((i + step) % size, i) for i in range(size)])


def sum_over(values, axis):
    if lax.axis_size(axis) == 2:
        return values + from_ahead(values, axis, 1)
    one, two, three = [from_ahead(values, axis, step) for step in (1, 2, 3)]
    return (values + two) + (one + three)


def exchange(values, axes):
    return lax.all_to_all(values, axes, split_axis=0, concat_axis=0, tiled=True)


def embed_kernel(
    me, x0, x1, x2, x3, resid, out_bias, gain, bias_row, requests,
    spread, pooled, inv_rms, inv_norm, held,
):
    rows, width = resid.shape
    quarter = width // 4
    for i, x_ref in enumerate((x0, x1, x2, x3)):
        held[i] = x_ref[...]
    squares = jnp.zeros((rows, LANES), F32)
    for b in range(width // LANES):
        here = slice(b * LANES, (b + 1) * LANES)
        start = b * LANES % quarter
        projected = held[me[0] ^ (b * LANES // quarter), :, start : start + LANES]
        value = resid[:, here].astype(F32) + projected.astype(F32) + out_bias[:, here]
        pooled[:, here] = value
        squares = squares + value * value
    mean = jnp.sum(squares, axis=1, keepdims=True) / width
    rms = jnp.broadcast_to(lax.rsqrt(mean + 1e-05), (rows, LANES))
    inv_rms[...] = rms

    def mixture(b):
        here = slice(b * LANES, (b + 1) * LANES)
        return pooled[:, here] * rms * gain[:, here] + bias_row[:, here]

    squares = jnp.zeros((rows, LANES), F32)
    for b in range(width // LANES):
        value = mixture(b)
        squares = squares + value * value
    total = jnp.sum(squares, axis=1, keepdims=True)
    norm = jnp.broadcast_to(lax.rsqrt(total + 1e-06), (rows, LANES))
    inv_norm[...] = norm
    wanted = requests[...].astype(F32)
    for b in range(width // LANES):
        spread[b] = jnp.concatenate([mixture(b) * norm, wanted]).astype(BF16)


def pullback_kernel(
    me, task, sums, spread, pooled, inv_rms, inv_norm, gain, bias_row,
    y0, y1, y2, y3, vectors, grad, held,
):
    rows, width = pooled.shape
    half = rows // 2
    quarter = width // 4
    lines = width // LANES
    rms, norm = inv_rms[...], inv_norm[...]

    def across(values):
        return jnp.broadcast_to(jnp.sum(values, axis=1, keepdims=True), values.shape)

    def embedded(b):
        here = slice(b * LANES, (b + 1) * LANES)
        normed = pooled[:, here] * rms
        return normed, (normed * gain[:, here] + bias_row[:, here]) * norm

    along = jnp.zeros((rows, LANES), F32)
    for b in range(width // LANES):
        own = spread[b].astype(F32)
        other = jnp.concatenate([own[half:rows], own[:half]])
        both = jnp.concatenate([sums[b, 0].astype(F32), sums[b, 1].astype(F32)])
        cotangent = (both - other) / TAU
        grad[:, b * LANES : (b + 1) * LANES] = cotangent
        along = along + embedded(b)[1] * cotangent
    along = across(along)
    inner = jnp.zeros((rows, LANES), F32)
    for b in range(width // LANES):
        here = slice(b * LANES, (b + 1) * LANES)
        normed, unit = embedded(b)
        d_mixture = norm * (grad[:, here] - unit * along)
        vectors[b : b + 1, :] = jnp.sum(d_mixture * normed, axis=0, keepdims=True)
        vectors[2 * lines + b : 2 * lines + b + 1, :] = jnp.sum(d_mixture, axis=0, keepdims=True)
        d_normed = d_mixture * gain[:, here]
        grad[:, here] = d_normed
        inner = inner + d_normed * normed
    inner = across(inner) / width
    for b in range(lines):
        here = slice(b * LANES, (b + 1) * LANES)
        d_pooled = rms * (grad[:, here] - pooled[:, here] * rms * inner)
        vectors[lines + b : lines + b + 1, :] = jnp.sum(d_pooled, axis=0, keepdims=True)
        start = b * LANES % quarter
        held[b * LANES // quarter, :, start : start + LANES] = (LOSS_SCALE * d_pooled).astype(BF16)
    vectors[3 * lines :, :] = jnp.full((8, LANES), task[0].astype(F32))
    for i, y_ref in enumerate((y0, y1, y2, y3)):
        y_ref[...] = held[me[0] ^ i]


def gather_kernel(hard_count, tok_rows, ids, q_ref, p_ref, neg_ref, hard_ref, wide, picked):
    rows = q_ref.shape[0]
    wide[...] = p_ref[...].astype(F32)

    def pick(block, carry):
        for i in range(tok_rows):
            for k in range(hard_count):
                source = ids[(block * hard_count + k) * tok_rows + i]
                picked[k, pl.ds(block * tok_rows + i, 1), :] = wide[pl.ds(source, 1), :]
        return carry

    lax.fori_loop(0, rows // tok_rows, pick, 0)
    q = q_ref[...].astype(F32)
    lane = lax.broadcasted_iota(jnp.int32, (rows, LANES), 1)
    hard = jnp.zeros((rows, LANES), F32)
    for k in range(hard_count):
        chosen = picked[k]
        neg_ref[k] = chosen.astype(BF16)
        hard = jnp.where(lane == k, jnp.sum(q * chosen, axis=1, keepdims=True), hard)
    hard_ref[...] = hard


def scatter_kernel(hard_count, tok_rows, ids, w_ref, q_ref, neg_ref, add_ref, slot, *parts):
    rows = q_ref.shape[0]
    for part in parts:
        part[...] = jnp.zeros_like(part)
    q = q_ref[...].astype(F32)
    total = jnp.zeros((rows, LANES), F32)
    for k in range(hard_count):
        weight = w_ref[:, k : k + 1].astype(F32)
        slot[k] = weight * q
        total = total + weight * neg_ref[k].astype(F32)
    add_ref[4 * rows :, :] = total.astype(BF16)

    def place(block, carry):
        for i in range(tok_rows):
            for k in range(hard_count):
                target = pl.ds(ids[(block * hard_count + k) * tok_rows + i], 1)
                parts[k][target, :] += slot[k, pl.ds(block * tok_rows + i, 1), :]
        return carry

    lax.fori_loop(0, rows // tok_rows, place, 0)
    added = parts[0][...]
    for k in range(1, hard_count):
        added = added + parts[k][...]
    add_ref[: 4 * rows, :] = added.astype(BF16)


def stream_chunks(w_ref, held, sems):
    chunks, depth = held.shape[0], held.shape[1]
    copies = [
        pltpu.make_async_copy(w_ref.at[pl.ds(c * depth, depth), :], held.at[c], sems.at[c])
        for c in range(chunks)
    ]
    for copy in copies:
        copy.start()
    return copies


def forward_kernel(x0, x1, x2, x3, w_ref, y0, y1, y2, y3, held, total, sems):
    depth = held.shape[1]
    rows = y0.shape[0]
    for c, copy in enumerate(stream_chunks(w_ref, held, sems)):
        copy.wait()
        here = slice(c * depth, (c + 1) * depth)
        x = jnp.concatenate([x_ref[:, here] for x_ref in (x0, x1, x2, x3)])
        term = jnp.dot(x, held[c], preferred_element_type=F32)
        total[...] = term if c == 0 else total[...] + term
    for i, y_ref in enumerate((y0, y1, y2, y3)):
        y_ref[...] = total[i * rows : (i + 1) * rows, :].astype(BF16)


def backward_kernel(x0, x1, x2, x3, w_ref, keep_ref, send_ref, held, sems):
    depth = held.shape[1]
    rows = keep_ref.shape[1]
    copies = stream_chunks(w_ref, held, sems)
    x = jnp.concatenate([x_ref[...] for x_ref in (x0, x1, x2, x3)])
    for c, copy in enumerate(copies):
        copy.wait()
        term = lax.dot_general(x, held[c], (((1,), (1,)), ((), ())), preferred_element_type=F32)
        here = slice(c * depth, (c + 1) * depth)
        for i in range(4):
            out_ref = send_ref if i % 2 else keep_ref
            out_ref[i // 2, :, here] = term[i * rows : (i + 1) * rows].astype(BF16)


def softmax_kernel(hard_count, at, score_ref, losses_ref, hard_ref, group_ref, held, sem):
    rows, width = score_ref.shape
    pairs = width - LANES
    scores = score_ref[:, :pairs] / TAU
    weights = jnp.exp(scores)
    slot = lax.broadcasted_iota(jnp.int32, (rows, LANES), 1)
    hard_weights = jnp.where(slot < hard_count, jnp.exp(score_ref[:, pairs:] / TAU), 0.0)
    totals = jnp.sum(weights, axis=1, keepdims=True) + jnp.sum(hard_weights, axis=1, keepdims=True)
    column = lax.broadcasted_iota(jnp.int32, (rows, pairs), 1)
    row = lax.broadcasted_iota(jnp.int32, (rows, pairs), 0)
    own = jnp.sum(jnp.where(column == row + at[0], scores, 0.0), axis=1, keepdims=True)
    losses_ref[...] = jnp.broadcast_to(jnp.log(totals) - own, (rows, LANES))
    hard_probs = (hard_weights / totals).astype(BF16)
    held[...] = (weights / totals).astype(BF16)
    copies = [
        pltpu.make_async_copy(held, group_ref.at[b], sem.at[b]) for b in range(group_ref.shape[0])
    ]
    for copy in copies:
        copy.start()
    for b in range(hard_ref.shape[0]):
        hard_ref[b] = hard_probs
    for copy in copies:
        copy.wait()


def sums_kernel(probs_ref, q_ref, p_ref, hard_ref, add_ref, near_ref, far_ref, out_ref):
    tok_rows = out_ref.shape[2]
    probs = probs_ref[...]
    sum_q = jnp.dot(probs, p_ref[...], preferred_element_type=F32)
    sum_q = sum_q + hard_ref[...].astype(F32)
    sum_p = lax.dot_general(
        probs, q_ref[...], (((0,), (0,)), ((), ())), preferred_element_type=F32
    )
    sum_p = sum_p + add_ref[...].astype(F32) + near_ref[...].astype(F32) + far_ref[...].astype(F32)
    for b in range(out_ref.shape[0]):
        here = slice(b * tok_rows, (b + 1) * tok_rows)
        out_ref[b, 0] = sum_q[here].astype(BF16)
        out_ref[b, 1] = sum_p[here].astype(BF16)


def finish_kernel(blocks, v0, v1, v2, v3, gain_ref, bias_ref, task_ref):
    lines = gain_ref.shape[0]
    four = (v0, v1, v2, v3)

    def total(start):
        parts = [v[start : start + lines, :] for v in four]
        return (parts[0] + parts[1]) + (parts[2] + parts[3])

    gain_ref[...] = total(0)
    bias_ref[...] = total(lines)
    row = lax.broadcasted_iota(jnp.int32, (8, LANES), 0).astype(F32)
    chosen = [
        jnp.where(jnp.abs(v[3 * lines :, :] / blocks - row) < 0.5, 1.0, 0.0) for v in four
    ]
    for b in range(lines):
        here = slice(2 * lines + b, 2 * lines + b + 1)
        parts = [mask * v[here, :] for mask, v in zip(chosen, four)]
        task_ref[:, b * LANES : (b + 1) * LANES] = (parts[0] + parts[1]) + (parts[2] + parts[3])


def local(resid, attn, out_proj, out_bias, gain, task_bias, task_ids, neg_owner, neg_row):
    tok_rows = resid.shape[1]
    width = resid.shape[2]
    hard_count = neg_owner.shape[1]
    row_count = 2 * tok_rows
    blocks = lax.axis_size(BLK)
    pairs = blocks * tok_rows
    me = lax.axis_index(GRP)
    vmem = pl.BlockSpec(memory_space=pltpu.VMEM)
    smem = pl.BlockSpec(memory_space=pltpu.SMEM)
    params = pltpu.CompilerParams(vmem_limit_bytes=24 * 1024 * 1024)

    stream = pltpu.CompilerParams(vmem_limit_bytes=52 * 1024 * 1024)

    attn_rows = attn.reshape(row_count, width)
    far_rows = swap_chip(attn_rows)
    near_rows = swap_core(attn_rows)
    half = LANES // 2
    fill = ((0, 1), (0, half - tok_rows))
    requests = jnp.concatenate(
        [jnp.pad(neg_owner.T, fill), jnp.pad(neg_row.T, fill)], axis=1
    ).astype(BF16)
    task_onehot = (jnp.arange(task_bias.shape[0]) == task_ids[0]).astype(F32)
    bias_row = jnp.sum(task_onehot[:, None] * task_bias, axis=0, keepdims=True)
    far_rows, near_rows, requests, bias_row = lax.optimization_barrier(
        (far_rows, near_rows, requests, bias_row)
    )


    chunks = 8
    held = [
        pltpu.VMEM((chunks, out_proj.shape[0] // chunks, out_proj.shape[1]), BF16),
        pltpu.SemaphoreType.DMA((chunks,)),
    ]
    hbm = pl.BlockSpec(memory_space=pltpu.HBM)
    columns = pl.pallas_call(
        forward_kernel,
        out_shape=[jax.ShapeDtypeStruct((row_count, out_proj.shape[1]), BF16)] * 4,
        in_specs=[vmem] * 4 + [hbm],
        out_specs=[vmem] * 4,
        scratch_shapes=[held[0], pltpu.VMEM((4 * row_count, out_proj.shape[1]), F32), held[1]],
        compiler_params=stream,
    )(attn_rows, near_rows, far_rows, swap_core(far_rows), out_proj)
    parts = [
        columns[0],
        swap_core(columns[1]),
        swap_chip(columns[2]),
        lax.ppermute(columns[3], GRP, DIAGONAL),
    ]

    place = me.astype(jnp.int32).reshape(1)
    rows_f32 = jax.ShapeDtypeStruct((row_count, LANES), F32)
    own_spread, pooled, inv_rms, inv_norm = pl.pallas_call(
        embed_kernel,
        out_shape=(
            jax.ShapeDtypeStruct((blocks, row_count + 8, LANES), BF16),
            jax.ShapeDtypeStruct((row_count, width), F32),
            rows_f32,
            rows_f32,
        ),
        in_specs=[smem] + [vmem] * 9,
        out_specs=(vmem,) * 4,
        scratch_shapes=[pltpu.VMEM((4, row_count, width // 4), BF16)],
        compiler_params=params,
    )(
        place,
        *parts,
        resid.reshape(row_count, width),
        out_bias[None],
        gain[None],
        bias_row,
        requests,
    )
    spread = exchange(own_spread, BLK)
    q_all = spread[:, :tok_rows].reshape(pairs, LANES)
    p_own = spread[:, tok_rows:row_count].reshape(pairs, LANES)
    requests = spread[:, row_count : row_count + hard_count].astype(jnp.int32)
    owner = requests[:, :, :tok_rows]
    ids = ((owner // blocks) ^ me) * pairs + (owner % blocks) * tok_rows
    ids = (ids + requests[:, :, half : half + tok_rows]).reshape(-1)
    p_far = swap_chip(p_own)
    p_all = jnp.concatenate([p_own, swap_core(p_own), p_far, swap_core(p_far)])

    score_part = lax.dot_general(
        q_all, p_own, (((1,), (1,)), ((), ())), preferred_element_type=F32
    )
    negatives, hard_part = pl.pallas_call(
        lambda *refs: gather_kernel(hard_count, tok_rows, *refs),
        out_shape=(
            jax.ShapeDtypeStruct((hard_count, pairs, LANES), BF16),
            jax.ShapeDtypeStruct((pairs, LANES), F32),
        ),
        in_specs=[smem, vmem, vmem],
        out_specs=(vmem, vmem),
        scratch_shapes=[
            pltpu.VMEM((4 * pairs, LANES), F32),
            pltpu.VMEM((hard_count, pairs, LANES), F32),
        ],
        compiler_params=params,
    )(ids, q_all, p_all)
    part = jnp.concatenate([score_part, hard_part], axis=1).astype(SEND)
    part = exchange(part.reshape(blocks, tok_rows, pairs + LANES), BLK)
    part = jnp.sum(part.astype(F32), axis=0)
    losses, hard_probs, group_probs = pl.pallas_call(
        lambda *refs: softmax_kernel(hard_count, *refs),
        out_shape=(
            jax.ShapeDtypeStruct((tok_rows, LANES), F32),
            jax.ShapeDtypeStruct((blocks, tok_rows, LANES), BF16),
            jax.ShapeDtypeStruct((blocks, tok_rows, pairs), BF16),
        ),
        in_specs=[smem, vmem],
        out_specs=(vmem, vmem, hbm),
        scratch_shapes=[
            pltpu.VMEM((tok_rows, pairs), BF16),
            pltpu.SemaphoreType.DMA((blocks,)),
        ],
        compiler_params=pltpu.CompilerParams(vmem_limit_bytes=58 * 1024 * 1024),
    )((lax.axis_index(BLK) * tok_rows).astype(jnp.int32).reshape(1), part)
    losses = losses[:, 0]
    hard_probs = exchange(hard_probs, BLK).reshape(pairs, LANES)
    group_probs = exchange(group_probs, BLK).reshape(pairs, pairs)

    hard_add = pl.pallas_call(
        lambda *refs: scatter_kernel(hard_count, tok_rows, *refs),
        out_shape=jax.ShapeDtypeStruct((5 * pairs, LANES), BF16),
        in_specs=[smem, vmem, vmem, vmem],
        out_specs=vmem,
        scratch_shapes=[pltpu.VMEM((hard_count, pairs, LANES), F32)]
        + [pltpu.VMEM((4 * pairs, LANES), F32)] * hard_count,
        compiler_params=params,
    )(ids, hard_probs, q_all, negatives)
    hard_add = hard_add.reshape(5, pairs, LANES)
    crossed = swap_core(jnp.stack([hard_add[1], hard_add[3]]))
    over_chip = swap_chip((hard_add[2].astype(F32) + crossed[1].astype(F32)).astype(BF16))
    sums = pl.pallas_call(
        sums_kernel,
        out_shape=jax.ShapeDtypeStruct((blocks, 2, tok_rows, LANES), BF16),
        in_specs=[vmem] * 7,
        out_specs=vmem,
        compiler_params=params,
    )(group_probs, q_all, p_own, hard_add[4], hard_add[0], crossed[0], over_chip)
    sums = exchange(sums, BLK)

    lines = width // LANES
    *cols, vectors = pl.pallas_call(
        pullback_kernel,
        out_shape=[jax.ShapeDtypeStruct((row_count, width // 4), BF16)] * 4
        + [jax.ShapeDtypeStruct((3 * lines + 8, LANES), F32)],
        in_specs=[smem] * 2 + [vmem] * 7,
        out_specs=[vmem] * 5,
        scratch_shapes=[
            pltpu.VMEM((row_count, width), F32),
            pltpu.VMEM((4, row_count, width // 4), BF16),
        ],
        compiler_params=params,
    )(place, task_ids, sums, own_spread, pooled, inv_rms, inv_norm, gain[None], bias_row)
    cols = [
        cols[0],
        swap_core(cols[1]),
        swap_chip(cols[2]),
        lax.ppermute(cols[3], GRP, DIAGONAL),
    ]
    vectors, *cols = lax.optimization_barrier((sum_over(vectors, "xh"), *cols))
    keep, send = pl.pallas_call(
        backward_kernel,
        out_shape=[jax.ShapeDtypeStruct((2, row_count, width), BF16)] * 2,
        in_specs=[vmem] * 4 + [hbm],
        out_specs=[vmem] * 2,
        scratch_shapes=held,
        compiler_params=stream,
    )(*cols, out_proj)
    vectors, keep, send = lax.optimization_barrier((vectors, keep, send))
    vectors = sum_over(vectors, "y")
    crossed = swap_core(send)
    far_sum = (keep[1].astype(F32) + crossed[1].astype(F32)).astype(BF16)
    first = swap_chip(far_sum[:, : width // 2])
    second = swap_chip(far_sum[:, width // 2 :])
    vectors, first = lax.optimization_barrier((vectors, first))
    vectors = sum_over(vectors, "z")
    far_sum = jnp.concatenate([first, second], axis=1).astype(F32)
    grad_attn = keep[0].astype(F32) + crossed[0].astype(F32) + far_sum

    four = [
        vectors,
        swap_core(vectors),
        swap_chip(vectors),
        lax.ppermute(vectors, GRP, DIAGONAL),
    ]
    grad_gain, grad_out_bias, grad_task_bias = pl.pallas_call(
        lambda *refs: finish_kernel(blocks, *refs),
        out_shape=[jax.ShapeDtypeStruct((lines, LANES), F32)] * 2
        + [jax.ShapeDtypeStruct(task_bias.shape, F32)],
        in_specs=[vmem] * 4,
        out_specs=[vmem] * 3,
        compiler_params=params,
    )(*four)
    return (
        losses,
        grad_attn.reshape(2, tok_rows, width),
        grad_gain.reshape(width),
        grad_task_bias,
        grad_out_bias.reshape(width),
    )


def solution(mesh):
    fine = Mesh(mesh.devices.reshape(2, 2, 2, 4, 4), ALL)
    in_specs = (
        P(None, ALL, None),
        P(None, ALL, None),
        P(None, GRP),
        P(),
        P(),
        P(),
        P(GRP),
        P(ALL, None),
        P(ALL, None),
    )
    out_specs = (P(ALL), P(None, ALL, None), P(), P(), P())
    return jax.shard_map(local, mesh=fine, in_specs=in_specs, out_specs=out_specs, check_vma=False)
```

```python
import jax
import jax.numpy as jnp
from jax import lax
from jax.experimental import pallas as pl
from jax.experimental.pallas import tpu as pltpu
from jax.sharding import Mesh, PartitionSpec as P

TAU = 0.02
LOSS_SCALE = 256.0
GRP = ("xl", "co")
BLK = ("xh", "y", "z")
ALL = GRP + BLK
SWAP = [(0, 1), (1, 0)]
DIAGONAL = [(0, 3), (1, 2), (2, 1), (3, 0)]
LANES = 128
F32 = jnp.float32
BF16 = jnp.bfloat16
SEND = jnp.float16


def swap_core(values):
    return lax.ppermute(values, "co", SWAP)


def swap_chip(values):
    return lax.ppermute(values, "xl", SWAP)


def from_ahead(values, axis, step):
    size = lax.axis_size(axis)
    return lax.ppermute(values, axis, [((i + step) % size, i) for i in range(size)])


def double_over(values, axis):
    size = lax.axis_size(axis)
    step = 1
    while step < size:
        values = values + lax.ppermute(values, axis, [(i, i ^ step) for i in range(size)])
        step *= 2
    return values


def sum_over(values, axis):
    if lax.axis_size(axis) == 2:
        return values + from_ahead(values, axis, 1)
    one, two, three = [from_ahead(values, axis, step) for step in (1, 2, 3)]
    return (values + two) + (one + three)


def exchange(values, axes):
    return lax.all_to_all(values, axes, split_axis=0, concat_axis=0, tiled=True)


def embed_kernel(
    me, x0, x1, x2, x3, resid, out_bias, gain, bias_row, requests,
    spread, pooled, inv_rms, inv_norm, held,
):
    rows, width = resid.shape
    quarter = width // 4
    for i, x_ref in enumerate((x0, x1, x2, x3)):
        held[i] = x_ref[...]
    squares = jnp.zeros((rows, LANES), F32)
    for b in range(width // LANES):
        here = slice(b * LANES, (b + 1) * LANES)
        start = b * LANES % quarter
        projected = held[me[0] ^ (b * LANES // quarter), :, start : start + LANES]
        value = resid[:, here].astype(F32) + projected.astype(F32) + out_bias[:, here]
        pooled[:, here] = value
        squares = squares + value * value
    mean = jnp.sum(squares, axis=1, keepdims=True) / width
    rms = jnp.broadcast_to(lax.rsqrt(mean + 1e-05), (rows, LANES))
    inv_rms[...] = rms

    def mixture(b):
        here = slice(b * LANES, (b + 1) * LANES)
        return pooled[:, here] * rms * gain[:, here] + bias_row[:, here]

    squares = jnp.zeros((rows, LANES), F32)
    for b in range(width // LANES):
        value = mixture(b)
        squares = squares + value * value
    total = jnp.sum(squares, axis=1, keepdims=True)
    norm = jnp.broadcast_to(lax.rsqrt(total + 1e-06), (rows, LANES))
    inv_norm[...] = norm
    wanted = requests[...].astype(F32)
    for b in range(width // LANES):
        spread[b] = jnp.concatenate([mixture(b) * norm, wanted]).astype(BF16)


def pullback_kernel(
    me, task, sums, spread, pooled, inv_rms, inv_norm, gain, bias_row,
    y0, y1, y2, y3, vectors, grad, held,
):
    rows, width = pooled.shape
    half = rows // 2
    quarter = width // 4
    lines = width // LANES
    rms, norm = inv_rms[...], inv_norm[...]

    def across(values):
        return jnp.broadcast_to(jnp.sum(values, axis=1, keepdims=True), values.shape)

    def embedded(b):
        here = slice(b * LANES, (b + 1) * LANES)
        normed = pooled[:, here] * rms
        return normed, (normed * gain[:, here] + bias_row[:, here]) * norm

    along = jnp.zeros((rows, LANES), F32)
    for b in range(width // LANES):
        own = spread[b].astype(F32)
        other = jnp.concatenate([own[half:rows], own[:half]])
        both = jnp.concatenate([sums[b, 0].astype(F32), sums[b, 1].astype(F32)])
        cotangent = (both - other) / TAU
        grad[:, b * LANES : (b + 1) * LANES] = cotangent
        along = along + embedded(b)[1] * cotangent
    along = across(along)
    inner = jnp.zeros((rows, LANES), F32)
    for b in range(width // LANES):
        here = slice(b * LANES, (b + 1) * LANES)
        normed, unit = embedded(b)
        d_mixture = norm * (grad[:, here] - unit * along)
        vectors[b : b + 1, :] = jnp.sum(d_mixture * normed, axis=0, keepdims=True)
        vectors[2 * lines + b : 2 * lines + b + 1, :] = jnp.sum(d_mixture, axis=0, keepdims=True)
        d_normed = d_mixture * gain[:, here]
        grad[:, here] = d_normed
        inner = inner + d_normed * normed
    inner = across(inner) / width
    for b in range(lines):
        here = slice(b * LANES, (b + 1) * LANES)
        d_pooled = rms * (grad[:, here] - pooled[:, here] * rms * inner)
        vectors[lines + b : lines + b + 1, :] = jnp.sum(d_pooled, axis=0, keepdims=True)
        start = b * LANES % quarter
        held[b * LANES // quarter, :, start : start + LANES] = (LOSS_SCALE * d_pooled).astype(BF16)
    vectors[3 * lines :, :] = jnp.full((8, LANES), task[0].astype(F32))
    for i, y_ref in enumerate((y0, y1, y2, y3)):
        y_ref[...] = held[me[0] ^ i]


def gather_kernel(hard_count, tok_rows, ids, q_ref, p_ref, neg_ref, hard_ref, wide, picked):
    rows = q_ref.shape[0]
    wide[...] = p_ref[...].astype(F32)

    def pick(block, carry):
        for i in range(tok_rows):
            for k in range(hard_count):
                source = ids[(block * hard_count + k) * tok_rows + i]
                picked[k, pl.ds(block * tok_rows + i, 1), :] = wide[pl.ds(source, 1), :]
        return carry

    lax.fori_loop(0, rows // tok_rows, pick, 0)
    q = q_ref[...].astype(F32)
    lane = lax.broadcasted_iota(jnp.int32, (rows, LANES), 1)
    hard = jnp.zeros((rows, LANES), F32)
    for k in range(hard_count):
        chosen = picked[k]
        neg_ref[k] = chosen.astype(BF16)
        hard = jnp.where(lane == k, jnp.sum(q * chosen, axis=1, keepdims=True), hard)
    hard_ref[...] = hard


def scatter_kernel(hard_count, tok_rows, ids, w_ref, q_ref, neg_ref, add_ref, slot, *parts):
    rows = q_ref.shape[0]
    for part in parts:
        part[...] = jnp.zeros_like(part)
    q = q_ref[...].astype(F32)
    total = jnp.zeros((rows, LANES), F32)
    for k in range(hard_count):
        weight = w_ref[:, k : k + 1].astype(F32)
        slot[k] = weight * q
        total = total + weight * neg_ref[k].astype(F32)
    add_ref[4 * rows :, :] = total.astype(BF16)

    def place(block, carry):
        for i in range(tok_rows):
            for k in range(hard_count):
                target = pl.ds(ids[(block * hard_count + k) * tok_rows + i], 1)
                parts[k][target, :] += slot[k, pl.ds(block * tok_rows + i, 1), :]
        return carry

    lax.fori_loop(0, rows // tok_rows, place, 0)
    added = parts[0][...]
    for k in range(1, hard_count):
        added = added + parts[k][...]
    add_ref[: 4 * rows, :] = added.astype(BF16)


def stream_chunks(w_ref, held, sems):
    chunks, depth = held.shape[0], held.shape[1]
    copies = [
        pltpu.make_async_copy(w_ref.at[pl.ds(c * depth, depth), :], held.at[c], sems.at[c])
        for c in range(chunks)
    ]
    for copy in copies:
        copy.start()
    return copies


def forward_kernel(x0, x1, x2, x3, w_ref, y0, y1, y2, y3, held, total, sems):
    depth = held.shape[1]
    rows = y0.shape[0]
    for c, copy in enumerate(stream_chunks(w_ref, held, sems)):
        copy.wait()
        here = slice(c * depth, (c + 1) * depth)
        x = jnp.concatenate([x_ref[:, here] for x_ref in (x0, x1, x2, x3)])
        term = jnp.dot(x, held[c], preferred_element_type=F32)
        total[...] = term if c == 0 else total[...] + term
    for i, y_ref in enumerate((y0, y1, y2, y3)):
        y_ref[...] = total[i * rows : (i + 1) * rows, :].astype(BF16)


def backward_kernel(x0, x1, x2, x3, w_ref, keep_ref, send_ref, held, sems):
    depth = held.shape[1]
    rows = keep_ref.shape[1]
    copies = stream_chunks(w_ref, held, sems)
    x = jnp.concatenate([x_ref[...] for x_ref in (x0, x1, x2, x3)])
    for c, copy in enumerate(copies):
        copy.wait()
        term = lax.dot_general(x, held[c], (((1,), (1,)), ((), ())), preferred_element_type=F32)
        here = slice(c * depth, (c + 1) * depth)
        for i in range(4):
            out_ref = send_ref if i % 2 else keep_ref
            out_ref[i // 2, :, here] = term[i * rows : (i + 1) * rows].astype(BF16)


def softmax_kernel(hard_count, at, score_ref, losses_ref, hard_ref, group_ref):
    rows, width = score_ref.shape
    pairs = width - LANES
    scores = score_ref[:, :pairs] / TAU
    weights = jnp.exp(scores)
    slot = lax.broadcasted_iota(jnp.int32, (rows, LANES), 1)
    hard_weights = jnp.where(slot < hard_count, jnp.exp(score_ref[:, pairs:] / TAU), 0.0)
    totals = jnp.sum(weights, axis=1, keepdims=True) + jnp.sum(hard_weights, axis=1, keepdims=True)
    column = lax.broadcasted_iota(jnp.int32, (rows, pairs), 1)
    row = lax.broadcasted_iota(jnp.int32, (rows, pairs), 0)
    own = jnp.sum(jnp.where(column == row + at[0], scores, 0.0), axis=1, keepdims=True)
    losses_ref[...] = jnp.broadcast_to(jnp.log(totals) - own, (rows, LANES))
    hard_probs = (hard_weights / totals).astype(BF16)
    probs = (weights / totals).astype(BF16)
    for b in range(hard_ref.shape[0]):
        hard_ref[b] = hard_probs
        group_ref[b] = probs


def sums_kernel(probs_ref, q_ref, p_ref, hard_ref, add_ref, near_ref, far_ref, out_ref):
    tok_rows = out_ref.shape[2]
    probs = probs_ref[...]
    sum_q = jnp.dot(probs, p_ref[...], preferred_element_type=F32)
    sum_q = sum_q + hard_ref[...].astype(F32)
    sum_p = lax.dot_general(
        probs, q_ref[...], (((0,), (0,)), ((), ())), preferred_element_type=F32
    )
    sum_p = sum_p + add_ref[...].astype(F32) + near_ref[...].astype(F32) + far_ref[...].astype(F32)
    for b in range(out_ref.shape[0]):
        here = slice(b * tok_rows, (b + 1) * tok_rows)
        out_ref[b, 0] = sum_q[here].astype(BF16)
        out_ref[b, 1] = sum_p[here].astype(BF16)


def finish_kernel(blocks, v0, v1, v2, v3, gain_ref, bias_ref, task_ref):
    lines = gain_ref.shape[0]
    four = (v0, v1, v2, v3)

    def total(start):
        parts = [v[start : start + lines, :] for v in four]
        return (parts[0] + parts[1]) + (parts[2] + parts[3])

    gain_ref[...] = total(0)
    bias_ref[...] = total(lines)
    row = lax.broadcasted_iota(jnp.int32, (8, LANES), 0).astype(F32)
    chosen = [
        jnp.where(jnp.abs(v[3 * lines :, :] / blocks - row) < 0.5, 1.0, 0.0) for v in four
    ]
    for b in range(lines):
        here = slice(2 * lines + b, 2 * lines + b + 1)
        parts = [mask * v[here, :] for mask, v in zip(chosen, four)]
        task_ref[:, b * LANES : (b + 1) * LANES] = (parts[0] + parts[1]) + (parts[2] + parts[3])


def local(resid, attn, out_proj, out_bias, gain, task_bias, task_ids, neg_owner, neg_row):
    tok_rows = resid.shape[1]
    width = resid.shape[2]
    hard_count = neg_owner.shape[1]
    row_count = 2 * tok_rows
    blocks = lax.axis_size(BLK)
    pairs = blocks * tok_rows
    me = lax.axis_index(GRP)
    vmem = pl.BlockSpec(memory_space=pltpu.VMEM)
    smem = pl.BlockSpec(memory_space=pltpu.SMEM)
    params = pltpu.CompilerParams(vmem_limit_bytes=24 * 1024 * 1024)

    stream = pltpu.CompilerParams(vmem_limit_bytes=52 * 1024 * 1024)

    attn_rows = attn.reshape(row_count, width)
    far_rows = swap_chip(attn_rows)
    near_rows = swap_core(attn_rows)
    half = LANES // 2
    fill = ((0, 1), (0, half - tok_rows))
    requests = jnp.concatenate(
        [jnp.pad(neg_owner.T, fill), jnp.pad(neg_row.T, fill)], axis=1
    ).astype(BF16)
    task_onehot = (jnp.arange(task_bias.shape[0]) == task_ids[0]).astype(F32)
    bias_row = jnp.sum(task_onehot[:, None] * task_bias, axis=0, keepdims=True)
    far_rows, near_rows, requests, bias_row = lax.optimization_barrier(
        (far_rows, near_rows, requests, bias_row)
    )


    chunks = 8
    held = [
        pltpu.VMEM((chunks, out_proj.shape[0] // chunks, out_proj.shape[1]), BF16),
        pltpu.SemaphoreType.DMA((chunks,)),
    ]
    hbm = pl.BlockSpec(memory_space=pltpu.HBM)
    columns = pl.pallas_call(
        forward_kernel,
        out_shape=[jax.ShapeDtypeStruct((row_count, out_proj.shape[1]), BF16)] * 4,
        in_specs=[vmem] * 4 + [hbm],
        out_specs=[vmem] * 4,
        scratch_shapes=[held[0], pltpu.VMEM((4 * row_count, out_proj.shape[1]), F32), held[1]],
        compiler_params=stream,
    )(attn_rows, near_rows, far_rows, swap_core(far_rows), out_proj)
    parts = [
        columns[0],
        swap_core(columns[1]),
        swap_chip(columns[2]),
        lax.ppermute(columns[3], GRP, DIAGONAL),
    ]

    place = me.astype(jnp.int32).reshape(1)
    rows_f32 = jax.ShapeDtypeStruct((row_count, LANES), F32)
    own_spread, pooled, inv_rms, inv_norm = pl.pallas_call(
        embed_kernel,
        out_shape=(
            jax.ShapeDtypeStruct((blocks, row_count + 8, LANES), BF16),
            jax.ShapeDtypeStruct((row_count, width), F32),
            rows_f32,
            rows_f32,
        ),
        in_specs=[smem] + [vmem] * 9,
        out_specs=(vmem,) * 4,
        scratch_shapes=[pltpu.VMEM((4, row_count, width // 4), BF16)],
        compiler_params=params,
    )(
        place,
        *parts,
        resid.reshape(row_count, width),
        out_bias[None],
        gain[None],
        bias_row,
        requests,
    )
    spread = exchange(own_spread, BLK)
    q_all = spread[:, :tok_rows].reshape(pairs, LANES)
    p_own = spread[:, tok_rows:row_count].reshape(pairs, LANES)
    requests = spread[:, row_count : row_count + hard_count].astype(jnp.int32)
    owner = requests[:, :, :tok_rows]
    ids = ((owner // blocks) ^ me) * pairs + (owner % blocks) * tok_rows
    ids = (ids + requests[:, :, half : half + tok_rows]).reshape(-1)
    p_far = swap_chip(p_own)
    p_all = jnp.concatenate([p_own, swap_core(p_own), p_far, swap_core(p_far)])

    score_part = lax.dot_general(
        q_all, p_own, (((1,), (1,)), ((), ())), preferred_element_type=F32
    )
    negatives, hard_part = pl.pallas_call(
        lambda *refs: gather_kernel(hard_count, tok_rows, *refs),
        out_shape=(
            jax.ShapeDtypeStruct((hard_count, pairs, LANES), BF16),
            jax.ShapeDtypeStruct((pairs, LANES), F32),
        ),
        in_specs=[smem, vmem, vmem],
        out_specs=(vmem, vmem),
        scratch_shapes=[
            pltpu.VMEM((4 * pairs, LANES), F32),
            pltpu.VMEM((hard_count, pairs, LANES), F32),
        ],
        compiler_params=params,
    )(ids, q_all, p_all)
    part = jnp.concatenate([score_part, hard_part], axis=1).astype(SEND)
    part = exchange(part.reshape(blocks, tok_rows, pairs + LANES), BLK)
    part = jnp.sum(part.astype(F32), axis=0)
    losses, hard_probs, group_probs = pl.pallas_call(
        lambda *refs: softmax_kernel(hard_count, *refs),
        out_shape=(
            jax.ShapeDtypeStruct((tok_rows, LANES), F32),
            jax.ShapeDtypeStruct((blocks, tok_rows, LANES), BF16),
            jax.ShapeDtypeStruct((blocks, tok_rows, pairs), BF16),
        ),
        in_specs=[smem, vmem],
        out_specs=(vmem,) * 3,
        compiler_params=params,
    )((lax.axis_index(BLK) * tok_rows).astype(jnp.int32).reshape(1), part)
    losses = losses[:, 0]
    hard_probs = exchange(hard_probs, BLK).reshape(pairs, LANES)
    group_probs = exchange(group_probs, BLK).reshape(pairs, pairs)

    hard_add = pl.pallas_call(
        lambda *refs: scatter_kernel(hard_count, tok_rows, *refs),
        out_shape=jax.ShapeDtypeStruct((5 * pairs, LANES), BF16),
        in_specs=[smem, vmem, vmem, vmem],
        out_specs=vmem,
        scratch_shapes=[pltpu.VMEM((hard_count, pairs, LANES), F32)]
        + [pltpu.VMEM((4 * pairs, LANES), F32)] * hard_count,
        compiler_params=params,
    )(ids, hard_probs, q_all, negatives)
    hard_add = hard_add.reshape(5, pairs, LANES)
    crossed = swap_core(jnp.stack([hard_add[1], hard_add[3]]))
    over_chip = swap_chip((hard_add[2].astype(F32) + crossed[1].astype(F32)).astype(BF16))
    sums = pl.pallas_call(
        sums_kernel,
        out_shape=jax.ShapeDtypeStruct((blocks, 2, tok_rows, LANES), BF16),
        in_specs=[vmem] * 7,
        out_specs=vmem,
        compiler_params=params,
    )(group_probs, q_all, p_own, hard_add[4], hard_add[0], crossed[0], over_chip)
    sums = exchange(sums, BLK)

    lines = width // LANES
    *cols, vectors = pl.pallas_call(
        pullback_kernel,
        out_shape=[jax.ShapeDtypeStruct((row_count, width // 4), BF16)] * 4
        + [jax.ShapeDtypeStruct((3 * lines + 8, LANES), F32)],
        in_specs=[smem] * 2 + [vmem] * 7,
        out_specs=[vmem] * 5,
        scratch_shapes=[
            pltpu.VMEM((row_count, width), F32),
            pltpu.VMEM((4, row_count, width // 4), BF16),
        ],
        compiler_params=params,
    )(place, task_ids, sums, own_spread, pooled, inv_rms, inv_norm, gain[None], bias_row)
    cols = [
        cols[0],
        swap_core(cols[1]),
        swap_chip(cols[2]),
        lax.ppermute(cols[3], GRP, DIAGONAL),
    ]
    vectors, *cols = lax.optimization_barrier((sum_over(vectors, "xh"), *cols))
    keep, send = pl.pallas_call(
        backward_kernel,
        out_shape=[jax.ShapeDtypeStruct((2, row_count, width), BF16)] * 2,
        in_specs=[vmem] * 4 + [hbm],
        out_specs=[vmem] * 2,
        scratch_shapes=held,
        compiler_params=stream,
    )(*cols, out_proj)
    vectors, keep, send = lax.optimization_barrier((vectors, keep, send))
    vectors = sum_over(vectors, "y")
    crossed = swap_core(send)
    far_sum = (keep[1].astype(F32) + crossed[1].astype(F32)).astype(BF16)
    first = swap_chip(far_sum[:, : width // 2])
    second = swap_chip(far_sum[:, width // 2 :])
    vectors = double_over(vectors, "z")
    vectors, first = lax.optimization_barrier((vectors, first))
    far_sum = jnp.concatenate([first, second], axis=1).astype(F32)
    grad_attn = keep[0].astype(F32) + crossed[0].astype(F32) + far_sum

    four = [
        vectors,
        swap_core(vectors),
        swap_chip(vectors),
        lax.ppermute(vectors, GRP, DIAGONAL),
    ]
    grad_gain, grad_out_bias, grad_task_bias = pl.pallas_call(
        lambda *refs: finish_kernel(blocks, *refs),
        out_shape=[jax.ShapeDtypeStruct((lines, LANES), F32)] * 2
        + [jax.ShapeDtypeStruct(task_bias.shape, F32)],
        in_specs=[vmem] * 4,
        out_specs=[vmem] * 3,
        compiler_params=params,
    )(*four)
    return (
        losses,
        grad_attn.reshape(2, tok_rows, width),
        grad_gain.reshape(width),
        grad_task_bias,
        grad_out_bias.reshape(width),
    )


def solution(mesh):
    fine = Mesh(mesh.devices.reshape(2, 2, 2, 4, 4), ALL)
    in_specs = (
        P(None, ALL, None),
        P(None, ALL, None),
        P(None, GRP),
        P(),
        P(),
        P(),
        P(GRP),
        P(ALL, None),
        P(ALL, None),
    )
    out_specs = (P(ALL), P(None, ALL, None), P(), P(), P())
    return jax.shard_map(local, mesh=fine, in_specs=in_specs, out_specs=out_specs, check_vma=False)
```

```python
import jax
import jax.numpy as jnp
from jax import lax
from jax.experimental import pallas as pl
from jax.experimental.pallas import tpu as pltpu
from jax.sharding import Mesh, PartitionSpec as P

TAU = 0.02
LOSS_SCALE = 256.0
GRP = ("xl", "co")
BLK = ("xh", "y", "z")
ALL = GRP + BLK
SWAP = [(0, 1), (1, 0)]
DIAGONAL = [(0, 3), (1, 2), (2, 1), (3, 0)]
LANES = 128
F32 = jnp.float32
BF16 = jnp.bfloat16
SEND = jnp.float16


def swap_core(values):
    return lax.ppermute(values, "co", SWAP)


def swap_chip(values):
    return lax.ppermute(values, "xl", SWAP)


def from_ahead(values, axis, step):
    size = lax.axis_size(axis)
    return lax.ppermute(values, axis, [((i + step) % size, i) for i in range(size)])


def double_over(values, axis):
    size = lax.axis_size(axis)
    step = 1
    while step < size:
        values = values + lax.ppermute(values, axis, [(i, i ^ step) for i in range(size)])
        step *= 2
    return values


def sum_over(values, axis):
    if lax.axis_size(axis) == 2:
        return values + from_ahead(values, axis, 1)
    one, two, three = [from_ahead(values, axis, step) for step in (1, 2, 3)]
    return (values + two) + (one + three)


def exchange(values, axes):
    return lax.all_to_all(values, axes, split_axis=0, concat_axis=0, tiled=True)


def embed_kernel(
    me, x0, x1, x2, x3, resid, out_bias, gain, bias_row, requests,
    spread, pooled, inv_rms, inv_norm, held,
):
    rows, width = resid.shape
    quarter = width // 4
    for i, x_ref in enumerate((x0, x1, x2, x3)):
        held[i] = x_ref[...]
    squares = jnp.zeros((rows, LANES), F32)
    for b in range(width // LANES):
        here = slice(b * LANES, (b + 1) * LANES)
        start = b * LANES % quarter
        projected = held[me[0] ^ (b * LANES // quarter), :, start : start + LANES]
        value = resid[:, here].astype(F32) + projected.astype(F32) + out_bias[:, here]
        pooled[:, here] = value
        squares = squares + value * value
    mean = jnp.sum(squares, axis=1, keepdims=True) / width
    rms = jnp.broadcast_to(lax.rsqrt(mean + 1e-05), (rows, LANES))
    inv_rms[...] = rms

    def mixture(b):
        here = slice(b * LANES, (b + 1) * LANES)
        return pooled[:, here] * rms * gain[:, here] + bias_row[:, here]

    squares = jnp.zeros((rows, LANES), F32)
    for b in range(width // LANES):
        value = mixture(b)
        squares = squares + value * value
    total = jnp.sum(squares, axis=1, keepdims=True)
    norm = jnp.broadcast_to(lax.rsqrt(total + 1e-06), (rows, LANES))
    inv_norm[...] = norm
    wanted = requests[...].astype(F32)
    for b in range(width // LANES):
        spread[b] = jnp.concatenate([mixture(b) * norm, wanted]).astype(BF16)


def pullback_kernel(
    me, task, sums, spread, pooled, inv_rms, inv_norm, gain, bias_row,
    y0, y1, y2, y3, vectors, grad, held,
):
    rows, width = pooled.shape
    half = rows // 2
    quarter = width // 4
    lines = width // LANES
    rms, norm = inv_rms[...], inv_norm[...]

    def across(values):
        return jnp.broadcast_to(jnp.sum(values, axis=1, keepdims=True), values.shape)

    def embedded(b):
        here = slice(b * LANES, (b + 1) * LANES)
        normed = pooled[:, here] * rms
        return normed, (normed * gain[:, here] + bias_row[:, here]) * norm

    along = jnp.zeros((rows, LANES), F32)
    for b in range(width // LANES):
        own = spread[b].astype(F32)
        other = jnp.concatenate([own[half:rows], own[:half]])
        both = jnp.concatenate([sums[b, 0].astype(F32), sums[b, 1].astype(F32)])
        cotangent = (both - other) / TAU
        grad[:, b * LANES : (b + 1) * LANES] = cotangent
        along = along + embedded(b)[1] * cotangent
    along = across(along)
    inner = jnp.zeros((rows, LANES), F32)
    for b in range(width // LANES):
        here = slice(b * LANES, (b + 1) * LANES)
        normed, unit = embedded(b)
        d_mixture = norm * (grad[:, here] - unit * along)
        vectors[b : b + 1, :] = jnp.sum(d_mixture * normed, axis=0, keepdims=True)
        vectors[2 * lines + b : 2 * lines + b + 1, :] = jnp.sum(d_mixture, axis=0, keepdims=True)
        d_normed = d_mixture * gain[:, here]
        grad[:, here] = d_normed
        inner = inner + d_normed * normed
    inner = across(inner) / width
    for b in range(lines):
        here = slice(b * LANES, (b + 1) * LANES)
        d_pooled = rms * (grad[:, here] - pooled[:, here] * rms * inner)
        vectors[lines + b : lines + b + 1, :] = jnp.sum(d_pooled, axis=0, keepdims=True)
        start = b * LANES % quarter
        held[b * LANES // quarter, :, start : start + LANES] = (LOSS_SCALE * d_pooled).astype(BF16)
    vectors[3 * lines :, :] = jnp.full((8, LANES), task[0].astype(F32))
    for i, y_ref in enumerate((y0, y1, y2, y3)):
        y_ref[...] = held[me[0] ^ i]


def gather_kernel(hard_count, tok_rows, ids, q_ref, p_ref, neg_ref, hard_ref, wide, picked):
    rows = q_ref.shape[0]
    wide[...] = p_ref[...].astype(F32)

    def pick(block, carry):
        for i in range(tok_rows):
            for k in range(hard_count):
                source = ids[(block * hard_count + k) * tok_rows + i]
                picked[k, pl.ds(block * tok_rows + i, 1), :] = wide[pl.ds(source, 1), :]
        return carry

    lax.fori_loop(0, rows // tok_rows, pick, 0)
    q = q_ref[...].astype(F32)
    lane = lax.broadcasted_iota(jnp.int32, (rows, LANES), 1)
    hard = jnp.zeros((rows, LANES), F32)
    for k in range(hard_count):
        chosen = picked[k]
        neg_ref[k] = chosen.astype(BF16)
        hard = jnp.where(lane == k, jnp.sum(q * chosen, axis=1, keepdims=True), hard)
    hard_ref[...] = hard


def scatter_kernel(hard_count, tok_rows, ids, w_ref, q_ref, neg_ref, add_ref, slot, *parts):
    rows = q_ref.shape[0]
    for part in parts:
        part[...] = jnp.zeros_like(part)
    q = q_ref[...].astype(F32)
    total = jnp.zeros((rows, LANES), F32)
    for k in range(hard_count):
        weight = w_ref[:, k : k + 1].astype(F32)
        slot[k] = weight * q
        total = total + weight * neg_ref[k].astype(F32)
    add_ref[4 * rows :, :] = total.astype(BF16)

    def place(block, carry):
        for i in range(tok_rows):
            for k in range(hard_count):
                target = pl.ds(ids[(block * hard_count + k) * tok_rows + i], 1)
                parts[k][target, :] += slot[k, pl.ds(block * tok_rows + i, 1), :]
        return carry

    lax.fori_loop(0, rows // tok_rows, place, 0)
    added = parts[0][...]
    for k in range(1, hard_count):
        added = added + parts[k][...]
    add_ref[: 4 * rows, :] = added.astype(BF16)


def stream_chunks(w_ref, held, sems):
    chunks, depth = held.shape[0], held.shape[1]
    copies = [
        pltpu.make_async_copy(w_ref.at[pl.ds(c * depth, depth), :], held.at[c], sems.at[c])
        for c in range(chunks)
    ]
    for copy in copies:
        copy.start()
    return copies


def forward_kernel(x0, x1, x2, x3, w_ref, y0, y1, y2, y3, held, total, sems):
    depth = held.shape[1]
    rows = y0.shape[0]
    for c, copy in enumerate(stream_chunks(w_ref, held, sems)):
        copy.wait()
        here = slice(c * depth, (c + 1) * depth)
        x = jnp.concatenate([x_ref[:, here] for x_ref in (x0, x1, x2, x3)])
        term = jnp.dot(x, held[c], preferred_element_type=F32)
        total[...] = term if c == 0 else total[...] + term
    for i, y_ref in enumerate((y0, y1, y2, y3)):
        y_ref[...] = total[i * rows : (i + 1) * rows, :].astype(BF16)


def backward_kernel(x0, x1, x2, x3, w_ref, keep_ref, send_ref, held, sems):
    depth = held.shape[1]
    rows = keep_ref.shape[1]
    copies = stream_chunks(w_ref, held, sems)
    x = jnp.concatenate([x_ref[...] for x_ref in (x0, x1, x2, x3)])
    for c, copy in enumerate(copies):
        copy.wait()
        term = lax.dot_general(x, held[c], (((1,), (1,)), ((), ())), preferred_element_type=F32)
        here = slice(c * depth, (c + 1) * depth)
        for i in range(4):
            out_ref = send_ref if i % 2 else keep_ref
            out_ref[i // 2, :, here] = term[i * rows : (i + 1) * rows].astype(BF16)


def softmax_kernel(hard_count, at, score_ref, losses_ref, hard_ref, group_ref):
    rows, width = score_ref.shape
    pairs = width - LANES
    scores = score_ref[:, :pairs] / TAU
    weights = jnp.exp(scores)
    slot = lax.broadcasted_iota(jnp.int32, (rows, LANES), 1)
    hard_weights = jnp.where(slot < hard_count, jnp.exp(score_ref[:, pairs:] / TAU), 0.0)
    totals = jnp.sum(weights, axis=1, keepdims=True) + jnp.sum(hard_weights, axis=1, keepdims=True)
    column = lax.broadcasted_iota(jnp.int32, (rows, pairs), 1)
    row = lax.broadcasted_iota(jnp.int32, (rows, pairs), 0)
    own = jnp.sum(jnp.where(column == row + at[0], scores, 0.0), axis=1, keepdims=True)
    losses_ref[...] = jnp.broadcast_to(jnp.log(totals) - own, (rows, LANES))
    hard_probs = (hard_weights / totals).astype(BF16)
    probs = (weights / totals).astype(BF16)
    for b in range(hard_ref.shape[0]):
        hard_ref[b] = hard_probs
        group_ref[b] = probs


def sums_kernel(probs_ref, q_ref, p_ref, hard_ref, add_ref, near_ref, far_ref, out_ref):
    tok_rows = out_ref.shape[2]
    probs = probs_ref[...]
    sum_q = jnp.dot(probs, p_ref[...], preferred_element_type=F32)
    sum_q = sum_q + hard_ref[...].astype(F32)
    sum_p = lax.dot_general(
        probs, q_ref[...], (((0,), (0,)), ((), ())), preferred_element_type=F32
    )
    sum_p = sum_p + add_ref[...].astype(F32) + near_ref[...].astype(F32) + far_ref[...].astype(F32)
    for b in range(out_ref.shape[0]):
        here = slice(b * tok_rows, (b + 1) * tok_rows)
        out_ref[b, 0] = sum_q[here].astype(BF16)
        out_ref[b, 1] = sum_p[here].astype(BF16)


def finish_kernel(blocks, v0, v1, v2, v3, gain_ref, bias_ref, task_ref):
    lines = gain_ref.shape[0]
    four = (v0, v1, v2, v3)

    def total(start):
        parts = [v[start : start + lines, :] for v in four]
        return (parts[0] + parts[1]) + (parts[2] + parts[3])

    gain_ref[...] = total(0)
    bias_ref[...] = total(lines)
    row = lax.broadcasted_iota(jnp.int32, (8, LANES), 0).astype(F32)
    chosen = [
        jnp.where(jnp.abs(v[3 * lines :, :] / blocks - row) < 0.5, 1.0, 0.0) for v in four
    ]
    for b in range(lines):
        here = slice(2 * lines + b, 2 * lines + b + 1)
        parts = [mask * v[here, :] for mask, v in zip(chosen, four)]
        task_ref[:, b * LANES : (b + 1) * LANES] = (parts[0] + parts[1]) + (parts[2] + parts[3])


def local(resid, attn, out_proj, out_bias, gain, task_bias, task_ids, neg_owner, neg_row):
    tok_rows = resid.shape[1]
    width = resid.shape[2]
    hard_count = neg_owner.shape[1]
    row_count = 2 * tok_rows
    blocks = lax.axis_size(BLK)
    pairs = blocks * tok_rows
    me = lax.axis_index(GRP)
    vmem = pl.BlockSpec(memory_space=pltpu.VMEM)
    smem = pl.BlockSpec(memory_space=pltpu.SMEM)
    params = pltpu.CompilerParams(vmem_limit_bytes=24 * 1024 * 1024)

    stream = pltpu.CompilerParams(vmem_limit_bytes=52 * 1024 * 1024)

    attn_rows = attn.reshape(row_count, width)
    far_rows = swap_chip(attn_rows)
    near_rows = swap_core(attn_rows)
    half = LANES // 2
    fill = ((0, 1), (0, half - tok_rows))
    requests = jnp.concatenate(
        [jnp.pad(neg_owner.T, fill), jnp.pad(neg_row.T, fill)], axis=1
    ).astype(BF16)
    task_onehot = (jnp.arange(task_bias.shape[0]) == task_ids[0]).astype(F32)
    bias_row = jnp.sum(task_onehot[:, None] * task_bias, axis=0, keepdims=True)
    far_rows, near_rows, requests, bias_row = lax.optimization_barrier(
        (far_rows, near_rows, requests, bias_row)
    )


    chunks = 8
    held = [
        pltpu.VMEM((chunks, out_proj.shape[0] // chunks, out_proj.shape[1]), BF16),
        pltpu.SemaphoreType.DMA((chunks,)),
    ]
    hbm = pl.BlockSpec(memory_space=pltpu.HBM)
    columns = pl.pallas_call(
        forward_kernel,
        out_shape=[jax.ShapeDtypeStruct((row_count, out_proj.shape[1]), BF16)] * 4,
        in_specs=[vmem] * 4 + [hbm],
        out_specs=[vmem] * 4,
        scratch_shapes=[held[0], pltpu.VMEM((4 * row_count, out_proj.shape[1]), F32), held[1]],
        compiler_params=stream,
    )(attn_rows, near_rows, far_rows, swap_core(far_rows), out_proj)
    parts = [
        columns[0],
        swap_core(columns[1]),
        swap_chip(columns[2]),
        lax.ppermute(columns[3], GRP, DIAGONAL),
    ]

    place = me.astype(jnp.int32).reshape(1)
    rows_f32 = jax.ShapeDtypeStruct((row_count, LANES), F32)
    own_spread, pooled, inv_rms, inv_norm = pl.pallas_call(
        embed_kernel,
        out_shape=(
            jax.ShapeDtypeStruct((blocks, row_count + 8, LANES), BF16),
            jax.ShapeDtypeStruct((row_count, width), F32),
            rows_f32,
            rows_f32,
        ),
        in_specs=[smem] + [vmem] * 9,
        out_specs=(vmem,) * 4,
        scratch_shapes=[pltpu.VMEM((4, row_count, width // 4), BF16)],
        compiler_params=params,
    )(
        place,
        *parts,
        resid.reshape(row_count, width),
        out_bias[None],
        gain[None],
        bias_row,
        requests,
    )
    spread = exchange(own_spread, BLK)
    q_all = spread[:, :tok_rows].reshape(pairs, LANES)
    p_own = spread[:, tok_rows:row_count].reshape(pairs, LANES)
    requests = spread[:, row_count : row_count + hard_count].astype(jnp.int32)
    owner = requests[:, :, :tok_rows]
    ids = ((owner // blocks) ^ me) * pairs + (owner % blocks) * tok_rows
    ids = (ids + requests[:, :, half : half + tok_rows]).reshape(-1)
    p_far = swap_chip(p_own)
    p_all = jnp.concatenate([p_own, swap_core(p_own), p_far, swap_core(p_far)])

    score_part = lax.dot_general(
        q_all, p_own, (((1,), (1,)), ((), ())), preferred_element_type=F32
    )
    negatives, hard_part = pl.pallas_call(
        lambda *refs: gather_kernel(hard_count, tok_rows, *refs),
        out_shape=(
            jax.ShapeDtypeStruct((hard_count, pairs, LANES), BF16),
            jax.ShapeDtypeStruct((pairs, LANES), F32),
        ),
        in_specs=[smem, vmem, vmem],
        out_specs=(vmem, vmem),
        scratch_shapes=[
            pltpu.VMEM((4 * pairs, LANES), F32),
            pltpu.VMEM((hard_count, pairs, LANES), F32),
        ],
        compiler_params=params,
    )(ids, q_all, p_all)
    part = jnp.concatenate([score_part, hard_part], axis=1).astype(SEND)
    part = exchange(part.reshape(blocks, tok_rows, pairs + LANES), BLK)
    part = jnp.sum(part.astype(F32), axis=0)
    losses, hard_probs, group_probs = pl.pallas_call(
        lambda *refs: softmax_kernel(hard_count, *refs),
        out_shape=(
            jax.ShapeDtypeStruct((tok_rows, LANES), F32),
            jax.ShapeDtypeStruct((blocks, tok_rows, LANES), BF16),
            jax.ShapeDtypeStruct((blocks, tok_rows, pairs), BF16),
        ),
        in_specs=[smem, vmem],
        out_specs=(vmem,) * 3,
        compiler_params=params,
    )((lax.axis_index(BLK) * tok_rows).astype(jnp.int32).reshape(1), part)
    losses = losses[:, 0]
    hard_probs = exchange(hard_probs, BLK).reshape(pairs, LANES)
    group_probs = exchange(group_probs, BLK).reshape(pairs, pairs)

    hard_add = pl.pallas_call(
        lambda *refs: scatter_kernel(hard_count, tok_rows, *refs),
        out_shape=jax.ShapeDtypeStruct((5 * pairs, LANES), BF16),
        in_specs=[smem, vmem, vmem, vmem],
        out_specs=vmem,
        scratch_shapes=[pltpu.VMEM((hard_count, pairs, LANES), F32)]
        + [pltpu.VMEM((4 * pairs, LANES), F32)] * hard_count,
        compiler_params=params,
    )(ids, hard_probs, q_all, negatives)
    hard_add = hard_add.reshape(5, pairs, LANES)
    crossed = swap_core(jnp.stack([hard_add[1], hard_add[3]]))
    over_chip = swap_chip((hard_add[2].astype(F32) + crossed[1].astype(F32)).astype(BF16))
    sums = pl.pallas_call(
        sums_kernel,
        out_shape=jax.ShapeDtypeStruct((blocks, 2, tok_rows, LANES), BF16),
        in_specs=[vmem] * 7,
        out_specs=vmem,
        compiler_params=params,
    )(group_probs, q_all, p_own, hard_add[4], hard_add[0], crossed[0], over_chip)
    sums = exchange(sums, BLK)

    lines = width // LANES
    *cols, vectors = pl.pallas_call(
        pullback_kernel,
        out_shape=[jax.ShapeDtypeStruct((row_count, width // 4), BF16)] * 4
        + [jax.ShapeDtypeStruct((3 * lines + 8, LANES), F32)],
        in_specs=[smem] * 2 + [vmem] * 7,
        out_specs=[vmem] * 5,
        scratch_shapes=[
            pltpu.VMEM((row_count, width), F32),
            pltpu.VMEM((4, row_count, width // 4), BF16),
        ],
        compiler_params=params,
    )(place, task_ids, sums, own_spread, pooled, inv_rms, inv_norm, gain[None], bias_row)
    cols = [
        cols[0],
        swap_core(cols[1]),
        swap_chip(cols[2]),
        lax.ppermute(cols[3], GRP, DIAGONAL),
    ]
    vectors, *cols = lax.optimization_barrier((sum_over(vectors, "xh"), *cols))
    keep, send = pl.pallas_call(
        backward_kernel,
        out_shape=[jax.ShapeDtypeStruct((2, row_count, width), BF16)] * 2,
        in_specs=[vmem] * 4 + [hbm],
        out_specs=[vmem] * 2,
        scratch_shapes=held,
        compiler_params=stream,
    )(*cols, out_proj)
    vectors, keep, send = lax.optimization_barrier((vectors, keep, send))
    vectors = sum_over(vectors, "y")
    crossed = swap_core(send)
    far_sum = (keep[1].astype(F32) + crossed[1].astype(F32)).astype(BF16)
    far_sum = swap_chip(far_sum)
    vectors = double_over(vectors, "z")
    vectors, far_sum = lax.optimization_barrier((vectors, far_sum))
    far_sum = far_sum.astype(F32)
    grad_attn = keep[0].astype(F32) + crossed[0].astype(F32) + far_sum

    four = [
        vectors,
        swap_core(vectors),
        swap_chip(vectors),
        lax.ppermute(vectors, GRP, DIAGONAL),
    ]
    grad_gain, grad_out_bias, grad_task_bias = pl.pallas_call(
        lambda *refs: finish_kernel(blocks, *refs),
        out_shape=[jax.ShapeDtypeStruct((lines, LANES), F32)] * 2
        + [jax.ShapeDtypeStruct(task_bias.shape, F32)],
        in_specs=[vmem] * 4,
        out_specs=[vmem] * 3,
        compiler_params=params,
    )(*four)
    return (
        losses,
        grad_attn.reshape(2, tok_rows, width),
        grad_gain.reshape(width),
        grad_task_bias,
        grad_out_bias.reshape(width),
    )


def solution(mesh):
    fine = Mesh(mesh.devices.reshape(2, 2, 2, 4, 4), ALL)
    in_specs = (
        P(None, ALL, None),
        P(None, ALL, None),
        P(None, GRP),
        P(),
        P(),
        P(),
        P(GRP),
        P(ALL, None),
        P(ALL, None),
    )
    out_specs = (P(ALL), P(None, ALL, None), P(), P(), P())
    return jax.shard_map(local, mesh=fine, in_specs=in_specs, out_specs=out_specs, check_vma=False)
```

```python
import jax
import jax.numpy as jnp
from jax import lax
from jax.experimental import pallas as pl
from jax.experimental.pallas import tpu as pltpu
from jax.sharding import Mesh, PartitionSpec as P

TAU = 0.02
LOSS_SCALE = 256.0
GRP = ("xl", "co")
BLK = ("xh", "y", "z")
ALL = GRP + BLK
SWAP = [(0, 1), (1, 0)]
DIAGONAL = [(0, 3), (1, 2), (2, 1), (3, 0)]
LANES = 128
F32 = jnp.float32
BF16 = jnp.bfloat16
SEND = jnp.float16


def swap_core(values):
    return lax.ppermute(values, "co", SWAP)


def swap_chip(values):
    return lax.ppermute(values, "xl", SWAP)


def from_ahead(values, axis, step):
    size = lax.axis_size(axis)
    return lax.ppermute(values, axis, [((i + step) % size, i) for i in range(size)])


def double_over(values, axis):
    size = lax.axis_size(axis)
    step = 1
    while step < size:
        values = values + lax.ppermute(values, axis, [(i, i ^ step) for i in range(size)])
        step *= 2
    return values


def sum_over(values, axis):
    if lax.axis_size(axis) == 2:
        return values + from_ahead(values, axis, 1)
    one, two, three = [from_ahead(values, axis, step) for step in (1, 2, 3)]
    return (values + two) + (one + three)


def exchange(values, axes):
    return lax.all_to_all(values, axes, split_axis=0, concat_axis=0, tiled=True)


def embed_kernel(
    me, x0, x1, x2, x3, resid, out_bias, gain, bias_row, requests,
    spread, pooled, inv_rms, inv_norm, held,
):
    rows, width = resid.shape
    quarter = width // 4
    for i, x_ref in enumerate((x0, x1, x2, x3)):
        held[i] = x_ref[...]
    squares = jnp.zeros((rows, LANES), F32)
    for b in range(width // LANES):
        here = slice(b * LANES, (b + 1) * LANES)
        start = b * LANES % quarter
        projected = held[me[0] ^ (b * LANES // quarter), :, start : start + LANES]
        value = resid[:, here].astype(F32) + projected.astype(F32) + out_bias[:, here]
        pooled[:, here] = value
        squares = squares + value * value
    mean = jnp.sum(squares, axis=1, keepdims=True) / width
    rms = jnp.broadcast_to(lax.rsqrt(mean + 1e-05), (rows, LANES))
    inv_rms[...] = rms

    def mixture(b):
        here = slice(b * LANES, (b + 1) * LANES)
        return pooled[:, here] * rms * gain[:, here] + bias_row[:, here]

    squares = jnp.zeros((rows, LANES), F32)
    for b in range(width // LANES):
        value = mixture(b)
        squares = squares + value * value
    total = jnp.sum(squares, axis=1, keepdims=True)
    norm = jnp.broadcast_to(lax.rsqrt(total + 1e-06), (rows, LANES))
    inv_norm[...] = norm
    wanted = requests[...].astype(F32)
    for b in range(width // LANES):
        spread[b] = jnp.concatenate([mixture(b) * norm, wanted]).astype(BF16)


def pullback_kernel(
    me, task, sums, spread, pooled, inv_rms, inv_norm, gain, bias_row,
    y0, y1, y2, y3, vectors, grad, held,
):
    rows, width = pooled.shape
    half = rows // 2
    quarter = width // 4
    lines = width // LANES
    rms, norm = inv_rms[...], inv_norm[...]

    def across(values):
        return jnp.broadcast_to(jnp.sum(values, axis=1, keepdims=True), values.shape)

    def embedded(b):
        here = slice(b * LANES, (b + 1) * LANES)
        normed = pooled[:, here] * rms
        return normed, (normed * gain[:, here] + bias_row[:, here]) * norm

    along = jnp.zeros((rows, LANES), F32)
    for b in range(width // LANES):
        own = spread[b].astype(F32)
        other = jnp.concatenate([own[half:rows], own[:half]])
        both = jnp.concatenate([sums[b, 0].astype(F32), sums[b, 1].astype(F32)])
        cotangent = (both - other) / TAU
        grad[:, b * LANES : (b + 1) * LANES] = cotangent
        along = along + embedded(b)[1] * cotangent
    along = across(along)
    inner = jnp.zeros((rows, LANES), F32)
    for b in range(width // LANES):
        here = slice(b * LANES, (b + 1) * LANES)
        normed, unit = embedded(b)
        d_mixture = norm * (grad[:, here] - unit * along)
        vectors[b : b + 1, :] = jnp.sum(d_mixture * normed, axis=0, keepdims=True)
        vectors[2 * lines + b : 2 * lines + b + 1, :] = jnp.sum(d_mixture, axis=0, keepdims=True)
        d_normed = d_mixture * gain[:, here]
        grad[:, here] = d_normed
        inner = inner + d_normed * normed
    inner = across(inner) / width
    for b in range(lines):
        here = slice(b * LANES, (b + 1) * LANES)
        d_pooled = rms * (grad[:, here] - pooled[:, here] * rms * inner)
        vectors[lines + b : lines + b + 1, :] = jnp.sum(d_pooled, axis=0, keepdims=True)
        start = b * LANES % quarter
        held[b * LANES // quarter, :, start : start + LANES] = (LOSS_SCALE * d_pooled).astype(BF16)
    vectors[3 * lines :, :] = jnp.full((8, LANES), task[0].astype(F32))
    for i, y_ref in enumerate((y0, y1, y2, y3)):
        y_ref[...] = held[me[0] ^ i]


def gather_kernel(hard_count, tok_rows, ids, q_ref, p_ref, neg_ref, hard_ref, wide, picked):
    rows = q_ref.shape[0]
    wide[...] = p_ref[...].astype(F32)

    def pick(block, carry):
        for i in range(tok_rows):
            for k in range(hard_count):
                source = ids[(block * hard_count + k) * tok_rows + i]
                picked[k, pl.ds(block * tok_rows + i, 1), :] = wide[pl.ds(source, 1), :]
        return carry

    lax.fori_loop(0, rows // tok_rows, pick, 0)
    q = q_ref[...].astype(F32)
    lane = lax.broadcasted_iota(jnp.int32, (rows, LANES), 1)
    hard = jnp.zeros((rows, LANES), F32)
    for k in range(hard_count):
        chosen = picked[k]
        neg_ref[k] = chosen.astype(BF16)
        hard = jnp.where(lane == k, jnp.sum(q * chosen, axis=1, keepdims=True), hard)
    hard_ref[...] = hard


def scatter_kernel(hard_count, tok_rows, ids, w_ref, q_ref, neg_ref, add_ref, slot, *parts):
    rows = q_ref.shape[0]
    for part in parts:
        part[...] = jnp.zeros_like(part)
    q = q_ref[...].astype(F32)
    total = jnp.zeros((rows, LANES), F32)
    for k in range(hard_count):
        weight = w_ref[:, k : k + 1].astype(F32)
        slot[k] = weight * q
        total = total + weight * neg_ref[k].astype(F32)
    add_ref[4 * rows :, :] = total.astype(BF16)

    def place(block, carry):
        for i in range(tok_rows):
            for k in range(hard_count):
                target = pl.ds(ids[(block * hard_count + k) * tok_rows + i], 1)
                parts[k][target, :] += slot[k, pl.ds(block * tok_rows + i, 1), :]
        return carry

    lax.fori_loop(0, rows // tok_rows, place, 0)
    added = parts[0][...]
    for k in range(1, hard_count):
        added = added + parts[k][...]
    add_ref[: 4 * rows, :] = added.astype(BF16)


def stream_chunks(w_ref, held, sems):
    chunks, depth = held.shape[0], held.shape[1]
    copies = [
        pltpu.make_async_copy(w_ref.at[pl.ds(c * depth, depth), :], held.at[c], sems.at[c])
        for c in range(chunks)
    ]
    for copy in copies:
        copy.start()
    return copies


def forward_kernel(x0, x1, x2, x3, w_ref, y0, y1, y2, y3, held, total, sems):
    depth = held.shape[1]
    rows = y0.shape[0]
    for c, copy in enumerate(stream_chunks(w_ref, held, sems)):
        copy.wait()
        here = slice(c * depth, (c + 1) * depth)
        x = jnp.concatenate([x_ref[:, here] for x_ref in (x0, x1, x2, x3)])
        term = jnp.dot(x, held[c], preferred_element_type=F32)
        total[...] = term if c == 0 else total[...] + term
    for i, y_ref in enumerate((y0, y1, y2, y3)):
        y_ref[...] = total[i * rows : (i + 1) * rows, :].astype(BF16)


def backward_kernel(x0, x1, x2, x3, w_ref, keep_ref, send_ref, held, sems):
    depth = held.shape[1]
    rows = keep_ref.shape[1]
    copies = stream_chunks(w_ref, held, sems)
    x = jnp.concatenate([x_ref[...] for x_ref in (x0, x1, x2, x3)])
    for c, copy in enumerate(copies):
        copy.wait()
        term = lax.dot_general(x, held[c], (((1,), (1,)), ((), ())), preferred_element_type=F32)
        here = slice(c * depth, (c + 1) * depth)
        for i in range(4):
            out_ref = send_ref if i % 2 else keep_ref
            out_ref[i // 2, :, here] = term[i * rows : (i + 1) * rows].astype(BF16)


def softmax_kernel(hard_count, at, score_ref, losses_ref, hard_ref, group_ref):
    rows, width = score_ref.shape
    pairs = width - LANES
    scores = score_ref[:, :pairs] / TAU
    weights = jnp.exp(scores)
    slot = lax.broadcasted_iota(jnp.int32, (rows, LANES), 1)
    hard_weights = jnp.where(slot < hard_count, jnp.exp(score_ref[:, pairs:] / TAU), 0.0)
    totals = jnp.sum(weights, axis=1, keepdims=True) + jnp.sum(hard_weights, axis=1, keepdims=True)
    column = lax.broadcasted_iota(jnp.int32, (rows, pairs), 1)
    row = lax.broadcasted_iota(jnp.int32, (rows, pairs), 0)
    own = jnp.sum(jnp.where(column == row + at[0], scores, 0.0), axis=1, keepdims=True)
    losses_ref[...] = jnp.broadcast_to(jnp.log(totals) - own, (rows, LANES))
    hard_probs = (hard_weights / totals).astype(BF16)
    probs = (weights / totals).astype(BF16)
    for b in range(hard_ref.shape[0]):
        hard_ref[b] = hard_probs
        group_ref[b] = probs


def sums_kernel(probs_ref, q_ref, p_ref, hard_ref, add_ref, near_ref, far_ref, out_ref):
    tok_rows = out_ref.shape[2]
    probs = probs_ref[...]
    sum_q = jnp.dot(probs, p_ref[...], preferred_element_type=F32)
    sum_q = sum_q + hard_ref[...].astype(F32)
    sum_p = lax.dot_general(
        probs, q_ref[...], (((0,), (0,)), ((), ())), preferred_element_type=F32
    )
    sum_p = sum_p + add_ref[...].astype(F32) + near_ref[...].astype(F32) + far_ref[...].astype(F32)
    for b in range(out_ref.shape[0]):
        here = slice(b * tok_rows, (b + 1) * tok_rows)
        out_ref[b, 0] = sum_q[here].astype(BF16)
        out_ref[b, 1] = sum_p[here].astype(BF16)


def finish_kernel(blocks, v0, v1, v2, v3, gain_ref, bias_ref, task_ref):
    lines = gain_ref.shape[0]
    four = (v0, v1, v2, v3)

    def total(start):
        parts = [v[start : start + lines, :] for v in four]
        return (parts[0] + parts[1]) + (parts[2] + parts[3])

    gain_ref[...] = total(0)
    bias_ref[...] = total(lines)
    row = lax.broadcasted_iota(jnp.int32, (8, LANES), 0).astype(F32)
    chosen = [
        jnp.where(jnp.abs(v[3 * lines :, :] / blocks - row) < 0.5, 1.0, 0.0) for v in four
    ]
    for b in range(lines):
        here = slice(2 * lines + b, 2 * lines + b + 1)
        parts = [mask * v[here, :] for mask, v in zip(chosen, four)]
        task_ref[:, b * LANES : (b + 1) * LANES] = (parts[0] + parts[1]) + (parts[2] + parts[3])


def local(resid, attn, out_proj, out_bias, gain, task_bias, task_ids, neg_owner, neg_row):
    tok_rows = resid.shape[1]
    width = resid.shape[2]
    hard_count = neg_owner.shape[1]
    row_count = 2 * tok_rows
    blocks = lax.axis_size(BLK)
    pairs = blocks * tok_rows
    me = lax.axis_index(GRP)
    vmem = pl.BlockSpec(memory_space=pltpu.VMEM)
    smem = pl.BlockSpec(memory_space=pltpu.SMEM)
    params = pltpu.CompilerParams(vmem_limit_bytes=24 * 1024 * 1024)

    stream = pltpu.CompilerParams(vmem_limit_bytes=52 * 1024 * 1024)

    attn_rows = attn.reshape(row_count, width)
    far_rows = swap_chip(attn_rows)
    near_rows = swap_core(attn_rows)
    half = LANES // 2
    fill = ((0, 1), (0, half - tok_rows))
    requests = jnp.concatenate(
        [jnp.pad(neg_owner.T, fill), jnp.pad(neg_row.T, fill)], axis=1
    ).astype(BF16)
    task_onehot = (jnp.arange(task_bias.shape[0]) == task_ids[0]).astype(F32)
    bias_row = jnp.sum(task_onehot[:, None] * task_bias, axis=0, keepdims=True)
    far_rows, near_rows, requests, bias_row = lax.optimization_barrier(
        (far_rows, near_rows, requests, bias_row)
    )


    chunks = 8
    held = [
        pltpu.VMEM((chunks, out_proj.shape[0] // chunks, out_proj.shape[1]), BF16),
        pltpu.SemaphoreType.DMA((chunks,)),
    ]
    hbm = pl.BlockSpec(memory_space=pltpu.HBM)
    columns = pl.pallas_call(
        forward_kernel,
        out_shape=[jax.ShapeDtypeStruct((row_count, out_proj.shape[1]), BF16)] * 4,
        in_specs=[vmem] * 4 + [hbm],
        out_specs=[vmem] * 4,
        scratch_shapes=[held[0], pltpu.VMEM((4 * row_count, out_proj.shape[1]), F32), held[1]],
        compiler_params=stream,
    )(attn_rows, near_rows, far_rows, swap_core(far_rows), out_proj)
    parts = [
        columns[0],
        swap_core(columns[1]),
        swap_chip(columns[2]),
        lax.ppermute(columns[3], GRP, DIAGONAL),
    ]

    place = me.astype(jnp.int32).reshape(1)
    rows_f32 = jax.ShapeDtypeStruct((row_count, LANES), F32)
    own_spread, pooled, inv_rms, inv_norm = pl.pallas_call(
        embed_kernel,
        out_shape=(
            jax.ShapeDtypeStruct((blocks, row_count + 8, LANES), BF16),
            jax.ShapeDtypeStruct((row_count, width), F32),
            rows_f32,
            rows_f32,
        ),
        in_specs=[smem] + [vmem] * 9,
        out_specs=(vmem,) * 4,
        scratch_shapes=[pltpu.VMEM((4, row_count, width // 4), BF16)],
        compiler_params=params,
    )(
        place,
        *parts,
        resid.reshape(row_count, width),
        out_bias[None],
        gain[None],
        bias_row,
        requests,
    )
    spread = exchange(own_spread, BLK)
    q_all = spread[:, :tok_rows].reshape(pairs, LANES)
    p_own = spread[:, tok_rows:row_count].reshape(pairs, LANES)
    requests = spread[:, row_count : row_count + hard_count].astype(jnp.int32)
    owner = requests[:, :, :tok_rows]
    ids = ((owner // blocks) ^ me) * pairs + (owner % blocks) * tok_rows
    ids = (ids + requests[:, :, half : half + tok_rows]).reshape(-1)
    p_far = swap_chip(p_own)
    p_all = jnp.concatenate([p_own, swap_core(p_own), p_far, swap_core(p_far)])

    score_part = lax.dot_general(
        q_all, p_own, (((1,), (1,)), ((), ())), preferred_element_type=F32
    )
    negatives, hard_part = pl.pallas_call(
        lambda *refs: gather_kernel(hard_count, tok_rows, *refs),
        out_shape=(
            jax.ShapeDtypeStruct((hard_count, pairs, LANES), BF16),
            jax.ShapeDtypeStruct((pairs, LANES), F32),
        ),
        in_specs=[smem, vmem, vmem],
        out_specs=(vmem, vmem),
        scratch_shapes=[
            pltpu.VMEM((4 * pairs, LANES), F32),
            pltpu.VMEM((hard_count, pairs, LANES), F32),
        ],
        compiler_params=params,
    )(ids, q_all, p_all)
    part = jnp.concatenate([score_part, hard_part], axis=1).astype(SEND)
    part = exchange(part.reshape(blocks, tok_rows, pairs + LANES), BLK)
    part = jnp.sum(part.astype(F32), axis=0)
    losses, hard_probs, group_probs = pl.pallas_call(
        lambda *refs: softmax_kernel(hard_count, *refs),
        out_shape=(
            jax.ShapeDtypeStruct((tok_rows, LANES), F32),
            jax.ShapeDtypeStruct((blocks, tok_rows, LANES), BF16),
            jax.ShapeDtypeStruct((blocks, tok_rows, pairs), BF16),
        ),
        in_specs=[smem, vmem],
        out_specs=(vmem,) * 3,
        compiler_params=params,
    )((lax.axis_index(BLK) * tok_rows).astype(jnp.int32).reshape(1), part)
    losses = losses[:, 0]
    hard_probs = exchange(hard_probs, BLK).reshape(pairs, LANES)
    group_probs = exchange(group_probs, BLK).reshape(pairs, pairs)

    hard_add = pl.pallas_call(
        lambda *refs: scatter_kernel(hard_count, tok_rows, *refs),
        out_shape=jax.ShapeDtypeStruct((5 * pairs, LANES), BF16),
        in_specs=[smem, vmem, vmem, vmem],
        out_specs=vmem,
        scratch_shapes=[pltpu.VMEM((hard_count, pairs, LANES), F32)]
        + [pltpu.VMEM((4 * pairs, LANES), F32)] * hard_count,
        compiler_params=params,
    )(ids, hard_probs, q_all, negatives)
    hard_add = hard_add.reshape(5, pairs, LANES)
    crossed = swap_core(jnp.stack([hard_add[1], hard_add[3]]))
    over_chip = swap_chip((hard_add[2].astype(F32) + crossed[1].astype(F32)).astype(BF16))
    sums = pl.pallas_call(
        sums_kernel,
        out_shape=jax.ShapeDtypeStruct((blocks, 2, tok_rows, LANES), BF16),
        in_specs=[vmem] * 7,
        out_specs=vmem,
        compiler_params=params,
    )(group_probs, q_all, p_own, hard_add[4], hard_add[0], crossed[0], over_chip)
    sums = exchange(sums, BLK)

    lines = width // LANES
    *cols, vectors = pl.pallas_call(
        pullback_kernel,
        out_shape=[jax.ShapeDtypeStruct((row_count, width // 4), BF16)] * 4
        + [jax.ShapeDtypeStruct((3 * lines + 8, LANES), F32)],
        in_specs=[smem] * 2 + [vmem] * 7,
        out_specs=[vmem] * 5,
        scratch_shapes=[
            pltpu.VMEM((row_count, width), F32),
            pltpu.VMEM((4, row_count, width // 4), BF16),
        ],
        compiler_params=params,
    )(place, task_ids, sums, own_spread, pooled, inv_rms, inv_norm, gain[None], bias_row)
    cols = [
        cols[0],
        swap_core(cols[1]),
        swap_chip(cols[2]),
        lax.ppermute(cols[3], GRP, DIAGONAL),
    ]
    vectors, *cols = lax.optimization_barrier((sum_over(vectors, "xh"), *cols))
    keep, send = pl.pallas_call(
        backward_kernel,
        out_shape=[jax.ShapeDtypeStruct((2, row_count, width), BF16)] * 2,
        in_specs=[vmem] * 4 + [hbm],
        out_specs=[vmem] * 2,
        scratch_shapes=held,
        compiler_params=stream,
    )(*cols, out_proj)
    vectors, keep, send = lax.optimization_barrier((vectors, keep, send))
    vectors = double_over(vectors, "y")
    crossed = swap_core(send)
    far_sum = (keep[1].astype(F32) + crossed[1].astype(F32)).astype(BF16)
    far_sum = swap_chip(far_sum)
    vectors = double_over(vectors, "z")
    vectors, far_sum = lax.optimization_barrier((vectors, far_sum))
    far_sum = far_sum.astype(F32)
    grad_attn = keep[0].astype(F32) + crossed[0].astype(F32) + far_sum

    four = [
        vectors,
        swap_core(vectors),
        swap_chip(vectors),
        lax.ppermute(vectors, GRP, DIAGONAL),
    ]
    grad_gain, grad_out_bias, grad_task_bias = pl.pallas_call(
        lambda *refs: finish_kernel(blocks, *refs),
        out_shape=[jax.ShapeDtypeStruct((lines, LANES), F32)] * 2
        + [jax.ShapeDtypeStruct(task_bias.shape, F32)],
        in_specs=[vmem] * 4,
        out_specs=[vmem] * 3,
        compiler_params=params,
    )(*four)
    return (
        losses,
        grad_attn.reshape(2, tok_rows, width),
        grad_gain.reshape(width),
        grad_task_bias,
        grad_out_bias.reshape(width),
    )


def solution(mesh):
    fine = Mesh(mesh.devices.reshape(2, 2, 2, 4, 4), ALL)
    in_specs = (
        P(None, ALL, None),
        P(None, ALL, None),
        P(None, GRP),
        P(),
        P(),
        P(),
        P(GRP),
        P(ALL, None),
        P(ALL, None),
    )
    out_specs = (P(ALL), P(None, ALL, None), P(), P(), P())
    return jax.shard_map(local, mesh=fine, in_specs=in_specs, out_specs=out_specs, check_vma=False)
```

```python
import jax
import jax.numpy as jnp
from jax import lax
from jax.experimental import pallas as pl
from jax.experimental.pallas import tpu as pltpu
from jax.sharding import Mesh, PartitionSpec as P

TAU = 0.02
LOSS_SCALE = 256.0
GRP = ("xl", "co")
BLK = ("xh", "y", "z")
ALL = GRP + BLK
SWAP = [(0, 1), (1, 0)]
DIAGONAL = [(0, 3), (1, 2), (2, 1), (3, 0)]
LANES = 128
F32 = jnp.float32
BF16 = jnp.bfloat16
SEND = jnp.float16


def swap_core(values):
    return lax.ppermute(values, "co", SWAP)


def swap_chip(values):
    return lax.ppermute(values, "xl", SWAP)


def from_ahead(values, axis, step):
    size = lax.axis_size(axis)
    return lax.ppermute(values, axis, [((i + step) % size, i) for i in range(size)])


def double_over(values, axis):
    size = lax.axis_size(axis)
    step = 1
    while step < size:
        values = values + lax.ppermute(values, axis, [(i, i ^ step) for i in range(size)])
        step *= 2
    return values


def sum_over(values, axis):
    if lax.axis_size(axis) == 2:
        return values + from_ahead(values, axis, 1)
    one, two, three = [from_ahead(values, axis, step) for step in (1, 2, 3)]
    return (values + two) + (one + three)


def exchange(values, axes):
    return lax.all_to_all(values, axes, split_axis=0, concat_axis=0, tiled=True)


def embed_kernel(
    me, x0, x1, x2, x3, resid, out_bias, gain, bias_row, requests,
    spread, pooled, inv_rms, inv_norm, held,
):
    rows, width = resid.shape
    quarter = width // 4
    for i, x_ref in enumerate((x0, x1, x2, x3)):
        held[i] = x_ref[...]
    squares = jnp.zeros((rows, LANES), F32)
    for b in range(width // LANES):
        here = slice(b * LANES, (b + 1) * LANES)
        start = b * LANES % quarter
        projected = held[me[0] ^ (b * LANES // quarter), :, start : start + LANES]
        value = resid[:, here].astype(F32) + projected.astype(F32) + out_bias[:, here]
        pooled[:, here] = value
        squares = squares + value * value
    mean = jnp.sum(squares, axis=1, keepdims=True) / width
    rms = jnp.broadcast_to(lax.rsqrt(mean + 1e-05), (rows, LANES))
    inv_rms[...] = rms

    def mixture(b):
        here = slice(b * LANES, (b + 1) * LANES)
        return pooled[:, here] * rms * gain[:, here] + bias_row[:, here]

    squares = jnp.zeros((rows, LANES), F32)
    for b in range(width // LANES):
        value = mixture(b)
        squares = squares + value * value
    total = jnp.sum(squares, axis=1, keepdims=True)
    norm = jnp.broadcast_to(lax.rsqrt(total + 1e-06), (rows, LANES))
    inv_norm[...] = norm
    wanted = requests[...].astype(F32)
    for b in range(width // LANES):
        spread[b] = jnp.concatenate([mixture(b) * norm, wanted]).astype(BF16)


def pullback_kernel(
    me, task, sums, spread, pooled, inv_rms, inv_norm, gain, bias_row,
    y0, y1, y2, y3, vectors, grad, held,
):
    rows, width = pooled.shape
    half = rows // 2
    quarter = width // 4
    lines = width // LANES
    rms, norm = inv_rms[...], inv_norm[...]

    def across(values):
        return jnp.broadcast_to(jnp.sum(values, axis=1, keepdims=True), values.shape)

    def embedded(b):
        here = slice(b * LANES, (b + 1) * LANES)
        normed = pooled[:, here] * rms
        return normed, (normed * gain[:, here] + bias_row[:, here]) * norm

    along = jnp.zeros((rows, LANES), F32)
    for b in range(width // LANES):
        own = spread[b].astype(F32)
        other = jnp.concatenate([own[half:rows], own[:half]])
        both = jnp.concatenate([sums[b, 0].astype(F32), sums[b, 1].astype(F32)])
        cotangent = (both - other) / TAU
        grad[:, b * LANES : (b + 1) * LANES] = cotangent
        along = along + embedded(b)[1] * cotangent
    along = across(along)
    inner = jnp.zeros((rows, LANES), F32)
    for b in range(width // LANES):
        here = slice(b * LANES, (b + 1) * LANES)
        normed, unit = embedded(b)
        d_mixture = norm * (grad[:, here] - unit * along)
        vectors[b : b + 1, :] = jnp.sum(d_mixture * normed, axis=0, keepdims=True)
        vectors[2 * lines + b : 2 * lines + b + 1, :] = jnp.sum(d_mixture, axis=0, keepdims=True)
        d_normed = d_mixture * gain[:, here]
        grad[:, here] = d_normed
        inner = inner + d_normed * normed
    inner = across(inner) / width
    for b in range(lines):
        here = slice(b * LANES, (b + 1) * LANES)
        d_pooled = rms * (grad[:, here] - pooled[:, here] * rms * inner)
        vectors[lines + b : lines + b + 1, :] = jnp.sum(d_pooled, axis=0, keepdims=True)
        start = b * LANES % quarter
        held[b * LANES // quarter, :, start : start + LANES] = (LOSS_SCALE * d_pooled).astype(BF16)
    vectors[3 * lines :, :] = jnp.full((8, LANES), task[0].astype(F32))
    for i, y_ref in enumerate((y0, y1, y2, y3)):
        y_ref[...] = held[me[0] ^ i]


def gather_kernel(hard_count, tok_rows, ids, q_ref, p_ref, neg_ref, hard_ref, wide, picked):
    rows = q_ref.shape[0]
    wide[...] = p_ref[...].astype(F32)

    def pick(block, carry):
        for i in range(tok_rows):
            for k in range(hard_count):
                source = ids[(block * hard_count + k) * tok_rows + i]
                picked[k, pl.ds(block * tok_rows + i, 1), :] = wide[pl.ds(source, 1), :]
        return carry

    lax.fori_loop(0, rows // tok_rows, pick, 0)
    q = q_ref[...].astype(F32)
    lane = lax.broadcasted_iota(jnp.int32, (rows, LANES), 1)
    hard = jnp.zeros((rows, LANES), F32)
    for k in range(hard_count):
        chosen = picked[k]
        neg_ref[k] = chosen.astype(BF16)
        hard = jnp.where(lane == k, jnp.sum(q * chosen, axis=1, keepdims=True), hard)
    hard_ref[...] = hard


def scatter_kernel(hard_count, tok_rows, ids, w_ref, q_ref, neg_ref, add_ref, slot, *parts):
    rows = q_ref.shape[0]
    for part in parts:
        part[...] = jnp.zeros_like(part)
    q = q_ref[...].astype(F32)
    total = jnp.zeros((rows, LANES), F32)
    for k in range(hard_count):
        weight = w_ref[:, k : k + 1].astype(F32)
        slot[k] = weight * q
        total = total + weight * neg_ref[k].astype(F32)
    add_ref[4 * rows :, :] = total.astype(BF16)

    def place(block, carry):
        for i in range(tok_rows):
            for k in range(hard_count):
                target = pl.ds(ids[(block * hard_count + k) * tok_rows + i], 1)
                parts[k][target, :] += slot[k, pl.ds(block * tok_rows + i, 1), :]
        return carry

    lax.fori_loop(0, rows // tok_rows, place, 0)
    added = parts[0][...]
    for k in range(1, hard_count):
        added = added + parts[k][...]
    add_ref[: 4 * rows, :] = added.astype(BF16)


def stream_chunks(w_ref, held, sems):
    chunks, depth = held.shape[0], held.shape[1]
    copies = [
        pltpu.make_async_copy(w_ref.at[pl.ds(c * depth, depth), :], held.at[c], sems.at[c])
        for c in range(chunks)
    ]
    for copy in copies:
        copy.start()
    return copies


def forward_kernel(x0, x1, x2, x3, w_ref, y0, y1, y2, y3, held, total, sems):
    depth = held.shape[1]
    rows = y0.shape[0]
    for c, copy in enumerate(stream_chunks(w_ref, held, sems)):
        copy.wait()
        here = slice(c * depth, (c + 1) * depth)
        x = jnp.concatenate([x_ref[:, here] for x_ref in (x0, x1, x2, x3)])
        term = jnp.dot(x, held[c], preferred_element_type=F32)
        total[...] = term if c == 0 else total[...] + term
    for i, y_ref in enumerate((y0, y1, y2, y3)):
        y_ref[...] = total[i * rows : (i + 1) * rows, :].astype(BF16)


def backward_kernel(x0, x1, x2, x3, w_ref, keep_ref, send_ref, held, sems):
    depth = held.shape[1]
    rows = keep_ref.shape[1]
    copies = stream_chunks(w_ref, held, sems)
    x = jnp.concatenate([x_ref[...] for x_ref in (x0, x1, x2, x3)])
    for c, copy in enumerate(copies):
        copy.wait()
        term = lax.dot_general(x, held[c], (((1,), (1,)), ((), ())), preferred_element_type=F32)
        here = slice(c * depth, (c + 1) * depth)
        for i in range(4):
            out_ref = send_ref if i % 2 else keep_ref
            out_ref[i // 2, :, here] = term[i * rows : (i + 1) * rows].astype(BF16)


def softmax_kernel(hard_count, at, score_ref, losses_ref, hard_ref, group_ref):
    rows, width = score_ref.shape
    pairs = width - LANES
    scores = score_ref[:, :pairs] / TAU
    weights = jnp.exp(scores)
    slot = lax.broadcasted_iota(jnp.int32, (rows, LANES), 1)
    hard_weights = jnp.where(slot < hard_count, jnp.exp(score_ref[:, pairs:] / TAU), 0.0)
    totals = jnp.sum(weights, axis=1, keepdims=True) + jnp.sum(hard_weights, axis=1, keepdims=True)
    column = lax.broadcasted_iota(jnp.int32, (rows, pairs), 1)
    row = lax.broadcasted_iota(jnp.int32, (rows, pairs), 0)
    own = jnp.sum(jnp.where(column == row + at[0], scores, 0.0), axis=1, keepdims=True)
    losses_ref[...] = jnp.broadcast_to(jnp.log(totals) - own, (rows, LANES))
    hard_probs = (hard_weights / totals).astype(BF16)
    probs = (weights / totals).astype(BF16)
    for b in range(hard_ref.shape[0]):
        hard_ref[b] = hard_probs
        group_ref[b] = probs


def sums_kernel(probs_ref, q_ref, p_ref, hard_ref, add_ref, near_ref, far_ref, out_ref):
    tok_rows = out_ref.shape[2]
    probs = probs_ref[...]
    sum_q = jnp.dot(probs, p_ref[...], preferred_element_type=F32)
    sum_q = sum_q + hard_ref[...].astype(F32)
    sum_p = lax.dot_general(
        probs, q_ref[...], (((0,), (0,)), ((), ())), preferred_element_type=F32
    )
    sum_p = sum_p + add_ref[...].astype(F32) + near_ref[...].astype(F32) + far_ref[...].astype(F32)
    for b in range(out_ref.shape[0]):
        here = slice(b * tok_rows, (b + 1) * tok_rows)
        out_ref[b, 0] = sum_q[here].astype(BF16)
        out_ref[b, 1] = sum_p[here].astype(BF16)


def finish_kernel(blocks, v0, v1, v2, v3, gain_ref, bias_ref, task_ref):
    lines = gain_ref.shape[0]
    four = (v0, v1, v2, v3)

    def total(start):
        parts = [v[start : start + lines, :] for v in four]
        return (parts[0] + parts[1]) + (parts[2] + parts[3])

    gain_ref[...] = total(0)
    bias_ref[...] = total(lines)
    row = lax.broadcasted_iota(jnp.int32, (8, LANES), 0).astype(F32)
    chosen = [
        jnp.where(jnp.abs(v[3 * lines :, :] / blocks - row) < 0.5, 1.0, 0.0) for v in four
    ]
    for b in range(lines):
        here = slice(2 * lines + b, 2 * lines + b + 1)
        parts = [mask * v[here, :] for mask, v in zip(chosen, four)]
        task_ref[:, b * LANES : (b + 1) * LANES] = (parts[0] + parts[1]) + (parts[2] + parts[3])


def local(resid, attn, out_proj, out_bias, gain, task_bias, task_ids, neg_owner, neg_row):
    tok_rows = resid.shape[1]
    width = resid.shape[2]
    hard_count = neg_owner.shape[1]
    row_count = 2 * tok_rows
    blocks = lax.axis_size(BLK)
    pairs = blocks * tok_rows
    me = lax.axis_index(GRP)
    vmem = pl.BlockSpec(memory_space=pltpu.VMEM)
    smem = pl.BlockSpec(memory_space=pltpu.SMEM)
    params = pltpu.CompilerParams(vmem_limit_bytes=24 * 1024 * 1024)

    stream = pltpu.CompilerParams(vmem_limit_bytes=52 * 1024 * 1024)

    attn_rows = attn.reshape(row_count, width)
    far_rows = swap_chip(attn_rows)
    near_rows = swap_core(attn_rows)
    half = LANES // 2
    fill = ((0, 1), (0, half - tok_rows))
    requests = jnp.concatenate(
        [jnp.pad(neg_owner.T, fill), jnp.pad(neg_row.T, fill)], axis=1
    ).astype(BF16)
    task_onehot = (jnp.arange(task_bias.shape[0]) == task_ids[0]).astype(F32)
    bias_row = jnp.sum(task_onehot[:, None] * task_bias, axis=0, keepdims=True)
    far_rows, near_rows, requests, bias_row = lax.optimization_barrier(
        (far_rows, near_rows, requests, bias_row)
    )


    chunks = 8
    held = [
        pltpu.VMEM((chunks, out_proj.shape[0] // chunks, out_proj.shape[1]), BF16),
        pltpu.SemaphoreType.DMA((chunks,)),
    ]
    hbm = pl.BlockSpec(memory_space=pltpu.HBM)
    columns = pl.pallas_call(
        forward_kernel,
        out_shape=[jax.ShapeDtypeStruct((row_count, out_proj.shape[1]), BF16)] * 4,
        in_specs=[vmem] * 4 + [hbm],
        out_specs=[vmem] * 4,
        scratch_shapes=[held[0], pltpu.VMEM((4 * row_count, out_proj.shape[1]), F32), held[1]],
        compiler_params=stream,
    )(attn_rows, near_rows, far_rows, swap_core(far_rows), out_proj)
    parts = [
        columns[0],
        swap_core(columns[1]),
        swap_chip(columns[2]),
        lax.ppermute(columns[3], GRP, DIAGONAL),
    ]

    place = me.astype(jnp.int32).reshape(1)
    rows_f32 = jax.ShapeDtypeStruct((row_count, LANES), F32)
    own_spread, pooled, inv_rms, inv_norm = pl.pallas_call(
        embed_kernel,
        out_shape=(
            jax.ShapeDtypeStruct((blocks, row_count + 8, LANES), BF16),
            jax.ShapeDtypeStruct((row_count, width), F32),
            rows_f32,
            rows_f32,
        ),
        in_specs=[smem] + [vmem] * 9,
        out_specs=(vmem,) * 4,
        scratch_shapes=[pltpu.VMEM((4, row_count, width // 4), BF16)],
        compiler_params=params,
    )(
        place,
        *parts,
        resid.reshape(row_count, width),
        out_bias[None],
        gain[None],
        bias_row,
        requests,
    )
    spread = exchange(own_spread, BLK)
    q_all = spread[:, :tok_rows].reshape(pairs, LANES)
    p_own = spread[:, tok_rows:row_count].reshape(pairs, LANES)
    requests = spread[:, row_count : row_count + hard_count].astype(jnp.int32)
    owner = requests[:, :, :tok_rows]
    ids = ((owner // blocks) ^ me) * pairs + (owner % blocks) * tok_rows
    ids = (ids + requests[:, :, half : half + tok_rows]).reshape(-1)
    p_far = swap_chip(p_own)
    p_all = jnp.concatenate([p_own, swap_core(p_own), p_far, swap_core(p_far)])

    score_part = lax.dot_general(
        q_all, p_own, (((1,), (1,)), ((), ())), preferred_element_type=F32
    )
    negatives, hard_part = pl.pallas_call(
        lambda *refs: gather_kernel(hard_count, tok_rows, *refs),
        out_shape=(
            jax.ShapeDtypeStruct((hard_count, pairs, LANES), BF16),
            jax.ShapeDtypeStruct((pairs, LANES), F32),
        ),
        in_specs=[smem, vmem, vmem],
        out_specs=(vmem, vmem),
        scratch_shapes=[
            pltpu.VMEM((4 * pairs, LANES), F32),
            pltpu.VMEM((hard_count, pairs, LANES), F32),
        ],
        compiler_params=params,
    )(ids, q_all, p_all)
    part = jnp.concatenate([score_part, hard_part], axis=1).astype(SEND)
    part = exchange(part.reshape(blocks, tok_rows, pairs + LANES), BLK)
    part = jnp.sum(part.astype(F32), axis=0)
    losses, hard_probs, group_probs = pl.pallas_call(
        lambda *refs: softmax_kernel(hard_count, *refs),
        out_shape=(
            jax.ShapeDtypeStruct((tok_rows, LANES), F32),
            jax.ShapeDtypeStruct((blocks, tok_rows, LANES), BF16),
            jax.ShapeDtypeStruct((blocks, tok_rows, pairs), BF16),
        ),
        in_specs=[smem, vmem],
        out_specs=(vmem,) * 3,
        compiler_params=params,
    )((lax.axis_index(BLK) * tok_rows).astype(jnp.int32).reshape(1), part)
    losses = losses[:, 0]
    hard_probs = exchange(hard_probs, BLK).reshape(pairs, LANES)
    group_probs = exchange(group_probs, BLK).reshape(pairs, pairs)

    hard_add = pl.pallas_call(
        lambda *refs: scatter_kernel(hard_count, tok_rows, *refs),
        out_shape=jax.ShapeDtypeStruct((5 * pairs, LANES), BF16),
        in_specs=[smem, vmem, vmem, vmem],
        out_specs=vmem,
        scratch_shapes=[pltpu.VMEM((hard_count, pairs, LANES), F32)]
        + [pltpu.VMEM((4 * pairs, LANES), F32)] * hard_count,
        compiler_params=params,
    )(ids, hard_probs, q_all, negatives)
    hard_add = hard_add.reshape(5, pairs, LANES)
    crossed = swap_core(jnp.stack([hard_add[1], hard_add[3]]))
    over_chip = swap_chip((hard_add[2].astype(F32) + crossed[1].astype(F32)).astype(BF16))
    sums = pl.pallas_call(
        sums_kernel,
        out_shape=jax.ShapeDtypeStruct((blocks, 2, tok_rows, LANES), BF16),
        in_specs=[vmem] * 7,
        out_specs=vmem,
        compiler_params=params,
    )(group_probs, q_all, p_own, hard_add[4], hard_add[0], crossed[0], over_chip)
    sums = exchange(sums, BLK)

    lines = width // LANES
    *cols, vectors = pl.pallas_call(
        pullback_kernel,
        out_shape=[jax.ShapeDtypeStruct((row_count, width // 4), BF16)] * 4
        + [jax.ShapeDtypeStruct((3 * lines + 8, LANES), F32)],
        in_specs=[smem] * 2 + [vmem] * 7,
        out_specs=[vmem] * 5,
        scratch_shapes=[
            pltpu.VMEM((row_count, width), F32),
            pltpu.VMEM((4, row_count, width // 4), BF16),
        ],
        compiler_params=params,
    )(place, task_ids, sums, own_spread, pooled, inv_rms, inv_norm, gain[None], bias_row)
    cols = [
        cols[0],
        swap_core(cols[1]),
        swap_chip(cols[2]),
        lax.ppermute(cols[3], GRP, DIAGONAL),
    ]
    vectors, *cols = lax.optimization_barrier((sum_over(vectors, "xh"), *cols))
    keep, send = pl.pallas_call(
        backward_kernel,
        out_shape=[jax.ShapeDtypeStruct((2, row_count, width), BF16)] * 2,
        in_specs=[vmem] * 4 + [hbm],
        out_specs=[vmem] * 2,
        scratch_shapes=held,
        compiler_params=stream,
    )(*cols, out_proj)
    vectors, keep, send = lax.optimization_barrier((vectors, keep, send))
    vectors = double_over(vectors, "y")
    crossed = swap_core(send)
    far_sum = (keep[1].astype(F32) + crossed[1].astype(F32)).astype(BF16)
    far_sum = swap_chip(far_sum)
    vectors = sum_over(vectors, "z")
    vectors, far_sum = lax.optimization_barrier((vectors, far_sum))
    far_sum = far_sum.astype(F32)
    grad_attn = keep[0].astype(F32) + crossed[0].astype(F32) + far_sum

    four = [
        vectors,
        swap_core(vectors),
        swap_chip(vectors),
        lax.ppermute(vectors, GRP, DIAGONAL),
    ]
    grad_gain, grad_out_bias, grad_task_bias = pl.pallas_call(
        lambda *refs: finish_kernel(blocks, *refs),
        out_shape=[jax.ShapeDtypeStruct((lines, LANES), F32)] * 2
        + [jax.ShapeDtypeStruct(task_bias.shape, F32)],
        in_specs=[vmem] * 4,
        out_specs=[vmem] * 3,
        compiler_params=params,
    )(*four)
    return (
        losses,
        grad_attn.reshape(2, tok_rows, width),
        grad_gain.reshape(width),
        grad_task_bias,
        grad_out_bias.reshape(width),
    )


def solution(mesh):
    fine = Mesh(mesh.devices.reshape(2, 2, 2, 4, 4), ALL)
    in_specs = (
        P(None, ALL, None),
        P(None, ALL, None),
        P(None, GRP),
        P(),
        P(),
        P(),
        P(GRP),
        P(ALL, None),
        P(ALL, None),
    )
    out_specs = (P(ALL), P(None, ALL, None), P(), P(), P())
    return jax.shard_map(local, mesh=fine, in_specs=in_specs, out_specs=out_specs, check_vma=False)
```
